128 devices in a mesh: group: 4 (over z), dom: 32 (over x, y, core).
Axes of the slice: x: 4, y: 4, z: 4, core: 2. Of those that a mesh axis runs over, the one named last changes fastest.
Arguments:
- node_features: bfloat16 [131072, 128], P(('group', 'dom')), may hold values from -6 to 6
- edge_features: bfloat16 [524288, 128], P(('group', 'dom')), may hold values from -6 to 6
- coarse_features: bfloat16 [32768, 128], P(('group', 'dom')), may hold values from -6 to 6
- edge_w_one: bfloat16 [384, 128], replicated, may hold values from -0.3125 to 0.3125
- edge_w_two: bfloat16 [128, 128], replicated, may hold values from -0.5 to 0.5
- node_w_one: bfloat16 [256, 128], replicated, may hold values from -0.375 to 0.375
- node_w_two: bfloat16 [128, 128], replicated, may hold values from -0.5 to 0.5
- coarse_w_one: bfloat16 [256, 128], replicated, may hold values from -0.375 to 0.375
- coarse_w_two: bfloat16 [128, 128], replicated, may hold values from -0.5 to 0.5
- edge_source: int32 [524288], P(('group', 'dom')), may hold values from 0 to 1535, as said below
- edge_target: int32 [524288], P(('group', 'dom')), may hold values from 0 to 1023
- boundary: int32 [128, 256], P(('group', 'dom')), may hold values from 0 to 1023, as said below
- ghost_pos: int32 [128, 32, 16], P(('group', 'dom')), may hold values from 0 to 255
- restr_order: int32 [128, 1024], P(('group', 'dom')), may hold values from 0 to 1023, each once within a row
- restr_count: int32 [128, 4], P(('group', 'dom')), may hold values from 1 to 512, 1024 in all within a row
- coarse_slot: int32 [128, 4, 512], P(('group', 'dom')), may hold values from 0 to 255
- node_cotangent: bfloat16 [131072, 128], P(('group', 'dom')), may hold values from -6 to 6
- edge_cotangent: bfloat16 [524288, 128], P(('group', 'dom')), may hold values from -6 to 6
- coarse_cotangent: bfloat16 [32768, 128], P(('group', 'dom')), may hold values from -6 to 6
Outputs:
- grad_nodes: float32 [131072, 128], P(('group', 'dom'))
- grad_edges: float32 [524288, 128], P(('group', 'dom'))
- grad_coarse: float32 [32768, 128], P(('group', 'dom'))
- grad_edge_w_one: float32 [384, 128], replicated
- grad_edge_w_two: float32 [128, 128], replicated
- grad_node_w_one: float32 [256, 128], replicated
- grad_node_w_two: float32 [128, 128], replicated
- grad_coarse_w_one: float32 [256, 128], replicated
- grad_coarse_w_two: float32 [128, 128], replicated
The draws below stay inside these ranges and needn't reach their ends.
Inputs may be any that keep to these rules, and one draw needn't show every extreme that they name: `boundary`: the 256 rows of a partition are distinct. `edge_source`: about one entry in four names a ghost row. `restr_count`: each partition's counts sum to 1024; its largest is exactly 512.
All inputs are finite; a program needn't handle non-finite values.
Results may differ from the reference program's by a relative error of at most 0.01.
Values may be sent and summed in bfloat16 or wider, within the bound.
No kernel may reach another device: no remote copies, remote signals or barrier semaphores. Data moves between devices by JAX's collectives and lax.ppermute only.
A program may use at most 64 MiB of HBM per device.

```python
import math
import jax
import jax.numpy as jnp
import numpy as np
from jax import lax

LAT = 128
NF = 1024
E_DEV = 4096
BND = 256
SLOT = 16
RS = 512
NCD = 256
PARTS_SIZE = 128
GHOSTS = 512
NODES = 131072
EDGES = 524288
COARSE = 32768
N_GROUP = 4
N_DOM = 32


def draw_boundary(key, part):
    key = jax.random.fold_in(key, 11)
    part_keys = jax.random.split(key, PARTS_SIZE)

    def pick_rows(sub_key):
        return jax.random.permutation(sub_key, NF)[:BND].astype(jnp.int32)
    return jax.vmap(pick_rows)(part_keys)


def draw_edge_source(key, part):
    key = jax.random.fold_in(key, 23)
    first_key, second_key, third_key = jax.random.split(key, 3)
    local_ids = jax.random.randint(first_key, (EDGES,), 0, NF, dtype=jnp.int32)
    ghost_ids = NF + jax.random.randint(second_key, (EDGES,), 0, GHOSTS, dtype=jnp.int32)
    choose_ghost = jax.random.randint(third_key, (EDGES,), 0, 4, dtype=jnp.int32) == 0
    return jnp.where(choose_ghost, ghost_ids, local_ids)


def with_ends(array, key, smallest, high):
    index_at = [jax.random.randint(jax.random.fold_in(key, axis), (), 0, length) for axis, length in enumerate(array.shape)]
    main_axis = array.shape.index(max(array.shape))
    next_to = index_at[:main_axis] + [(index_at[main_axis] + 1) % array.shape[main_axis]] + index_at[main_axis + 1:]
    return array.at[tuple(index_at)].set(smallest).at[tuple(next_to)].set(high)


def block_levels(own_key, shape, cuts, least, high):
    gain, own = 1.0, jax.random.fold_in(own_key, 6)
    for axis_at, blocks in cuts:
        heights = jnp.exp(jax.random.uniform(jax.random.fold_in(own, axis_at), (blocks,), jnp.float32, least / len(cuts), high / len(cuts)))
        gain = gain * jnp.repeat(heights, shape[axis_at] // blocks).reshape([-1 if axis == axis_at else 1 for axis in range(len(shape))])
    return gain


def profile(number_of, total, limit, skew):
    portions = [(1 << 20) // math.isqrt(grade ** skew) + 1 for grade in range(2, number_of + 1)]
    rest, given = total - limit - (number_of - 1), [1] * (number_of - 1)
    while rest > 0:
        candidates = [i for i in range(number_of - 1) if given[i] < limit]
        whole, budget = sum([portions[i] for i in candidates]), rest
        for i in candidates:
            more = min(limit - given[i], max(1, budget * portions[i] // whole), rest)
            given[i] = given[i] + more
            rest = rest - more
    return np.array([limit] + given)


def ragged_sizes(stream_key, count, total, bound, lean):
    if count == 2:
        one = jax.random.randint(stream_key, (), max(1, total - bound), min(bound, total - 1) + 1)
        return jnp.stack([one, total - one])
    tallies = jnp.asarray(profile(count, total, bound, lean), jnp.int32)
    pairs = (count - 1) // 2
    source_of, receiver = tallies[1:1 + 2 * pairs:2], tallies[2:2 + 2 * pairs:2]
    room = jnp.minimum(source_of - 1, bound - receiver)
    moved = jax.random.randint(jax.random.fold_in(stream_key, 1), (pairs,), 0, 1 << 20) % (room + 1)
    tallies = tallies.at[1:1 + 2 * pairs:2].set(source_of - moved).at[2:2 + 2 * pairs:2].set(receiver + moved)
    return tallies[jax.random.permutation(jax.random.fold_in(stream_key, 2), count)]


def bell_draw(key, extent, scale, reach, shards=(), held_as=jnp.bfloat16):
    level = block_levels(key, extent, shards, -0.22, 0.18) if shards else 1.0
    array = jax.random.normal(key, extent, jnp.float32) * scale * level
    return jnp.minimum(jnp.maximum(array, -reach), reach).astype(held_as)


def setup_inputs(seed: int = 0) -> dict:
    key_list = jax.random.split(jax.random.key(seed), 20)
    return {
        "node_features": bell_draw(key_list[0], (NODES, LAT), 1.0, 6.0, ((0, 128),)),
        "edge_features": bell_draw(key_list[1], (EDGES, LAT), 1.0, 6.0, ((0, 128),)),
        "coarse_features": bell_draw(key_list[2], (COARSE, LAT), 1.0, 6.0, ((0, 128),)),
        "edge_w_one": bell_draw(key_list[3], (3 * LAT, LAT), (3 * LAT) ** -0.5, 0.3125),
        "edge_w_two": bell_draw(key_list[4], (LAT, LAT), LAT ** -0.5, 0.5),
        "node_w_one": bell_draw(key_list[5], (2 * LAT, LAT), (2 * LAT) ** -0.5, 0.375),
        "node_w_two": bell_draw(key_list[6], (LAT, LAT), LAT ** -0.5, 0.5),
        "coarse_w_one": bell_draw(key_list[7], (2 * LAT, LAT), (2 * LAT) ** -0.5, 0.375),
        "coarse_w_two": bell_draw(key_list[8], (LAT, LAT), LAT ** -0.5, 0.5),
        "edge_source": draw_edge_source(jax.random.fold_in(key_list[19], 71), 0),
        "edge_target": with_ends(jax.random.randint(key_list[10], (EDGES,), 0, NF), jax.random.fold_in(key_list[10], 1), 0, NF - 1).astype(jnp.int32),
        "boundary": draw_boundary(jax.random.fold_in(key_list[19], 71), 0),
        "ghost_pos": with_ends(jax.random.randint(key_list[12], (PARTS_SIZE, N_DOM, SLOT), 0, BND), jax.random.fold_in(key_list[12], 1), 0, BND - 1).astype(jnp.int32),
        "restr_order": jax.vmap(lambda own: jax.random.permutation(own, NF))(jax.random.split(key_list[13], PARTS_SIZE)).reshape((PARTS_SIZE, NF)).astype(jnp.int32),
        "restr_count": jax.vmap(lambda own: ragged_sizes(own, N_GROUP, NF, RS, 1))(jax.random.split(key_list[14], PARTS_SIZE)).reshape((PARTS_SIZE, N_GROUP)).astype(jnp.int32),
        "coarse_slot": with_ends(jax.random.randint(key_list[15], (PARTS_SIZE, N_GROUP, RS), 0, NCD), jax.random.fold_in(key_list[15], 1), 0, NCD - 1).astype(jnp.int32),
        "node_cotangent": bell_draw(key_list[16], (NODES, LAT), 1.0, 6.0, ((0, 128),)),
        "edge_cotangent": bell_draw(key_list[17], (EDGES, LAT), 1.0, 6.0, ((0, 128),)),
        "coarse_cotangent": bell_draw(key_list[18], (COARSE, LAT), 1.0, 6.0, ((0, 128),)),
    }


NORM_EPSILON = 1e-05
POOL_SHARE = 0.25

def silu_slope(values):
    sig_val = jax.nn.sigmoid(values)
    return sig_val * (1.0 + values * (1.0 - sig_val))

def norm_rows(values):
    centred = values - lax.optimization_barrier(jnp.mean(values, axis=-1, keepdims=True))
    return centred * lax.rsqrt(lax.optimization_barrier(jnp.mean(centred * centred, axis=-1, keepdims=True)) + NORM_EPSILON)

def norm_back(values, grad_in):
    centred = values - lax.optimization_barrier(jnp.mean(values, axis=-1, keepdims=True))
    inv_std = lax.rsqrt(lax.optimization_barrier(jnp.mean(centred * centred, axis=-1, keepdims=True)) + NORM_EPSILON)
    normed = centred * inv_std
    return inv_std * (grad_in - lax.optimization_barrier(jnp.mean(grad_in, axis=-1, keepdims=True)) - normed * lax.optimization_barrier(jnp.mean(grad_in * normed, axis=-1, keepdims=True)))

def outer_sum(first_op, second_op):
    return lax.dot_general(first_op, second_op, (((0,), (0,)), ((), ())), preferred_element_type=jnp.float32)

def edge_forward(lookup, edges, source, target, w_one, w_two):
    stacked = jnp.concatenate([lookup[source], lookup[target], edges], axis=1)
    pre_act = jnp.dot(stacked, w_one, preferred_element_type=jnp.float32)
    hidden = jax.nn.silu(pre_act).astype(jnp.bfloat16)
    pre_norm = jnp.dot(hidden, w_two, preferred_element_type=jnp.float32)
    return (stacked, pre_act, hidden, pre_norm)

def node_forward(node_rows, message, target, v_one, v_two):
    row_count = node_rows.shape[0]
    summed = jax.ops.segment_sum(norm_rows(message), target, num_segments=row_count)
    joined = jnp.concatenate([node_rows, summed.astype(jnp.bfloat16)], axis=1)
    pre_act = jnp.dot(joined, v_one, preferred_element_type=jnp.float32)
    hidden = jax.nn.silu(pre_act).astype(jnp.bfloat16)
    pre_norm = jnp.dot(hidden, v_two, preferred_element_type=jnp.float32)
    updated = (node_rows.astype(jnp.float32) + norm_rows(pre_norm)).astype(jnp.bfloat16)
    return (joined, pre_act, hidden, pre_norm, updated)

def mlp_back(inputs_rows, pre_act, hidden, pre_norm, grad_out, w_one, w_two):
    grad_norm = norm_back(pre_norm, grad_out).astype(jnp.bfloat16)
    grad_w_two = outer_sum(hidden, grad_norm)
    grad_hidden = jnp.dot(grad_norm, w_two.T, preferred_element_type=jnp.float32)
    grad_pre = (grad_hidden * silu_slope(pre_act)).astype(jnp.bfloat16)
    grad_w_one = outer_sum(inputs_rows, grad_pre)
    grad_inputs = jnp.dot(grad_pre, w_one.T, preferred_element_type=jnp.float32)
    return (grad_inputs, grad_w_one, grad_w_two)

def reference(node_features, edge_features, coarse_features, edge_w_one, edge_w_two, node_w_one, node_w_two, coarse_w_one, coarse_w_two, edge_source, edge_target, boundary, ghost_pos, restr_order, restr_count, coarse_slot, node_cotangent, edge_cotangent, coarse_cotangent):
    groups = N_GROUP
    domains = N_DOM
    part_total = groups * domains
    latent = node_features.shape[1]
    node_blocks = node_features.reshape(part_total, NF, latent)
    border = boundary.reshape(groups, domains, BND)
    chosen_rows = jnp.take_along_axis(jnp.broadcast_to(border[:, None, :, :], (groups, domains, domains, BND)), ghost_pos.reshape(groups, domains, domains, SLOT), axis=3)
    sender = jnp.arange(groups, dtype=jnp.int32)[:, None, None, None] * domains + jnp.arange(domains, dtype=jnp.int32)[None, None, :, None]
    ghost_index = (sender * NF + chosen_rows).reshape(part_total, GHOSTS)
    ghost_blocks = node_features[ghost_index]
    edge_blocks = edge_features.reshape(part_total, E_DEV, latent)
    source_blocks = edge_source.reshape(part_total, E_DEV)
    target_blocks = edge_target.reshape(part_total, E_DEV)

    def first_pass(block_args):
        node_rows, edges, source, target, ghost_rows = block_args
        lookup = jnp.concatenate([node_rows, ghost_rows], axis=0)
        message = edge_forward(lookup, edges, source, target, edge_w_one, edge_w_two)[3]
        return node_forward(node_rows, message, target, node_w_one, node_w_two)[4]
    updated = lax.map(first_pass, (node_blocks, edge_blocks, source_blocks, target_blocks, ghost_blocks))
    counts = restr_count.reshape(part_total, groups)
    offsets = jnp.cumsum(counts, axis=1) - counts
    slot_ids = jnp.arange(RS, dtype=jnp.int32)
    position = jnp.minimum(offsets[:, :, None] + slot_ids[None, None, :], NF - 1)
    is_valid = slot_ids[None, None, :] < counts[:, :, None]
    send_rows = jnp.take_along_axis(restr_order, position.reshape(part_total, groups * RS), axis=1).reshape(part_total, groups, RS)
    global_rows = send_rows + (jnp.arange(part_total, dtype=jnp.int32) * NF)[:, None, None]
    keep_mask = is_valid[:, :, :, None].astype(jnp.bfloat16)
    sent_updated = updated.reshape(NODES, latent)[global_rows] * keep_mask
    sent_cotangent = node_cotangent[global_rows] * keep_mask

    def to_owner(values):
        shaped = values.reshape(groups, domains, groups, RS, latent)
        return jnp.transpose(shaped, (2, 1, 0, 3, 4)).reshape(part_total * groups * RS, latent)
    coarse_ids = (coarse_slot.reshape(part_total, groups * RS) + (jnp.arange(part_total, dtype=jnp.int32) * NCD)[:, None]).reshape(-1)
    pooled = (jax.ops.segment_sum(to_owner(sent_updated).astype(jnp.float32), coarse_ids, num_segments=COARSE) * POOL_SHARE).astype(jnp.bfloat16)
    from_fine = jax.ops.segment_sum(to_owner(sent_cotangent).astype(jnp.float32), coarse_ids, num_segments=COARSE)
    coarse_grad_out = (coarse_cotangent.astype(jnp.float32) + from_fine).astype(jnp.bfloat16)
    coarse_joined = jnp.concatenate([coarse_features, pooled], axis=1)
    coarse_pre = jnp.dot(coarse_joined, coarse_w_one, preferred_element_type=jnp.float32)
    coarse_hidden = jax.nn.silu(coarse_pre).astype(jnp.bfloat16)
    grad_c_two = outer_sum(coarse_hidden, coarse_grad_out)
    coarse_grad_hidden = jnp.dot(coarse_grad_out, coarse_w_two.T, preferred_element_type=jnp.float32)
    coarse_grad_pre = (coarse_grad_hidden * silu_slope(coarse_pre)).astype(jnp.bfloat16)
    grad_c_one = outer_sum(coarse_joined, coarse_grad_pre)
    coarse_grad_in = jnp.dot(coarse_grad_pre, coarse_w_one.T, preferred_element_type=jnp.float32)
    grad_coarse = coarse_cotangent.astype(jnp.float32) + coarse_grad_in[:, :latent]
    grad_pooled = coarse_grad_in[:, latent:] * POOL_SHARE
    returned = grad_pooled[coarse_ids].reshape(groups, domains, groups, RS, latent)
    returned = jnp.transpose(returned, (2, 1, 0, 3, 4)).reshape(part_total, groups, RS, latent)
    returned = returned * is_valid[:, :, :, None].astype(jnp.float32)
    fine_back = jax.ops.segment_sum(returned.reshape(-1, latent), global_rows.reshape(-1), num_segments=NODES)
    updated_grad = (node_cotangent.astype(jnp.float32) + fine_back).reshape(part_total, NF, latent)
    edge_cot_blocks = edge_cotangent.reshape(part_total, E_DEV, latent)

    def second_pass(block_args):
        node_rows, edges, source, target, ghost_rows, node_grad_in, edge_grad_in = block_args
        lookup = jnp.concatenate([node_rows, ghost_rows], axis=0)
        stacked, edge_pre, edge_hidden, message = edge_forward(lookup, edges, source, target, edge_w_one, edge_w_two)
        joined, node_pre, node_hidden, node_pre_norm, unused_rows = node_forward(node_rows, message, target, node_w_one, node_w_two)
        node_grad_join, grad_v_one, grad_v_two = mlp_back(joined, node_pre, node_hidden, node_pre_norm, node_grad_in, node_w_one, node_w_two)
        message_grad = edge_grad_in.astype(jnp.float32) + node_grad_join[:, latent:][target]
        stacked_grad, grad_w_one, grad_w_two = mlp_back(stacked, edge_pre, edge_hidden, message, message_grad, edge_w_one, edge_w_two)
        edge_out = edge_grad_in.astype(jnp.float32) + stacked_grad[:, 2 * latent:]
        lookup_grad = jax.ops.segment_sum(stacked_grad[:, :latent], source, num_segments=NF + GHOSTS)
        target_grad = jax.ops.segment_sum(stacked_grad[:, latent:2 * latent], target, num_segments=NF)
        local_grad = node_grad_in + node_grad_join[:, :latent] + lookup_grad[:NF] + target_grad
        return (local_grad, lookup_grad[NF:], edge_out, grad_w_one, grad_w_two, grad_v_one, grad_v_two)
    local_grad, ghost_grad, edge_out, grad_w_one, grad_w_two, grad_v_one, grad_v_two = lax.map(second_pass, (node_blocks, edge_blocks, source_blocks, target_blocks, ghost_blocks, updated_grad, edge_cot_blocks))
    ghost_back = jax.ops.segment_sum(ghost_grad.reshape(-1, latent), ghost_index.reshape(-1), num_segments=NODES)
    grad_nodes = local_grad.reshape(NODES, latent) + ghost_back
    grad_edges = edge_out.reshape(EDGES, latent)
    edge_scale = EDGES ** (-0.5)
    node_scale = NODES ** (-0.5)
    coarse_scale = COARSE ** (-0.5)
    return (grad_nodes, grad_edges, grad_coarse, lax.optimization_barrier(jnp.sum(grad_w_one, axis=0)) * edge_scale, lax.optimization_barrier(jnp.sum(grad_w_two, axis=0)) * edge_scale, lax.optimization_barrier(jnp.sum(grad_v_one, axis=0)) * node_scale, lax.optimization_barrier(jnp.sum(grad_v_two, axis=0)) * node_scale, grad_c_one * coarse_scale, grad_c_two * coarse_scale)
```

```python
import functools

import jax
import jax.numpy as jnp
from jax import lax
from jax.experimental import pallas as pl
from jax.experimental.pallas import tpu as pltpu
from jax.sharding import PartitionSpec as P

NORM_EPSILON = 1e-05
POOL_SHARE = 0.25
BF = jnp.bfloat16
F32 = jnp.float32
I32 = jnp.int32
LANES = 128
VMEM_BYTES = 48 * 1024 * 1024


def nn(a, b):
    return lax.dot_general(a, b, (((1,), (0,)), ((), ())), preferred_element_type=F32)


def nt(a, b):
    return lax.dot_general(a, b, (((1,), (1,)), ((), ())), preferred_element_type=F32)


def tn(a, b):
    return lax.dot_general(a, b, (((0,), (0,)), ((), ())), preferred_element_type=F32)


def as_hit(mask):
    return jnp.where(mask, 1.0, 0.0).astype(BF)


def hit_rows(index_row, count, base=0):
    width = index_row.shape[1]
    return as_hit(lax.broadcasted_iota(I32, (count, width), 0) == index_row - base)


def spread_column(index_row):
    width = index_row.shape[1]
    return jnp.transpose(jnp.broadcast_to(index_row, (LANES, width)))


def hit_columns(index_column, count, base=0):
    lane = lax.broadcasted_iota(I32, index_column.shape, 1)
    return jnp.concatenate(
        [as_hit(lane == index_column - (base + LANES * j)) for j in range(count // LANES)], axis=1
    )


def split_wide(values):
    high = values.astype(BF)
    low = (values - high.astype(F32)).astype(BF)
    return jnp.concatenate([high, low], axis=1)


def fold_wide(values):
    return values[:, :LANES] + values[:, LANES:]


def times_transposed(values, weights):
    return nt(split_wide(values), jnp.concatenate([weights, weights], axis=1))


def mean_lanes(values):
    return jnp.mean(values, axis=-1, keepdims=True)


def norm_parts(values):
    centred = values - mean_lanes(values)
    inv_std = lax.rsqrt(mean_lanes(centred * centred) + NORM_EPSILON)
    return centred * inv_std, inv_std


def norm_back(normed, inv_std, grad_in):
    return inv_std * (grad_in - mean_lanes(grad_in) - normed * mean_lanes(grad_in * normed))


def sigmoid(values):
    return 1.0 / (1.0 + jnp.exp(-values))


def slope(values, sig):
    return sig * (1.0 + values * (1.0 - sig))


def share_kernel(boundary_ref, wanted_ref, nodes_ref, out_ref):
    rows = nodes_ref.shape[0]
    border = boundary_ref.shape[1]
    shared = nn(hit_columns(spread_column(boundary_ref[...]), rows), nodes_ref[...]).astype(BF)
    out_ref[...] = nn(hit_columns(spread_column(wanted_ref[...]), border), shared).astype(BF)


def route_kernel(count_ref, slot_ref, order_ref, cot_ref, pool_ref, back_ref, cot_pool_ref):
    groups, capacity = slot_ref.shape
    rows = order_ref.shape[1]
    coarse = pool_ref.shape[0] // groups
    place = lax.broadcasted_iota(I32, (8, rows), 1)
    goal = jnp.zeros((8, rows), I32)
    start = 0
    for k in range(groups):
        count = count_ref[0, k]
        line = jnp.concatenate(
            [slot_ref[k : k + 1, :], jnp.zeros((1, rows - capacity), I32)], axis=1
        )
        line = pltpu.roll(jnp.broadcast_to(line, (8, rows)), start, 1)
        inside = (place >= start) & (place < start + count)
        goal = jnp.where(inside, line + k * coarse, goal)
        start = start + count
    to_coarse = hit_rows(goal[0:1, :], groups * coarse)
    to_fine = hit_rows(order_ref[...], rows)
    pool = nt(to_coarse, to_fine).astype(BF)
    pool_ref[...] = pool
    back_ref[...] = nt(to_fine, to_coarse).astype(BF)
    cot_pool_ref[...] = nn(pool, cot_ref[...]).astype(BF)


def edge_first_kernel(source_ref, target_ref, nodes_ref, edges_ref, w_ref, src_ref, tgt_ref, pre_ref):
    rows = nodes_ref.shape[0]
    nodes = nodes_ref[...]
    src = nn(hit_columns(spread_column(source_ref[...]), rows), nodes).astype(BF)
    tgt = nn(hit_columns(spread_column(target_ref[...]), rows), nodes).astype(BF)
    src_ref[...] = src
    tgt_ref[...] = tgt
    pre_ref[...] = nn(jnp.concatenate([src, tgt, edges_ref[...]], axis=1), w_ref[...])


def edge_second_kernel(
    source_ref, target_ref, pre_in_ref, src_in_ref, ghosts_ref, w1_ref, w2_ref,
    nodes_ref, v1_ref, v2_ref, pool_ref, cot_pool_ref,
    pre_ref, src_ref, summed_ref, send_ref, total,
):
    step = pl.program_id(0)
    rows = nodes_ref.shape[0]
    ghost_count = ghosts_ref.shape[0]

    @pl.when(step == 0)
    def _():
        total[...] = jnp.zeros_like(total)

    found = nn(
        hit_columns(spread_column(source_ref[...]), ghost_count, rows), ghosts_ref[...]
    ).astype(BF)
    src_ref[...] = src_in_ref[...] + found
    pre = pre_in_ref[...] + nn(found, w1_ref[:LANES, :])
    pre_ref[...] = pre
    hidden = (pre * sigmoid(pre)).astype(BF)
    message, _ = norm_parts(nn(hidden, w2_ref[...]))
    total[...] += nn(hit_rows(target_ref[...], rows), split_wide(message))

    @pl.when(step == pl.num_programs(0) - 1)
    def _():
        summed = fold_wide(total[...]).astype(BF)
        summed_ref[...] = summed
        nodes = nodes_ref[...]
        pre_node = nn(jnp.concatenate([nodes, summed], axis=1), v1_ref[...])
        hidden_node = (pre_node * sigmoid(pre_node)).astype(BF)
        normed, _ = norm_parts(nn(hidden_node, v2_ref[...]))
        updated = (nodes.astype(F32) + normed).astype(BF)
        pooled = nn(pool_ref[...], updated).astype(BF)
        groups = send_ref.shape[0]
        coarse = send_ref.shape[1] // 2
        for k in range(groups):
            send_ref[k, :coarse, :] = pooled[k * coarse : (k + 1) * coarse, :]
            send_ref[k, coarse:, :] = cot_pool_ref[k * coarse : (k + 1) * coarse, :]


def coarse_kernel(
    got_ref, feat_ref, cot_ref, w1_ref, w2_ref, grad_ref, back_ref, g1_ref, g2_ref
):
    groups = got_ref.shape[0]
    coarse = feat_ref.shape[0]
    got = got_ref[0].astype(F32)
    for k in range(1, groups):
        got = got + got_ref[k].astype(F32)
    pooled = (got[:coarse] * POOL_SHARE).astype(BF)
    cot = cot_ref[...].astype(F32)
    grad_out = (cot + got[coarse:]).astype(BF)
    joined = jnp.concatenate([feat_ref[...], pooled], axis=1)
    pre = nn(joined, w1_ref[...])
    sig = sigmoid(pre)
    hidden = (pre * sig).astype(BF)
    g2_ref[...] = tn(hidden, grad_out)
    grad_pre = (nt(grad_out, w2_ref[...]) * slope(pre, sig)).astype(BF)
    g1_ref[...] = tn(joined, grad_pre)
    grad_in = nt(grad_pre, w1_ref[...])
    grad_ref[...] = cot + grad_in[:, :LANES]
    back = (grad_in[:, LANES:] * POOL_SHARE).astype(BF)
    for k in range(groups):
        back_ref[k] = back


def edge_back_kernel(
    target_ref, pre_ref, src_ref, tgt_ref, edges_ref, cot_ref, w1_ref, w2_ref,
    gp_ref, back_ref, node_cot_ref, nodes_ref, summed_ref, v1_ref, v2_ref, c1_ref, c2_ref,
    grad_pre_ref, local_ref, pack_ref, wide, gw1, gw2, gv1, gv2,
):
    step = pl.program_id(0)
    rows = nodes_ref.shape[0]

    @pl.when(step == 0)
    def _():
        gw1[...] = jnp.zeros_like(gw1)
        gw2[...] = jnp.zeros_like(gw2)
        updated_grad = node_cot_ref[...].astype(F32) + nn(back_ref[...], gp_ref[...])
        joined = jnp.concatenate([nodes_ref[...], summed_ref[...]], axis=1)
        pre = nn(joined, v1_ref[...])
        sig = sigmoid(pre)
        hidden = (pre * sig).astype(BF)
        normed, inv_std = norm_parts(nn(hidden, v2_ref[...]))
        grad_norm = norm_back(normed, inv_std, updated_grad).astype(BF)
        gv2[...] = tn(hidden, grad_norm)
        grad_pre = (nt(grad_norm, v2_ref[...]) * slope(pre, sig)).astype(BF)
        gv1[...] = tn(joined, grad_pre)
        grad_in = nt(grad_pre, v1_ref[...])
        local_ref[...] = updated_grad + grad_in[:, :LANES]
        wide[...] = split_wide(grad_in[:, LANES:])

    from_node = fold_wide(nn(hit_columns(spread_column(target_ref[...]), rows), wide[...]))
    message_grad = cot_ref[...].astype(F32) + from_node
    pre = pre_ref[...]
    sig = sigmoid(pre)
    hidden = (pre * sig).astype(BF)
    normed, inv_std = norm_parts(nn(hidden, w2_ref[...]))
    grad_norm = norm_back(normed, inv_std, message_grad).astype(BF)
    gw2[...] += tn(hidden, grad_norm)
    grad_pre = (nt(grad_norm, w2_ref[...]) * slope(pre, sig)).astype(BF)
    grad_pre_ref[...] = grad_pre
    stacked = jnp.concatenate([src_ref[...], tgt_ref[...], edges_ref[...]], axis=1)
    gw1[...] += tn(stacked, grad_pre)

    @pl.when(step == pl.num_programs(0) - 1)
    def _():
        place = 0
        for part in (gw1, gw2, gv1, gv2, c1_ref, c2_ref):
            size = part.shape[0]
            pack_ref[place : place + size, :] = part[...].astype(BF)
            place += size
        pack_ref[place:, :] = jnp.zeros((pack_ref.shape[0] - place, LANES), BF)


def ghost_back_kernel(source_ref, grad_pre_ref, w1_ref, out_ref, total, *, rows):
    step = pl.program_id(0)

    @pl.when(step == 0)
    def _():
        total[...] = jnp.zeros_like(total)

    total[...] += nn(hit_rows(source_ref[...], total.shape[0], rows), grad_pre_ref[...])

    @pl.when(step == pl.num_programs(0) - 1)
    def _():
        out_ref[...] = times_transposed(total[...], w1_ref[:LANES, :]).astype(BF)


def own_back_kernel(
    source_ref, target_ref, grad_pre_ref, cot_ref, local_ref, w1_ref,
    out_ref, edges_ref, by_source, by_target,
):
    step = pl.program_id(0)
    rows = by_source.shape[0]

    @pl.when(step == 0)
    def _():
        by_source[...] = jnp.zeros_like(by_source)
        by_target[...] = jnp.zeros_like(by_target)

    grad_pre = grad_pre_ref[...]
    by_source[...] += nn(hit_rows(source_ref[...], rows), grad_pre)
    by_target[...] += nn(hit_rows(target_ref[...], rows), grad_pre)
    edges_ref[...] = cot_ref[...].astype(F32) + nt(grad_pre, w1_ref[2 * LANES :, :])

    @pl.when(step == pl.num_programs(0) - 1)
    def _():
        out_ref[...] = (
            local_ref[...]
            + times_transposed(by_source[...], w1_ref[:LANES, :])
            + times_transposed(by_target[...], w1_ref[LANES : 2 * LANES, :])
        )


def add_back_kernel(boundary_ref, wanted_ref, got_ref, local_ref, out_ref):
    rows = local_ref.shape[0]
    border = boundary_ref.shape[1]
    border_grad = nn(hit_rows(wanted_ref[...], border), got_ref[...])
    out_ref[...] = local_ref[...] + fold_wide(
        nn(hit_rows(boundary_ref[...], rows), split_wide(border_grad))
    )


def add_parts_kernel(got_ref, out_ref):
    parts = got_ref.shape[0]
    total = got_ref[0].astype(F32)
    for k in range(1, parts):
        total = total + got_ref[k].astype(F32)
    total = total.astype(BF)
    for k in range(parts):
        out_ref[k] = total


def scale_kernel(pack_ref, *out_refs, scales):
    place = 0
    for out_ref, scale in zip(out_refs, scales):
        size = out_ref.shape[0]
        out_ref[...] = pack_ref[place : place + size, :].astype(F32) * scale
        place += size


def whole(shape):
    zeros = (0,) * len(shape)
    return pl.BlockSpec(shape, lambda *_: zeros)


def call(kernel, out_shapes, *args, flops=0, bytes_accessed=0, in_specs=None, out_specs=None,
         grid=None, scratch=(), name=None):
    single = not isinstance(out_shapes, (list, tuple))
    extra = {}
    if grid is not None:
        extra["grid"] = grid
    if in_specs is not None:
        extra["in_specs"] = in_specs
    if out_specs is not None:
        extra["out_specs"] = out_specs
    return pl.pallas_call(
        kernel,
        out_shape=out_shapes if single else list(out_shapes),
        scratch_shapes=list(scratch),
        compiler_params=pltpu.CompilerParams(vmem_limit_bytes=VMEM_BYTES),
        cost_estimate=pl.CostEstimate(
            flops=flops, bytes_accessed=bytes_accessed, transcendentals=0
        ),
        name=name,
        **extra,
    )(*args)


def local(
    node_features, edge_features, coarse_features,
    edge_w_one, edge_w_two, node_w_one, node_w_two, coarse_w_one, coarse_w_two,
    edge_source, edge_target, boundary, ghost_pos, restr_order, restr_count, coarse_slot,
    node_cotangent, edge_cotangent, coarse_cotangent,
):
    rows, latent = node_features.shape
    edges = edge_features.shape[0]
    coarse = coarse_features.shape[0]
    groups = lax.axis_size("group")
    domains = lax.axis_size("dom")
    parts = groups * domains
    slots = ghost_pos.shape[2]
    ghosts = domains * slots
    shape = jax.ShapeDtypeStruct
    block = 512
    grid = (edges // block,)
    index_spec = pl.BlockSpec((1, block), lambda i: (0, i))
    edge_spec = pl.BlockSpec((block, latent), lambda i: (i, 0))
    exchange = functools.partial(lax.all_to_all, split_axis=0, concat_axis=0, tiled=True)

    source = edge_source.reshape(1, edges)
    target = edge_target.reshape(1, edges)
    asked = exchange(ghost_pos.reshape(domains, slots), "dom").reshape(1, ghosts)
    coarse_to = exchange(coarse_slot.reshape(groups, -1), "group")

    share = call(
        share_kernel, shape((ghosts, latent), BF), boundary, asked, node_features,
        flops=10**9, bytes_accessed=10**6, name="share",
    )
    ghost_rows = exchange(share.reshape(domains, slots, latent), "dom").reshape(ghosts, latent)

    src_own, tgt_rows, pre_part = call(
        edge_first_kernel,
        [shape((edges, latent), BF), shape((edges, latent), BF), shape((edges, latent), F32)],
        source, target, node_features, edge_features, edge_w_one,
        grid=grid,
        in_specs=[index_spec, index_spec, whole((rows, latent)), edge_spec, whole((3 * latent, latent))],
        out_specs=[edge_spec, edge_spec, edge_spec],
        flops=5 * 10**9, bytes_accessed=6 * 10**6, name="edge_first",
    )
    pool, back, cot_pool = call(
        route_kernel,
        [shape((groups * coarse, rows), BF), shape((rows, groups * coarse), BF),
         shape((groups * coarse, latent), BF)],
        restr_count, coarse_to, restr_order, node_cotangent,
        in_specs=[pl.BlockSpec(memory_space=pltpu.SMEM)] + [pl.BlockSpec(memory_space=pltpu.VMEM)] * 3,
        flops=4 * 10**9, bytes_accessed=4 * 10**6, name="route",
    )
    pre, src_rows, summed, send = call(
        edge_second_kernel,
        [shape((edges, latent), F32), shape((edges, latent), BF), shape((rows, latent), BF),
         shape((groups, 2 * coarse, latent), BF)],
        source, target, pre_part, src_own, ghost_rows, edge_w_one, edge_w_two,
        node_features, node_w_one, node_w_two, pool, cot_pool,
        grid=grid,
        in_specs=[index_spec, index_spec, edge_spec, edge_spec, whole((ghosts, latent)),
                  whole((3 * latent, latent)), whole((latent, latent)), whole((rows, latent)),
                  whole((2 * latent, latent)), whole((latent, latent)),
                  whole((groups * coarse, rows)), whole((groups * coarse, latent))],
        out_specs=[edge_spec, edge_spec, whole((rows, latent)), whole((groups, 2 * coarse, latent))],
        scratch=[pltpu.VMEM((rows, 2 * latent), F32)],
        flops=5 * 10**9, bytes_accessed=8 * 10**6, name="edge_second",
    )
    got = exchange(send, "group")
    grad_coarse, coarse_back, grad_c_one, grad_c_two = call(
        coarse_kernel,
        [shape((coarse, latent), F32), shape((groups, coarse, latent), BF),
         shape((2 * latent, latent), F32), shape((latent, latent), F32)],
        got, coarse_features, coarse_cotangent, coarse_w_one, coarse_w_two,
        flops=10**8, bytes_accessed=10**6, name="coarse",
    )
    returned = exchange(coarse_back, "group").reshape(groups * coarse, latent)
    pack_rows = parts * 16
    grad_pre, node_local, pack = call(
        edge_back_kernel,
        [shape((edges, latent), BF), shape((rows, latent), F32), shape((pack_rows, latent), BF)],
        target, pre, src_rows, tgt_rows, edge_features, edge_cotangent, edge_w_one, edge_w_two,
        returned, back, node_cotangent, node_features, summed, node_w_one, node_w_two,
        grad_c_one, grad_c_two,
        grid=grid,
        in_specs=[index_spec, edge_spec, edge_spec, edge_spec, edge_spec, edge_spec,
                  whole((3 * latent, latent)), whole((latent, latent)),
                  whole((groups * coarse, latent)), whole((rows, groups * coarse)),
                  whole((rows, latent)), whole((rows, latent)), whole((rows, latent)),
                  whole((2 * latent, latent)), whole((latent, latent)),
                  whole((2 * latent, latent)), whole((latent, latent))],
        out_specs=[edge_spec, whole((rows, latent)), whole((pack_rows, latent))],
        scratch=[pltpu.VMEM((rows, 2 * latent), BF), pltpu.VMEM((3 * latent, latent), F32),
                 pltpu.VMEM((latent, latent), F32), pltpu.VMEM((2 * latent, latent), F32),
                 pltpu.VMEM((latent, latent), F32)],
        flops=6 * 10**9, bytes_accessed=10**7, name="edge_back",
    )
    pack_got = exchange(pack.reshape(parts, 16, latent), ("group", "dom"))
    ghost_grad = call(
        functools.partial(ghost_back_kernel, rows=rows), shape((ghosts, latent), BF),
        source, grad_pre, edge_w_one,
        grid=grid,
        in_specs=[index_spec, edge_spec, whole((3 * latent, latent))],
        out_specs=whole((ghosts, latent)),
        scratch=[pltpu.VMEM((ghosts, latent), F32)],
        flops=10**9, bytes_accessed=10**6, name="ghost_back",
    )
    ghost_got = exchange(ghost_grad.reshape(domains, slots, latent), "dom").reshape(ghosts, latent)
    own_local, grad_edges = call(
        own_back_kernel,
        [shape((rows, latent), F32), shape((edges, latent), F32)],
        source, target, grad_pre, edge_cotangent, node_local, edge_w_one,
        grid=grid,
        in_specs=[index_spec, index_spec, edge_spec, edge_spec, whole((rows, latent)),
                  whole((3 * latent, latent))],
        out_specs=[whole((rows, latent)), edge_spec],
        scratch=[pltpu.VMEM((rows, latent), F32), pltpu.VMEM((rows, latent), F32)],
        flops=4 * 10**9, bytes_accessed=5 * 10**6, name="own_back",
    )
    pack_sum = call(
        add_parts_kernel, shape((parts, 16, latent), BF), pack_got,
        flops=10**6, bytes_accessed=10**6, name="add_parts",
    )
    pack_all = exchange(pack_sum, ("group", "dom")).reshape(pack_rows, latent)
    grad_nodes = call(
        add_back_kernel, shape((rows, latent), F32), boundary, asked, ghost_got, own_local,
        flops=10**9, bytes_accessed=10**6, name="add_back",
    )
    edge_scale = (edges * parts) ** (-0.5)
    node_scale = (rows * parts) ** (-0.5)
    coarse_scale = (coarse * parts) ** (-0.5)
    weight_grads = call(
        functools.partial(
            scale_kernel,
            scales=(edge_scale, edge_scale, node_scale, node_scale, coarse_scale, coarse_scale),
        ),
        [shape((size * latent, latent), F32) for size in (3, 1, 2, 1, 2, 1)],
        pack_all,
        flops=10**6, bytes_accessed=10**6, name="scale",
    )
    return (grad_nodes, grad_edges, grad_coarse, *weight_grads)


def solution(mesh):
    rows = P(("group", "dom"), None)
    cube = P(("group", "dom"), None, None)
    line = P(("group", "dom"))
    placed = (
        rows, rows, rows, P(), P(), P(), P(), P(), P(), line, line, rows, cube, rows, rows, cube,
        rows, rows, rows,
    )
    return jax.shard_map(
        local,
        mesh=mesh,
        in_specs=placed,
        out_specs=(rows, rows, rows, P(), P(), P(), P(), P(), P()),
        check_vma=False,
    )
```

```python
import functools

import jax
import jax.numpy as jnp
from jax import lax
from jax.experimental import pallas as pl
from jax.experimental.pallas import tpu as pltpu
from jax.sharding import PartitionSpec as P

NORM_EPSILON = 1e-05
POOL_SHARE = 0.25
BF = jnp.bfloat16
F32 = jnp.float32
I32 = jnp.int32
LANES = 128


def nn(a, b):
    return lax.dot_general(a, b, (((1,), (0,)), ((), ())), preferred_element_type=F32)


def nt(a, b):
    return lax.dot_general(a, b, (((1,), (1,)), ((), ())), preferred_element_type=F32)


def tn(a, b):
    return lax.dot_general(a, b, (((0,), (0,)), ((), ())), preferred_element_type=F32)


def as_hit(mask):
    return jnp.where(mask, 1.0, 0.0).astype(BF)


def hit_rows(index_row, count, base=0):
    width = index_row.shape[1]
    return as_hit(lax.broadcasted_iota(I32, (count, width), 0) == index_row - base)


def spread_column(index_row):
    width = index_row.shape[1]
    return jnp.transpose(jnp.broadcast_to(index_row, (LANES, width)))


def hit_columns(index_column, count, base=0):
    lane = lax.broadcasted_iota(I32, index_column.shape, 1)
    return jnp.concatenate(
        [as_hit(lane == index_column - (base + LANES * j)) for j in range(count // LANES)], axis=1
    )


def halves(table):
    half = table.shape[0] // 2
    return jnp.concatenate([table[:half], table[half:]], axis=1)


def pick_rows(index_column, table_halves):
    half = table_halves.shape[0]
    upper = index_column >= half
    wide = nn(hit_columns(jnp.where(upper, index_column - half, index_column), half), table_halves)
    return jnp.where(upper, wide[:, LANES:], wide[:, :LANES])


def sum_rows(index_row, index_column, values, half):
    upper = index_column >= half
    nothing = jnp.zeros_like(values)
    both = jnp.concatenate(
        [jnp.where(upper, nothing, values), jnp.where(upper, values, nothing)], axis=1
    )
    return nn(hit_rows(jnp.where(index_row >= half, index_row - half, index_row), half), both)


def unfold(sums):
    return jnp.concatenate([sums[:, :LANES], sums[:, LANES:]], axis=0)


def split_wide(values):
    high = values.astype(BF)
    low = (values - high.astype(F32)).astype(BF)
    return jnp.concatenate([high, low], axis=1)


def fold_wide(values):
    return values[:, :LANES] + values[:, LANES:]


def times_transposed(values, weights):
    return nt(split_wide(values), jnp.concatenate([weights, weights], axis=1))


def mean_lanes(values):
    return jnp.mean(values, axis=-1, keepdims=True)


def norm_parts(values):
    centred = values - mean_lanes(values)
    inv_std = lax.rsqrt(mean_lanes(centred * centred) + NORM_EPSILON)
    return centred * inv_std, inv_std


def norm_back(normed, inv_std, grad_in):
    return inv_std * (grad_in - mean_lanes(grad_in) - normed * mean_lanes(grad_in * normed))


def sigmoid(values):
    return 1.0 / (1.0 + jnp.exp(-values))


def slope(values, sig):
    return sig * (1.0 + values * (1.0 - sig))


def spread_kernel(wanted_ref, out_ref):
    domains, slots = wanted_ref.shape
    ghosts = out_ref.shape[0]
    first = lax.broadcasted_iota(I32, (ghosts, domains), 0) // slots
    pick = as_hit(first == lax.broadcasted_iota(I32, (ghosts, domains), 1))
    by_owner = nn(pick, wanted_ref[...].astype(F32).astype(BF))
    slot = lax.broadcasted_iota(I32, (ghosts, slots), 0) % slots
    own = jnp.where(slot == lax.broadcasted_iota(I32, (ghosts, slots), 1), by_owner, 0.0).astype(BF)
    out_ref[...] = nn(own, jnp.ones((slots, LANES), BF)).astype(BF)


def share_kernel(boundary_ref, wanted_ref, nodes_ref, out_ref):
    border = boundary_ref.shape[1]
    shared = pick_rows(spread_column(boundary_ref[...]), halves(nodes_ref[...])).astype(BF)
    wanted = wanted_ref[...].astype(F32).astype(I32)
    out_ref[...] = nn(hit_columns(wanted, border), shared).astype(BF)


def route_kernel(group_ref, count_ref, order_ref, *refs, coarse):
    slot_refs, out_ref = refs[:-1], refs[-1]
    groups = len(slot_refs)
    capacity = slot_refs[0].shape[1]
    rows = order_ref.shape[1]
    here = group_ref[0, 0]
    place = lax.broadcasted_iota(I32, (8, rows), 1)
    owner = jnp.zeros((8, rows), I32)
    goal = jnp.zeros((8, rows), I32)
    for ahead, slot_ref in enumerate(slot_refs):
        k = lax.rem(here + ahead, groups)
        start = 0
        for other in range(groups - 1):
            start = start + jnp.where(other < k, count_ref[0, other], 0)
        line = jnp.concatenate(
            [slot_ref[pl.ds(here, 1), :], jnp.zeros((1, rows - capacity), I32)], axis=1
        )
        line = pltpu.roll(jnp.broadcast_to(line, (8, rows)), start, 1)
        inside = (place >= start) & (place < start + count_ref[0, k])
        owner = jnp.where(inside, ahead, owner)
        goal = jnp.where(inside, line, goal)
    digits = jnp.where(lax.broadcasted_iota(I32, (8, rows), 0) == 0, owner, goal)
    by_row = nt(digits.astype(F32).astype(BF), hit_rows(order_ref[...], rows))
    out_ref[...] = (by_row[0:1, :] * coarse + by_row[1:2, :]).astype(I32)


def edge_first_kernel(source_ref, target_ref, nodes_ref, src_ref, tgt_ref):
    nodes = halves(nodes_ref[...])
    src_ref[...] = pick_rows(spread_column(source_ref[...]), nodes).astype(BF)
    tgt_ref[...] = pick_rows(spread_column(target_ref[...]), nodes).astype(BF)


def edge_second_kernel(
    source_ref, target_ref, src_in_ref, tgt_ref, edges_ref, ghosts_ref, w1_ref, w2_ref,
    nodes_ref, v1_ref, v2_ref, goal_ref, node_cot_ref,
    pre_ref, src_ref, summed_ref, *rest,
):
    send_refs, total = rest[:-1], rest[-1]
    step = pl.program_id(0)
    rows = nodes_ref.shape[0]

    @pl.when(step == 0)
    def _():
        total[...] = jnp.zeros_like(total)

    found = pick_rows(spread_column(source_ref[...]) - rows, halves(ghosts_ref[...])).astype(BF)
    src = src_in_ref[...] + found
    src_ref[...] = src
    pre = nn(jnp.concatenate([src, tgt_ref[...], edges_ref[...]], axis=1), w1_ref[...])
    pre_ref[...] = pre
    hidden = (pre * sigmoid(pre)).astype(BF)
    message, _ = norm_parts(nn(hidden, w2_ref[...]))
    target = target_ref[...]
    total[...] += sum_rows(target, spread_column(target), message.astype(BF), rows // 2)

    @pl.when(step == pl.num_programs(0) - 1)
    def _():
        summed = unfold(total[...]).astype(BF)
        summed_ref[...] = summed
        nodes = nodes_ref[...]
        pre_node = nn(jnp.concatenate([nodes, summed], axis=1), v1_ref[...])
        hidden_node = (pre_node * sigmoid(pre_node)).astype(BF)
        normed, _ = norm_parts(nn(hidden_node, v2_ref[...]))
        updated = (nodes.astype(F32) + normed).astype(BF)
        coarse = send_refs[0].shape[0] // 2
        both = jnp.concatenate([updated, node_cot_ref[...]], axis=1)
        pooled = nn(hit_rows(goal_ref[...], len(send_refs) * coarse), both).astype(BF)
        for k, send_ref in enumerate(send_refs):
            send_ref[:coarse, :] = pooled[k * coarse : (k + 1) * coarse, :LANES]
            send_ref[coarse:, :] = pooled[k * coarse : (k + 1) * coarse, LANES:]


def coarse_kernel(feat_ref, cot_ref, w1_ref, w2_ref, *refs):
    got_refs, (grad_ref, back_ref, g1_ref, g2_ref) = refs[:-4], refs[-4:]
    coarse = feat_ref.shape[0]
    got = got_refs[0][...].astype(F32)
    for got_ref in got_refs[1:]:
        got = got + got_ref[...].astype(F32)
    pooled = (got[:coarse] * POOL_SHARE).astype(BF)
    cot = cot_ref[...].astype(F32)
    grad_out = (cot + got[coarse:]).astype(BF)
    joined = jnp.concatenate([feat_ref[...], pooled], axis=1)
    pre = nn(joined, w1_ref[...])
    sig = sigmoid(pre)
    hidden = (pre * sig).astype(BF)
    g2_ref[...] = tn(hidden, grad_out)
    grad_pre = (nt(grad_out, w2_ref[...]) * slope(pre, sig)).astype(BF)
    g1_ref[...] = tn(joined, grad_pre)
    grad_in = nt(grad_pre, w1_ref[...])
    grad_ref[...] = cot + grad_in[:, :LANES]
    back_ref[...] = (grad_in[:, LANES:] * POOL_SHARE).astype(BF)


def edge_back_kernel(
    target_ref, pre_ref, src_ref, tgt_ref, edges_ref, cot_ref, w1_ref, w2_ref,
    goal_ref, node_cot_ref, nodes_ref, summed_ref, v1_ref, v2_ref, c1_ref, c2_ref, *rest,
):
    gp_refs = rest[:-8]
    grad_pre_ref, local_ref, pack_ref, wide, gw1, gw2, gv1, gv2 = rest[-8:]
    step = pl.program_id(0)

    @pl.when(step == 0)
    def _():
        gw1[...] = jnp.zeros_like(gw1)
        gw2[...] = jnp.zeros_like(gw2)
        table = halves(jnp.concatenate([gp_ref[...] for gp_ref in gp_refs], axis=0))
        from_coarse = pick_rows(spread_column(goal_ref[...]), table)
        updated_grad = node_cot_ref[...].astype(F32) + from_coarse
        joined = jnp.concatenate([nodes_ref[...], summed_ref[...]], axis=1)
        pre = nn(joined, v1_ref[...])
        sig = sigmoid(pre)
        hidden = (pre * sig).astype(BF)
        normed, inv_std = norm_parts(nn(hidden, v2_ref[...]))
        grad_norm = norm_back(normed, inv_std, updated_grad).astype(BF)
        gv2[...] = tn(hidden, grad_norm)
        grad_pre = (nt(grad_norm, v2_ref[...]) * slope(pre, sig)).astype(BF)
        gv1[...] = tn(joined, grad_pre)
        grad_in = nt(grad_pre, v1_ref[...])
        local_ref[...] = updated_grad + grad_in[:, :LANES]
        wide[...] = halves(grad_in[:, LANES:].astype(BF))

    from_node = pick_rows(spread_column(target_ref[...]), wide[...])
    message_grad = cot_ref[...].astype(F32) + from_node
    pre = pre_ref[...]
    sig = sigmoid(pre)
    hidden = (pre * sig).astype(BF)
    normed, inv_std = norm_parts(nn(hidden, w2_ref[...]))
    grad_norm = norm_back(normed, inv_std, message_grad).astype(BF)
    gw2[...] += tn(hidden, grad_norm)
    grad_pre = (nt(grad_norm, w2_ref[...]) * slope(pre, sig)).astype(BF)
    grad_pre_ref[...] = grad_pre
    stacked = jnp.concatenate([src_ref[...], tgt_ref[...], edges_ref[...]], axis=1)
    gw1[...] += tn(stacked, grad_pre)

    @pl.when(step == pl.num_programs(0) - 1)
    def _():
        place = 0
        for part in (gw1, gw2, gv1, gv2, c1_ref, c2_ref):
            size = part.shape[0]
            pack_ref[place : place + size, :] = part[...].astype(BF)
            place += size
        pack_ref[place:, :] = jnp.zeros((pack_ref.shape[0] - place, LANES), BF)


def ghost_back_kernel(source_ref, grad_pre_ref, w1_ref, pack_ref, out_ref, total, *, rows):
    step = pl.program_id(0)

    @pl.when(step == 0)
    def _():
        total[...] = jnp.zeros_like(total)

    source = source_ref[...] - rows
    total[...] += sum_rows(source, spread_column(source), grad_pre_ref[...], total.shape[0])

    @pl.when(step == pl.num_programs(0) - 1)
    def _():
        ghost = times_transposed(unfold(total[...]), w1_ref[:LANES, :]).astype(BF)
        domains, both, _ = out_ref.shape
        share = pack_ref.shape[0] // domains
        out_ref[:, :share, :] = pack_ref[...].reshape(domains, share, LANES)
        out_ref[:, share:, :] = ghost.reshape(domains, both - share, LANES)


def own_back_kernel(
    source_ref, target_ref, grad_pre_ref, cot_ref, local_ref, w1_ref,
    out_ref, edges_ref, by_source, by_target,
):
    step = pl.program_id(0)
    half = by_source.shape[0]

    @pl.when(step == 0)
    def _():
        by_source[...] = jnp.zeros_like(by_source)
        by_target[...] = jnp.zeros_like(by_target)

    grad_pre = grad_pre_ref[...]
    source, target = source_ref[...], target_ref[...]
    by_source[...] += sum_rows(source, spread_column(source), grad_pre, half)
    by_target[...] += sum_rows(target, spread_column(target), grad_pre, half)
    edges_ref[...] = cot_ref[...].astype(F32) + nt(grad_pre, w1_ref[2 * LANES :, :])

    @pl.when(step == pl.num_programs(0) - 1)
    def _():
        out_ref[...] = (
            local_ref[...]
            + times_transposed(unfold(by_source[...]), w1_ref[:LANES, :])
            + times_transposed(unfold(by_target[...]), w1_ref[LANES : 2 * LANES, :])
        )


def add_back_kernel(boundary_ref, wanted_ref, got_ref, local_ref, out_ref):
    rows = local_ref.shape[0]
    border = boundary_ref.shape[1]
    wanted = jnp.transpose(wanted_ref[...].astype(F32))[0:1, :].astype(I32)
    slots = wanted.shape[1] // got_ref.shape[0]
    got = got_ref[:, got_ref.shape[1] - slots :, :].reshape(wanted.shape[1], LANES)
    border_grad = nn(hit_rows(wanted, border), got)
    out_ref[...] = local_ref[...] + fold_wide(
        nn(hit_rows(boundary_ref[...], rows), split_wide(border_grad))
    )


def add_parts_kernel(got_ref, out_ref):
    size = out_ref.shape[0]
    total = got_ref[0, :size, :].astype(F32)
    for k in range(1, got_ref.shape[0]):
        total = total + got_ref[k, :size, :].astype(F32)
    out_ref[...] = total


def add_groups_kernel(*refs):
    part_refs, out_ref = refs[:-1], refs[-1]
    total = part_refs[0][...]
    for part_ref in part_refs[1:]:
        total = total + part_ref[...]
    total = total.astype(BF)
    for k in range(out_ref.shape[0]):
        out_ref[k] = total


def scale_kernel(pack_ref, *out_refs, scales):
    place = 0
    for out_ref, scale in zip(out_refs, scales):
        size = out_ref.shape[0]
        out_ref[...] = pack_ref[place : place + size, :].astype(F32) * scale
        place += size


def whole(shape):
    zeros = (0,) * len(shape)
    return pl.BlockSpec(shape, lambda *_: zeros)


def call(kernel, out_shapes, *args, flops=0, bytes_accessed=0, in_specs=None, out_specs=None,
         grid=None, scratch=(), name=None, vmem=40):
    single = not isinstance(out_shapes, (list, tuple))
    extra = {}
    if grid is not None:
        extra["grid"] = grid
    if in_specs is not None:
        extra["in_specs"] = in_specs
    if out_specs is not None:
        extra["out_specs"] = out_specs
    return pl.pallas_call(
        kernel,
        out_shape=out_shapes if single else list(out_shapes),
        scratch_shapes=list(scratch),
        compiler_params=pltpu.CompilerParams(vmem_limit_bytes=vmem * 2**20),
        cost_estimate=pl.CostEstimate(
            flops=flops, bytes_accessed=bytes_accessed, transcendentals=0
        ),
        name=name,
        **extra,
    )(*args)


def local(
    node_features, edge_features, coarse_features,
    edge_w_one, edge_w_two, node_w_one, node_w_two, coarse_w_one, coarse_w_two,
    edge_source, edge_target, boundary, ghost_pos, restr_order, restr_count, coarse_slot,
    node_cotangent, edge_cotangent, coarse_cotangent,
):
    rows, latent = node_features.shape
    edges = edge_features.shape[0]
    coarse = coarse_features.shape[0]
    groups = lax.axis_size("group")
    domains = lax.axis_size("dom")
    parts = groups * domains
    slots = ghost_pos.shape[2]
    ghosts = domains * slots
    shape = jax.ShapeDtypeStruct
    block = 1024
    grid = (edges // block,)
    index_spec = pl.BlockSpec((1, block), lambda i: (0, i))
    edge_spec = pl.BlockSpec((block, latent), lambda i: (i, 0))
    exchange = functools.partial(lax.all_to_all, split_axis=0, concat_axis=0, tiled=True)

    def turned(step):
        return [(k, (k - step) % groups) for k in range(groups)]

    source = edge_source.reshape(1, edges)
    target = edge_target.reshape(1, edges)
    spread = call(
        spread_kernel, shape((ghosts, latent), BF), ghost_pos.reshape(domains, slots),
        flops=10**6, bytes_accessed=10**5, name="spread", vmem=8,
    )
    asked = exchange(spread.reshape(domains, slots, latent), "dom").reshape(ghosts, latent)
    slot_list = coarse_slot.reshape(groups, -1)
    here = lax.axis_index("group").astype(I32).reshape(1, 1)

    src_own, tgt_rows = call(
        edge_first_kernel,
        [shape((edges, latent), BF), shape((edges, latent), BF)],
        source, target, node_features,
        grid=grid,
        in_specs=[index_spec, index_spec, whole((rows, latent))],
        out_specs=[edge_spec, edge_spec],
        flops=4 * 10**9, bytes_accessed=3 * 10**6, name="edge_first", vmem=61,
    )
    asked, src_own, tgt_rows = lax.optimization_barrier((asked, src_own, tgt_rows))
    share = call(
        share_kernel, shape((ghosts, latent), BF), boundary, asked, node_features,
        flops=10**9, bytes_accessed=10**6, name="share", vmem=16,
    )
    share, slot_list = lax.optimization_barrier((share, slot_list))
    slot_lists = [slot_list] + [
        lax.ppermute(slot_list, "group", turned(ahead)) for ahead in range(1, groups)
    ]
    ghost_rows = exchange(share.reshape(domains, slots, latent), "dom").reshape(ghosts, latent)
    goal = call(
        functools.partial(route_kernel, coarse=coarse), shape((1, rows), I32),
        here, restr_count, restr_order, *slot_lists,
        in_specs=[pl.BlockSpec(memory_space=pltpu.SMEM)] * 2
        + [pl.BlockSpec(memory_space=pltpu.VMEM)] * (1 + groups),
        flops=10**9, bytes_accessed=10**6, name="route", vmem=16,
    )
    pre, src_rows, summed, *send = call(
        edge_second_kernel,
        [shape((edges, latent), F32), shape((edges, latent), BF), shape((rows, latent), BF)]
        + [shape((2 * coarse, latent), BF)] * groups,
        source, target, src_own, tgt_rows, edge_features, ghost_rows, edge_w_one, edge_w_two,
        node_features, node_w_one, node_w_two, goal, node_cotangent,
        grid=grid,
        in_specs=[index_spec, index_spec, edge_spec, edge_spec, edge_spec, whole((ghosts, latent)),
                  whole((3 * latent, latent)), whole((latent, latent)), whole((rows, latent)),
                  whole((2 * latent, latent)), whole((latent, latent)),
                  whole((1, rows)), whole((rows, latent))],
        out_specs=[edge_spec, edge_spec, whole((rows, latent))]
        + [whole((2 * coarse, latent))] * groups,
        scratch=[pltpu.VMEM((rows // 2, 2 * latent), F32)],
        flops=5 * 10**9, bytes_accessed=8 * 10**6, name="edge_second",
    )
    got = [send[0]] + [
        lax.ppermute(send[ahead], "group", turned(-ahead)) for ahead in range(1, groups)
    ]
    grad_coarse, coarse_back, grad_c_one, grad_c_two = call(
        coarse_kernel,
        [shape((coarse, latent), F32), shape((coarse, latent), BF),
         shape((2 * latent, latent), F32), shape((latent, latent), F32)],
        coarse_features, coarse_cotangent, coarse_w_one, coarse_w_two, *got,
        flops=10**8, bytes_accessed=10**6, name="coarse", vmem=16,
    )
    returned = [coarse_back] + [
        lax.ppermute(coarse_back, "group", turned(ahead)) for ahead in range(1, groups)
    ]
    share_rows = 48
    pack_rows = domains * share_rows
    grad_pre, node_local, pack = call(
        edge_back_kernel,
        [shape((edges, latent), BF), shape((rows, latent), F32), shape((pack_rows, latent), BF)],
        target, pre, src_rows, tgt_rows, edge_features, edge_cotangent, edge_w_one, edge_w_two,
        goal, node_cotangent, node_features, summed, node_w_one, node_w_two,
        grad_c_one, grad_c_two, *returned,
        grid=grid,
        in_specs=[index_spec, edge_spec, edge_spec, edge_spec, edge_spec, edge_spec,
                  whole((3 * latent, latent)), whole((latent, latent)),
                  whole((1, rows)),
                  whole((rows, latent)), whole((rows, latent)), whole((rows, latent)),
                  whole((2 * latent, latent)), whole((latent, latent)),
                  whole((2 * latent, latent)), whole((latent, latent))]
        + [whole((coarse, latent))] * groups,
        out_specs=[edge_spec, whole((rows, latent)), whole((pack_rows, latent))],
        scratch=[pltpu.VMEM((rows // 2, 2 * latent), BF), pltpu.VMEM((3 * latent, latent), F32),
                 pltpu.VMEM((latent, latent), F32), pltpu.VMEM((2 * latent, latent), F32),
                 pltpu.VMEM((latent, latent), F32)],
        flops=6 * 10**9, bytes_accessed=10**7, name="edge_back",
    )
    joint_shape = (domains, share_rows + slots, latent)
    joint = call(
        functools.partial(ghost_back_kernel, rows=rows), shape(joint_shape, BF),
        source, grad_pre, edge_w_one, pack,
        grid=grid,
        in_specs=[index_spec, edge_spec, whole((3 * latent, latent)), whole((pack_rows, latent))],
        out_specs=whole(joint_shape),
        scratch=[pltpu.VMEM((ghosts // 2, 2 * latent), F32)],
        flops=10**9, bytes_accessed=10**6, name="ghost_back", vmem=24,
    )
    own_local, grad_edges = call(
        own_back_kernel,
        [shape((rows, latent), F32), shape((edges, latent), F32)],
        source, target, grad_pre, edge_cotangent, node_local, edge_w_one,
        grid=grid,
        in_specs=[index_spec, index_spec, edge_spec, edge_spec, whole((rows, latent)),
                  whole((3 * latent, latent))],
        out_specs=[whole((rows, latent)), edge_spec],
        scratch=[pltpu.VMEM((rows // 2, 2 * latent), F32)] * 2,
        flops=4 * 10**9, bytes_accessed=5 * 10**6, name="own_back",
    )
    joint_got, own_local = lax.optimization_barrier((exchange(joint, "dom"), own_local))
    part_sum = call(
        add_parts_kernel, shape((share_rows, latent), F32), joint_got,
        flops=10**6, bytes_accessed=10**6, name="add_parts", vmem=16,
    )
    part_sums = [part_sum] + [
        lax.ppermute(part_sum, "group", turned(ahead)) for ahead in range(1, groups)
    ]
    pack_sum = call(
        add_groups_kernel, shape((domains, share_rows, latent), BF), *part_sums,
        flops=10**6, bytes_accessed=10**6, name="add_groups", vmem=16,
    )
    pack_all = exchange(pack_sum, "dom").reshape(pack_rows, latent)
    grad_nodes = call(
        add_back_kernel, shape((rows, latent), F32), boundary, asked, joint_got, own_local,
        flops=10**9, bytes_accessed=10**6, name="add_back", vmem=16,
    )
    edge_scale = (edges * parts) ** (-0.5)
    node_scale = (rows * parts) ** (-0.5)
    coarse_scale = (coarse * parts) ** (-0.5)
    weight_grads = call(
        functools.partial(
            scale_kernel,
            scales=(edge_scale, edge_scale, node_scale, node_scale, coarse_scale, coarse_scale),
        ),
        [shape((size * latent, latent), F32) for size in (3, 1, 2, 1, 2, 1)],
        pack_all,
        flops=10**6, bytes_accessed=10**6, name="scale", vmem=16,
    )
    return (grad_nodes, grad_edges, grad_coarse, *weight_grads)


def solution(mesh):
    rows = P(("group", "dom"), None)
    cube = P(("group", "dom"), None, None)
    line = P(("group", "dom"))
    placed = (
        rows, rows, rows, P(), P(), P(), P(), P(), P(), line, line, rows, cube, rows, rows, cube,
        rows, rows, rows,
    )
    return jax.shard_map(
        local,
        mesh=mesh,
        in_specs=placed,
        out_specs=(rows, rows, rows, P(), P(), P(), P(), P(), P()),
        check_vma=False,
    )
```

```python
import functools

import jax
import jax.numpy as jnp
from jax import lax
from jax.experimental import pallas as pl
from jax.experimental.pallas import tpu as pltpu
from jax.sharding import PartitionSpec as P

NORM_EPSILON = 1e-05
POOL_SHARE = 0.25
BF = jnp.bfloat16
F32 = jnp.float32
I32 = jnp.int32
LANES = 128
SECOND_SUB = 512
BACK_SUB = 2048


def nn(a, b):
    return lax.dot_general(a, b, (((1,), (0,)), ((), ())), preferred_element_type=F32)


def nt(a, b):
    return lax.dot_general(a, b, (((1,), (1,)), ((), ())), preferred_element_type=F32)


def tn(a, b):
    return lax.dot_general(a, b, (((0,), (0,)), ((), ())), preferred_element_type=F32)


def as_hit(mask):
    return jnp.where(mask, 1.0, 0.0).astype(BF)


def hit_rows(index_row, count, base=0):
    width = index_row.shape[1]
    return as_hit(lax.broadcasted_iota(I32, (count, width), 0) == index_row - base)


def spread_column(index_row):
    width = index_row.shape[1]
    return jnp.transpose(jnp.broadcast_to(index_row, (LANES, width)))


def hit_columns(index_column, count, base=0):
    lane = lax.broadcasted_iota(I32, index_column.shape, 1)
    return jnp.concatenate(
        [as_hit(lane == index_column - (base + LANES * j)) for j in range(count // LANES)], axis=1
    )


def halves(table):
    half = table.shape[0] // 2
    return jnp.concatenate([table[:half], table[half:]], axis=1)


def pick_rows(index_column, table_halves):
    half = table_halves.shape[0]
    upper = index_column >= half
    wide = nn(hit_columns(jnp.where(upper, index_column - half, index_column), half), table_halves)
    return jnp.where(upper, wide[:, LANES:], wide[:, :LANES])


def sum_rows(index_row, index_column, values, half):
    upper = index_column >= half
    nothing = jnp.zeros_like(values)
    both = jnp.concatenate(
        [jnp.where(upper, nothing, values), jnp.where(upper, values, nothing)], axis=1
    )
    return nn(hit_rows(jnp.where(index_row >= half, index_row - half, index_row), half), both)


def unfold(sums):
    return jnp.concatenate([sums[:, :LANES], sums[:, LANES:]], axis=0)


def split_wide(values):
    high = values.astype(BF)
    low = (values - high.astype(F32)).astype(BF)
    return jnp.concatenate([high, low], axis=1)


def fold_wide(values):
    return values[:, :LANES] + values[:, LANES:]


def times_transposed(values, weights):
    return nt(split_wide(values), jnp.concatenate([weights, weights], axis=1))


def mean_lanes(values):
    return jnp.mean(values, axis=-1, keepdims=True)


def norm_parts(values):
    centred = values - mean_lanes(values)
    inv_std = lax.rsqrt(mean_lanes(centred * centred) + NORM_EPSILON)
    return centred * inv_std, inv_std


def norm_back(normed, inv_std, grad_in):
    return inv_std * (grad_in - mean_lanes(grad_in) - normed * mean_lanes(grad_in * normed))


def sigmoid(values):
    return 1.0 / (1.0 + jnp.exp(-values))


def slope(values, sig):
    return sig * (1.0 + values * (1.0 - sig))


def spread_kernel(wanted_ref, out_ref):
    domains, slots = wanted_ref.shape
    ghosts = out_ref.shape[0]
    first = lax.broadcasted_iota(I32, (ghosts, domains), 0) // slots
    pick = as_hit(first == lax.broadcasted_iota(I32, (ghosts, domains), 1))
    by_owner = nn(pick, wanted_ref[...].astype(F32).astype(BF))
    slot = lax.broadcasted_iota(I32, (ghosts, slots), 0) % slots
    own = jnp.where(slot == lax.broadcasted_iota(I32, (ghosts, slots), 1), by_owner, 0.0).astype(BF)
    out_ref[...] = nn(own, jnp.ones((slots, LANES), BF)).astype(BF)


def share_kernel(boundary_ref, wanted_ref, nodes_ref, out_ref):
    border = boundary_ref.shape[1]
    shared = pick_rows(spread_column(boundary_ref[...]), halves(nodes_ref[...])).astype(BF)
    wanted = wanted_ref[...].astype(F32).astype(I32)
    out_ref[...] = nn(hit_columns(wanted, border), shared).astype(BF)


def route_kernel(group_ref, count_ref, order_ref, *refs, coarse):
    slot_refs, out_ref = refs[:-1], refs[-1]
    groups = len(slot_refs)
    capacity = slot_refs[0].shape[1]
    rows = order_ref.shape[1]
    here = group_ref[0, 0]
    place = lax.broadcasted_iota(I32, (8, rows), 1)
    owner = jnp.zeros((8, rows), I32)
    goal = jnp.zeros((8, rows), I32)
    for ahead, slot_ref in enumerate(slot_refs):
        k = lax.rem(here + ahead, groups)
        start = 0
        for other in range(groups - 1):
            start = start + jnp.where(other < k, count_ref[0, other], 0)
        line = jnp.concatenate(
            [slot_ref[pl.ds(here, 1), :], jnp.zeros((1, rows - capacity), I32)], axis=1
        )
        line = pltpu.roll(jnp.broadcast_to(line, (8, rows)), start, 1)
        inside = (place >= start) & (place < start + count_ref[0, k])
        owner = jnp.where(inside, ahead, owner)
        goal = jnp.where(inside, line, goal)
    digits = jnp.where(lax.broadcasted_iota(I32, (8, rows), 0) == 0, owner, goal)
    by_row = nt(digits.astype(F32).astype(BF), hit_rows(order_ref[...], rows))
    out_ref[...] = (by_row[0:1, :] * coarse + by_row[1:2, :]).astype(I32)


def edge_first_kernel(source_ref, target_ref, nodes_ref, src_ref, tgt_ref):
    nodes = halves(nodes_ref[...])
    src_ref[...] = pick_rows(spread_column(source_ref[...]), nodes).astype(BF)
    tgt_ref[...] = pick_rows(spread_column(target_ref[...]), nodes).astype(BF)


def edge_second_kernel(
    source_ref, target_ref, src_in_ref, tgt_ref, edges_ref, ghosts_ref, w1_ref, w2_ref,
    nodes_ref, v1_ref, v2_ref, goal_ref, node_cot_ref,
    pre_ref, src_ref, summed_ref, *rest,
):
    send_refs, total = rest[:-1], rest[-1]
    step = pl.program_id(0)
    rows = nodes_ref.shape[0]

    @pl.when(step == 0)
    def _():
        total[...] = jnp.zeros_like(total)

    ghosts = halves(ghosts_ref[...])
    from_ghost = spread_column(source_ref[...]) - rows
    target = target_ref[...]
    messages = []
    for part in range(0, target.shape[1], SECOND_SUB):
        here = slice(part, part + SECOND_SUB)
        src = src_in_ref[here, :] + pick_rows(from_ghost[here], ghosts).astype(BF)
        src_ref[here, :] = src
        pre = nn(jnp.concatenate([src, tgt_ref[here, :], edges_ref[here, :]], axis=1), w1_ref[...])
        pre_ref[here, :] = pre
        hidden = (pre * sigmoid(pre)).astype(BF)
        message, _ = norm_parts(nn(hidden, w2_ref[...]))
        messages.append(message.astype(BF))
    total[...] += sum_rows(
        target, spread_column(target), jnp.concatenate(messages, axis=0), rows // 2
    )

    @pl.when(step == pl.num_programs(0) - 1)
    def _():
        summed = unfold(total[...]).astype(BF)
        summed_ref[...] = summed
        nodes = nodes_ref[...]
        pre_node = nn(jnp.concatenate([nodes, summed], axis=1), v1_ref[...])
        hidden_node = (pre_node * sigmoid(pre_node)).astype(BF)
        normed, _ = norm_parts(nn(hidden_node, v2_ref[...]))
        updated = (nodes.astype(F32) + normed).astype(BF)
        coarse = send_refs[0].shape[0] // 2
        both = jnp.concatenate([updated, node_cot_ref[...]], axis=1)
        pooled = nn(hit_rows(goal_ref[...], len(send_refs) * coarse), both).astype(BF)
        for k, send_ref in enumerate(send_refs):
            send_ref[:coarse, :] = pooled[k * coarse : (k + 1) * coarse, :LANES]
            send_ref[coarse:, :] = pooled[k * coarse : (k + 1) * coarse, LANES:]


def coarse_kernel(feat_ref, cot_ref, w1_ref, w2_ref, *refs):
    got_refs, (grad_ref, back_ref, g1_ref, g2_ref) = refs[:-4], refs[-4:]
    coarse = feat_ref.shape[0]
    got = got_refs[0][...].astype(F32)
    for got_ref in got_refs[1:]:
        got = got + got_ref[...].astype(F32)
    pooled = (got[:coarse] * POOL_SHARE).astype(BF)
    cot = cot_ref[...].astype(F32)
    grad_out = (cot + got[coarse:]).astype(BF)
    joined = jnp.concatenate([feat_ref[...], pooled], axis=1)
    pre = nn(joined, w1_ref[...])
    sig = sigmoid(pre)
    hidden = (pre * sig).astype(BF)
    g2_ref[...] = tn(hidden, grad_out)
    grad_pre = (nt(grad_out, w2_ref[...]) * slope(pre, sig)).astype(BF)
    g1_ref[...] = tn(joined, grad_pre)
    grad_in = nt(grad_pre, w1_ref[...])
    grad_ref[...] = cot + grad_in[:, :LANES]
    back_ref[...] = (grad_in[:, LANES:] * POOL_SHARE).astype(BF)


def edge_back_kernel(
    source_ref, target_ref, pre_ref, src_ref, tgt_ref, edges_ref, cot_ref, w1_ref, w2_ref,
    goal_ref, node_cot_ref, nodes_ref, summed_ref, v1_ref, v2_ref, c1_ref, c2_ref, *rest,
):
    gp_refs = rest[:-10]
    grad_pre_ref, local_ref, joint_ref, wide, gw1, gw2, gv1, gv2, by_ghost, pack_ref = rest[-10:]
    step = pl.program_id(0)
    rows = nodes_ref.shape[0]

    @pl.when(step == 0)
    def _():
        by_ghost[...] = jnp.zeros_like(by_ghost)
        gw1[...] = jnp.zeros_like(gw1)
        gw2[...] = jnp.zeros_like(gw2)
        table = halves(jnp.concatenate([gp_ref[...] for gp_ref in gp_refs], axis=0))
        from_coarse = pick_rows(spread_column(goal_ref[...]), table)
        updated_grad = node_cot_ref[...].astype(F32) + from_coarse
        joined = jnp.concatenate([nodes_ref[...], summed_ref[...]], axis=1)
        pre = nn(joined, v1_ref[...])
        sig = sigmoid(pre)
        hidden = (pre * sig).astype(BF)
        normed, inv_std = norm_parts(nn(hidden, v2_ref[...]))
        grad_norm = norm_back(normed, inv_std, updated_grad).astype(BF)
        gv2[...] = tn(hidden, grad_norm)
        grad_pre = (nt(grad_norm, v2_ref[...]) * slope(pre, sig)).astype(BF)
        gv1[...] = tn(joined, grad_pre)
        grad_in = nt(grad_pre, v1_ref[...])
        local_ref[...] = updated_grad + grad_in[:, :LANES]
        wide[...] = halves(grad_in[:, LANES:].astype(BF))

    target = spread_column(target_ref[...])
    hiddens, grad_norms, grad_pres = [], [], []
    for part in range(0, target.shape[0], BACK_SUB):
        here = slice(part, part + BACK_SUB)
        message_grad = cot_ref[here, :].astype(F32) + pick_rows(target[here], wide[...])
        pre = pre_ref[here, :]
        sig = sigmoid(pre)
        hidden = (pre * sig).astype(BF)
        normed, inv_std = norm_parts(nn(hidden, w2_ref[...]))
        grad_norm = norm_back(normed, inv_std, message_grad).astype(BF)
        grad_pre = (nt(grad_norm, w2_ref[...]) * slope(pre, sig)).astype(BF)
        hiddens.append(hidden)
        grad_norms.append(grad_norm)
        grad_pres.append(grad_pre)
    grad_pre = jnp.concatenate(grad_pres, axis=0)
    grad_pre_ref[...] = grad_pre
    gw2[...] += tn(jnp.concatenate(hiddens, axis=0), jnp.concatenate(grad_norms, axis=0))
    stacked = jnp.concatenate([src_ref[...], tgt_ref[...], edges_ref[...]], axis=1)
    gw1[...] += tn(stacked, grad_pre)
    source = source_ref[...] - rows
    by_ghost[...] += sum_rows(source, spread_column(source), grad_pre, by_ghost.shape[0])

    @pl.when(step == pl.num_programs(0) - 1)
    def _():
        place = 0
        for part in (gw1, gw2, gv1, gv2, c1_ref, c2_ref):
            size = part.shape[0]
            pack_ref[place : place + size, :] = part[...].astype(BF)
            place += size
        pack_ref[place:, :] = jnp.zeros((pack_ref.shape[0] - place, LANES), BF)
        ghost = times_transposed(unfold(by_ghost[...]), w1_ref[:LANES, :]).astype(BF)
        domains, both, _ = joint_ref.shape
        share = pack_ref.shape[0] // domains
        joint_ref[:, :share, :] = pack_ref[...].reshape(domains, share, LANES)
        joint_ref[:, share:, :] = ghost.reshape(domains, both - share, LANES)


def own_back_kernel(
    source_ref, target_ref, grad_pre_ref, cot_ref, local_ref, w1_ref,
    out_ref, edges_ref, by_source, by_target,
):
    step = pl.program_id(0)
    half = by_source.shape[0]

    @pl.when(step == 0)
    def _():
        by_source[...] = jnp.zeros_like(by_source)
        by_target[...] = jnp.zeros_like(by_target)

    grad_pre = grad_pre_ref[...]
    source, target = source_ref[...], target_ref[...]
    by_source[...] += sum_rows(source, spread_column(source), grad_pre, half)
    by_target[...] += sum_rows(target, spread_column(target), grad_pre, half)
    edges_ref[...] = cot_ref[...].astype(F32) + nt(grad_pre, w1_ref[2 * LANES :, :])

    @pl.when(step == pl.num_programs(0) - 1)
    def _():
        out_ref[...] = (
            local_ref[...]
            + times_transposed(unfold(by_source[...]), w1_ref[:LANES, :])
            + times_transposed(unfold(by_target[...]), w1_ref[LANES : 2 * LANES, :])
        )


def add_back_kernel(boundary_ref, wanted_ref, got_ref, local_ref, out_ref):
    rows = local_ref.shape[0]
    border = boundary_ref.shape[1]
    wanted = jnp.transpose(wanted_ref[...].astype(F32))[0:1, :].astype(I32)
    slots = wanted.shape[1] // got_ref.shape[0]
    got = got_ref[:, got_ref.shape[1] - slots :, :].reshape(wanted.shape[1], LANES)
    border_grad = nn(hit_rows(wanted, border), got)
    out_ref[...] = local_ref[...] + fold_wide(
        nn(hit_rows(boundary_ref[...], rows), split_wide(border_grad))
    )


def add_parts_kernel(got_ref, out_ref):
    size = out_ref.shape[0]
    total = got_ref[0, :size, :].astype(F32)
    for k in range(1, got_ref.shape[0]):
        total = total + got_ref[k, :size, :].astype(F32)
    out_ref[...] = total


def add_groups_kernel(*refs):
    part_refs, out_ref = refs[:-1], refs[-1]
    total = part_refs[0][...]
    for part_ref in part_refs[1:]:
        total = total + part_ref[...]
    total = total.astype(BF)
    for k in range(out_ref.shape[0]):
        out_ref[k] = total


def scale_kernel(pack_ref, *out_refs, scales):
    place = 0
    for out_ref, scale in zip(out_refs, scales):
        size = out_ref.shape[0]
        out_ref[...] = pack_ref[place : place + size, :].astype(F32) * scale
        place += size


def whole(shape):
    zeros = (0,) * len(shape)
    return pl.BlockSpec(shape, lambda *_: zeros)


def call(kernel, out_shapes, *args, flops=0, bytes_accessed=0, in_specs=None, out_specs=None,
         grid=None, scratch=(), name=None, vmem=40):
    single = not isinstance(out_shapes, (list, tuple))
    extra = {}
    if grid is not None:
        extra["grid"] = grid
    if in_specs is not None:
        extra["in_specs"] = in_specs
    if out_specs is not None:
        extra["out_specs"] = out_specs
    return pl.pallas_call(
        kernel,
        out_shape=out_shapes if single else list(out_shapes),
        scratch_shapes=list(scratch),
        compiler_params=pltpu.CompilerParams(vmem_limit_bytes=vmem * 2**20),
        cost_estimate=pl.CostEstimate(
            flops=flops, bytes_accessed=bytes_accessed, transcendentals=0
        ),
        name=name,
        **extra,
    )(*args)


def local(
    node_features, edge_features, coarse_features,
    edge_w_one, edge_w_two, node_w_one, node_w_two, coarse_w_one, coarse_w_two,
    edge_source, edge_target, boundary, ghost_pos, restr_order, restr_count, coarse_slot,
    node_cotangent, edge_cotangent, coarse_cotangent,
):
    rows, latent = node_features.shape
    edges = edge_features.shape[0]
    coarse = coarse_features.shape[0]
    groups = lax.axis_size("group")
    domains = lax.axis_size("dom")
    parts = groups * domains
    slots = ghost_pos.shape[2]
    ghosts = domains * slots
    shape = jax.ShapeDtypeStruct

    def edge_blocks(block):
        return (
            (edges // block,),
            pl.BlockSpec((1, block), lambda i: (0, i)),
            pl.BlockSpec((block, latent), lambda i: (i, 0)),
        )

    exchange = functools.partial(lax.all_to_all, split_axis=0, concat_axis=0, tiled=True)

    def turned(step):
        return [(k, (k - step) % groups) for k in range(groups)]

    source = edge_source.reshape(1, edges)
    target = edge_target.reshape(1, edges)
    spread = call(
        spread_kernel, shape((ghosts, latent), BF), ghost_pos.reshape(domains, slots),
        flops=10**6, bytes_accessed=10**5, name="spread", vmem=8,
    )
    asked = exchange(spread.reshape(domains, slots, latent), "dom").reshape(ghosts, latent)
    slot_list = coarse_slot.reshape(groups, -1)
    here = lax.axis_index("group").astype(I32).reshape(1, 1)

    grid, index_spec, edge_spec = edge_blocks(2048)
    src_own, tgt_rows = call(
        edge_first_kernel,
        [shape((edges, latent), BF), shape((edges, latent), BF)],
        source, target, node_features,
        grid=grid,
        in_specs=[index_spec, index_spec, whole((rows, latent))],
        out_specs=[edge_spec, edge_spec],
        flops=4 * 10**9, bytes_accessed=3 * 10**6, name="edge_first", vmem=61,
    )
    asked, src_own, tgt_rows = lax.optimization_barrier((asked, src_own, tgt_rows))
    share = call(
        share_kernel, shape((ghosts, latent), BF), boundary, asked, node_features,
        flops=10**9, bytes_accessed=10**6, name="share", vmem=16,
    )
    share, slot_list = lax.optimization_barrier((share, slot_list))
    slot_lists = [slot_list] + [
        lax.ppermute(slot_list, "group", turned(ahead)) for ahead in range(1, groups)
    ]
    ghost_rows = exchange(share.reshape(domains, slots, latent), "dom").reshape(ghosts, latent)
    goal = call(
        functools.partial(route_kernel, coarse=coarse), shape((1, rows), I32),
        here, restr_count, restr_order, *slot_lists,
        in_specs=[pl.BlockSpec(memory_space=pltpu.SMEM)] * 2
        + [pl.BlockSpec(memory_space=pltpu.VMEM)] * (1 + groups),
        flops=10**9, bytes_accessed=10**6, name="route", vmem=16,
    )
    grid, index_spec, edge_spec = edge_blocks(4096)
    pre, src_rows, summed, *send = call(
        edge_second_kernel,
        [shape((edges, latent), F32), shape((edges, latent), BF), shape((rows, latent), BF)]
        + [shape((2 * coarse, latent), BF)] * groups,
        source, target, src_own, tgt_rows, edge_features, ghost_rows, edge_w_one, edge_w_two,
        node_features, node_w_one, node_w_two, goal, node_cotangent,
        grid=grid,
        in_specs=[index_spec, index_spec, edge_spec, edge_spec, edge_spec, whole((ghosts, latent)),
                  whole((3 * latent, latent)), whole((latent, latent)), whole((rows, latent)),
                  whole((2 * latent, latent)), whole((latent, latent)),
                  whole((1, rows)), whole((rows, latent))],
        out_specs=[edge_spec, edge_spec, whole((rows, latent))]
        + [whole((2 * coarse, latent))] * groups,
        scratch=[pltpu.VMEM((rows // 2, 2 * latent), F32)],
        flops=5 * 10**9, bytes_accessed=8 * 10**6, name="edge_second",
    )
    got = [send[0]] + [
        lax.ppermute(send[ahead], "group", turned(-ahead)) for ahead in range(1, groups)
    ]
    grad_coarse, coarse_back, grad_c_one, grad_c_two = call(
        coarse_kernel,
        [shape((coarse, latent), F32), shape((coarse, latent), BF),
         shape((2 * latent, latent), F32), shape((latent, latent), F32)],
        coarse_features, coarse_cotangent, coarse_w_one, coarse_w_two, *got,
        flops=10**8, bytes_accessed=10**6, name="coarse", vmem=16,
    )
    returned = [coarse_back] + [
        lax.ppermute(coarse_back, "group", turned(ahead)) for ahead in range(1, groups)
    ]
    share_rows = 48
    pack_rows = domains * share_rows
    grid, index_spec, edge_spec = edge_blocks(4096)
    joint_shape = (domains, share_rows + slots, latent)
    grad_pre, node_local, joint = call(
        edge_back_kernel,
        [shape((edges, latent), BF), shape((rows, latent), F32), shape(joint_shape, BF)],
        source, target, pre, src_rows, tgt_rows, edge_features, edge_cotangent, edge_w_one, edge_w_two,
        goal, node_cotangent, node_features, summed, node_w_one, node_w_two,
        grad_c_one, grad_c_two, *returned,
        grid=grid,
        in_specs=[index_spec, index_spec, edge_spec, edge_spec, edge_spec, edge_spec, edge_spec,
                  whole((3 * latent, latent)), whole((latent, latent)),
                  whole((1, rows)),
                  whole((rows, latent)), whole((rows, latent)), whole((rows, latent)),
                  whole((2 * latent, latent)), whole((latent, latent)),
                  whole((2 * latent, latent)), whole((latent, latent))]
        + [whole((coarse, latent))] * groups,
        out_specs=[edge_spec, whole((rows, latent)), whole(joint_shape)],
        scratch=[pltpu.VMEM((rows // 2, 2 * latent), BF), pltpu.VMEM((3 * latent, latent), F32),
                 pltpu.VMEM((latent, latent), F32), pltpu.VMEM((2 * latent, latent), F32),
                 pltpu.VMEM((latent, latent), F32), pltpu.VMEM((ghosts // 2, 2 * latent), F32),
                 pltpu.VMEM((pack_rows, latent), BF)],
        flops=6 * 10**9, bytes_accessed=10**7, name="edge_back",
    )
    grid, index_spec, edge_spec = edge_blocks(4096)
    own_local, grad_edges = call(
        own_back_kernel,
        [shape((rows, latent), F32), shape((edges, latent), F32)],
        source, target, grad_pre, edge_cotangent, node_local, edge_w_one,
        grid=grid,
        in_specs=[index_spec, index_spec, edge_spec, edge_spec, whole((rows, latent)),
                  whole((3 * latent, latent))],
        out_specs=[whole((rows, latent)), edge_spec],
        scratch=[pltpu.VMEM((rows // 2, 2 * latent), F32)] * 2,
        flops=4 * 10**9, bytes_accessed=5 * 10**6, name="own_back",
    )
    joint_got, own_local = lax.optimization_barrier((exchange(joint, "dom"), own_local))
    part_sum = call(
        add_parts_kernel, shape((share_rows, latent), F32), joint_got,
        flops=10**6, bytes_accessed=10**6, name="add_parts", vmem=16,
    )
    part_sums = [part_sum] + [
        lax.ppermute(part_sum, "group", turned(ahead)) for ahead in range(1, groups)
    ]
    pack_sum = call(
        add_groups_kernel, shape((domains, share_rows, latent), BF), *part_sums,
        flops=10**6, bytes_accessed=10**6, name="add_groups", vmem=16,
    )
    pack_all = exchange(pack_sum, "dom").reshape(pack_rows, latent)
    grad_nodes = call(
        add_back_kernel, shape((rows, latent), F32), boundary, asked, joint_got, own_local,
        flops=10**9, bytes_accessed=10**6, name="add_back", vmem=16,
    )
    edge_scale = (edges * parts) ** (-0.5)
    node_scale = (rows * parts) ** (-0.5)
    coarse_scale = (coarse * parts) ** (-0.5)
    weight_grads = call(
        functools.partial(
            scale_kernel,
            scales=(edge_scale, edge_scale, node_scale, node_scale, coarse_scale, coarse_scale),
        ),
        [shape((size * latent, latent), F32) for size in (3, 1, 2, 1, 2, 1)],
        pack_all,
        flops=10**6, bytes_accessed=10**6, name="scale", vmem=16,
    )
    return (grad_nodes, grad_edges, grad_coarse, *weight_grads)


def solution(mesh):
    rows = P(("group", "dom"), None)
    cube = P(("group", "dom"), None, None)
    line = P(("group", "dom"))
    placed = (
        rows, rows, rows, P(), P(), P(), P(), P(), P(), line, line, rows, cube, rows, rows, cube,
        rows, rows, rows,
    )
    return jax.shard_map(
        local,
        mesh=mesh,
        in_specs=placed,
        out_specs=(rows, rows, rows, P(), P(), P(), P(), P(), P()),
        check_vma=False,
    )
```

```python
import functools

import jax
import jax.numpy as jnp
from jax import lax
from jax.experimental import pallas as pl
from jax.experimental.pallas import tpu as pltpu
from jax.sharding import PartitionSpec as P

NORM_EPSILON = 1e-05
POOL_SHARE = 0.25
BF = jnp.bfloat16
F32 = jnp.float32
I32 = jnp.int32
LANES = 128
SECOND_SUB = 512
BACK_SUB = 2048


def nn(a, b):
    return lax.dot_general(a, b, (((1,), (0,)), ((), ())), preferred_element_type=F32)


def nt(a, b):
    return lax.dot_general(a, b, (((1,), (1,)), ((), ())), preferred_element_type=F32)


def tn(a, b):
    return lax.dot_general(a, b, (((0,), (0,)), ((), ())), preferred_element_type=F32)


def as_hit(mask):
    return jnp.where(mask, 1.0, 0.0).astype(BF)


def hit_rows(index_row, count, base=0):
    width = index_row.shape[1]
    return as_hit(lax.broadcasted_iota(I32, (count, width), 0) == index_row - base)


def spread_column(index_row):
    width = index_row.shape[1]
    return jnp.transpose(jnp.broadcast_to(index_row, (LANES, width)))


def hit_columns(index_column, count, base=0):
    lane = lax.broadcasted_iota(I32, index_column.shape, 1)
    return jnp.concatenate(
        [as_hit(lane == index_column - (base + LANES * j)) for j in range(count // LANES)], axis=1
    )


def halves(table):
    half = table.shape[0] // 2
    return jnp.concatenate([table[:half], table[half:]], axis=1)


def pick_rows(index_column, table_halves):
    half = table_halves.shape[0]
    upper = index_column >= half
    wide = nn(hit_columns(jnp.where(upper, index_column - half, index_column), half), table_halves)
    return jnp.where(upper, wide[:, LANES:], wide[:, :LANES])


def sum_rows(index_row, index_column, values, half):
    upper = index_column >= half
    nothing = jnp.zeros_like(values)
    both = jnp.concatenate(
        [jnp.where(upper, nothing, values), jnp.where(upper, values, nothing)], axis=1
    )
    return nn(hit_rows(jnp.where(index_row >= half, index_row - half, index_row), half), both)


def unfold(sums):
    return jnp.concatenate([sums[:, :LANES], sums[:, LANES:]], axis=0)


def split_wide(values):
    high = values.astype(BF)
    low = (values - high.astype(F32)).astype(BF)
    return jnp.concatenate([high, low], axis=1)


def fold_wide(values):
    return values[:, :LANES] + values[:, LANES:]


def times_transposed(values, weights):
    return nt(split_wide(values), jnp.concatenate([weights, weights], axis=1))


def mean_lanes(values):
    return jnp.mean(values, axis=-1, keepdims=True)


def norm_parts(values):
    centred = values - mean_lanes(values)
    inv_std = lax.rsqrt(mean_lanes(centred * centred) + NORM_EPSILON)
    return centred * inv_std, inv_std


def norm_back(normed, inv_std, grad_in):
    return inv_std * (grad_in - mean_lanes(grad_in) - normed * mean_lanes(grad_in * normed))


def sigmoid(values):
    return 1.0 / (1.0 + jnp.exp(-values))


def slope(values, sig):
    return sig * (1.0 + values * (1.0 - sig))


def spread_kernel(wanted_ref, out_ref):
    _, domains, slots = wanted_ref.shape
    ghosts = out_ref.shape[0]
    first = lax.broadcasted_iota(I32, (ghosts, domains), 0) // slots
    pick = as_hit(first == lax.broadcasted_iota(I32, (ghosts, domains), 1))
    by_owner = nn(pick, wanted_ref[0].astype(F32).astype(BF))
    slot = lax.broadcasted_iota(I32, (ghosts, slots), 0) % slots
    own = jnp.where(slot == lax.broadcasted_iota(I32, (ghosts, slots), 1), by_owner, 0.0).astype(BF)
    out_ref[...] = nn(own, jnp.ones((slots, LANES), BF)).astype(BF)


def share_kernel(boundary_ref, wanted_ref, nodes_ref, out_ref):
    border = boundary_ref.shape[1]
    shared = pick_rows(spread_column(boundary_ref[...]), halves(nodes_ref[...])).astype(BF)
    wanted = wanted_ref[...].astype(F32).astype(I32)
    out_ref[...] = nn(hit_columns(wanted, border), shared).astype(BF)


def pool_kernel(group_ref, count_ref, order_ref, updated_ref, node_cot_ref, *refs):
    groups = (len(refs) - 1) // 2
    slot_refs, out_ref, send_refs = refs[:groups], refs[groups], refs[groups + 1 :]
    coarse = send_refs[0].shape[0] // 2
    capacity = slot_refs[0].shape[1]
    rows = order_ref.shape[1]
    here = group_ref[0, 0]
    place = lax.broadcasted_iota(I32, (8, rows), 1)
    owner = jnp.zeros((8, rows), I32)
    goal = jnp.zeros((8, rows), I32)
    for ahead, slot_ref in enumerate(slot_refs):
        k = lax.rem(here + ahead, groups)
        start = 0
        for other in range(groups - 1):
            start = start + jnp.where(other < k, count_ref[0, other], 0)
        line = jnp.concatenate(
            [slot_ref[pl.ds(here, 1), :], jnp.zeros((1, rows - capacity), I32)], axis=1
        )
        line = pltpu.roll(jnp.broadcast_to(line, (8, rows)), start, 1)
        inside = (place >= start) & (place < start + count_ref[0, k])
        owner = jnp.where(inside, ahead, owner)
        goal = jnp.where(inside, line, goal)
    digits = jnp.where(lax.broadcasted_iota(I32, (8, rows), 0) == 0, owner, goal)
    by_row = nt(digits.astype(F32).astype(BF), hit_rows(order_ref[...], rows))
    goal = (by_row[0:1, :] * coarse + by_row[1:2, :]).astype(I32)
    out_ref[...] = goal
    both = jnp.concatenate([updated_ref[...], node_cot_ref[...]], axis=1)
    pooled = nn(hit_rows(goal, groups * coarse), both).astype(BF)
    for k, send_ref in enumerate(send_refs):
        send_ref[:coarse, :] = pooled[k * coarse : (k + 1) * coarse, :LANES]
        send_ref[coarse:, :] = pooled[k * coarse : (k + 1) * coarse, LANES:]


def edge_first_kernel(source_ref, target_ref, nodes_ref, out_ref):
    nodes = halves(nodes_ref[...])
    out_ref[0] = pick_rows(spread_column(source_ref[...]), nodes).astype(BF)
    out_ref[1] = pick_rows(spread_column(target_ref[...]), nodes).astype(BF)


def edge_second_kernel(
    source_ref, target_ref, own_ref, edges_ref, ghosts_ref, w1_ref, w2_ref,
    nodes_ref, v1_ref, v2_ref,
    pre_ref, src_ref, summed_ref, updated_ref, total,
):
    step = pl.program_id(0)
    rows = nodes_ref.shape[0]

    @pl.when(step == 0)
    def _():
        total[...] = jnp.zeros_like(total)

    ghosts = halves(ghosts_ref[...])
    from_ghost = spread_column(source_ref[...]) - rows
    target = target_ref[...]
    messages = []
    for part in range(0, target.shape[1], SECOND_SUB):
        here = slice(part, part + SECOND_SUB)
        src = own_ref[0, here, :] + pick_rows(from_ghost[here], ghosts).astype(BF)
        src_ref[here, :] = src
        stacked = jnp.concatenate([src, own_ref[1, here, :], edges_ref[here, :]], axis=1)
        pre = nn(stacked, w1_ref[...])
        pre_ref[here, :] = pre
        hidden = (pre * sigmoid(pre)).astype(BF)
        message, _ = norm_parts(nn(hidden, w2_ref[...]))
        messages.append(message.astype(BF))
    total[...] += sum_rows(
        target, spread_column(target), jnp.concatenate(messages, axis=0), rows // 2
    )

    @pl.when(step == pl.num_programs(0) - 1)
    def _():
        summed = unfold(total[...]).astype(BF)
        summed_ref[...] = summed
        nodes = nodes_ref[...]
        pre_node = nn(jnp.concatenate([nodes, summed], axis=1), v1_ref[...])
        hidden_node = (pre_node * sigmoid(pre_node)).astype(BF)
        normed, _ = norm_parts(nn(hidden_node, v2_ref[...]))
        updated_ref[...] = (nodes.astype(F32) + normed).astype(BF)


def coarse_kernel(feat_ref, cot_ref, w1_ref, w2_ref, *refs):
    got_refs, (grad_ref, back_ref, g1_ref, g2_ref) = refs[:-4], refs[-4:]
    coarse = feat_ref.shape[0]
    got = got_refs[0][...].astype(F32)
    for got_ref in got_refs[1:]:
        got = got + got_ref[...].astype(F32)
    pooled = (got[:coarse] * POOL_SHARE).astype(BF)
    cot = cot_ref[...].astype(F32)
    grad_out = (cot + got[coarse:]).astype(BF)
    joined = jnp.concatenate([feat_ref[...], pooled], axis=1)
    pre = nn(joined, w1_ref[...])
    sig = sigmoid(pre)
    hidden = (pre * sig).astype(BF)
    g2_ref[...] = tn(hidden, grad_out)
    grad_pre = (nt(grad_out, w2_ref[...]) * slope(pre, sig)).astype(BF)
    g1_ref[...] = tn(joined, grad_pre)
    grad_in = nt(grad_pre, w1_ref[...])
    grad_ref[...] = cot + grad_in[:, :LANES]
    back_ref[...] = (grad_in[:, LANES:] * POOL_SHARE).astype(BF)


def edge_back_kernel(
    source_ref, target_ref, pre_ref, src_ref, tgt_ref, edges_ref, cot_ref, w1_ref, w2_ref,
    goal_ref, node_cot_ref, nodes_ref, summed_ref, v1_ref, v2_ref, c1_ref, c2_ref, *rest,
):
    gp_refs = rest[:-10]
    grad_pre_ref, local_ref, joint_ref, wide, gw1, gw2, gv1, gv2, by_ghost, pack_ref = rest[-10:]
    step = pl.program_id(0)
    rows = nodes_ref.shape[0]

    @pl.when(step == 0)
    def _():
        by_ghost[...] = jnp.zeros_like(by_ghost)
        gw1[...] = jnp.zeros_like(gw1)
        gw2[...] = jnp.zeros_like(gw2)
        table = halves(jnp.concatenate([gp_ref[...] for gp_ref in gp_refs], axis=0))
        from_coarse = pick_rows(spread_column(goal_ref[...]), table)
        updated_grad = node_cot_ref[...].astype(F32) + from_coarse
        joined = jnp.concatenate([nodes_ref[...], summed_ref[...]], axis=1)
        pre = nn(joined, v1_ref[...])
        sig = sigmoid(pre)
        hidden = (pre * sig).astype(BF)
        normed, inv_std = norm_parts(nn(hidden, v2_ref[...]))
        grad_norm = norm_back(normed, inv_std, updated_grad).astype(BF)
        gv2[...] = tn(hidden, grad_norm)
        grad_pre = (nt(grad_norm, v2_ref[...]) * slope(pre, sig)).astype(BF)
        gv1[...] = tn(joined, grad_pre)
        grad_in = nt(grad_pre, v1_ref[...])
        local_ref[...] = updated_grad + grad_in[:, :LANES]
        wide[...] = halves(grad_in[:, LANES:].astype(BF))

    target = spread_column(target_ref[...])
    hiddens, grad_norms, grad_pres = [], [], []
    for part in range(0, target.shape[0], BACK_SUB):
        here = slice(part, part + BACK_SUB)
        message_grad = cot_ref[here, :].astype(F32) + pick_rows(target[here], wide[...])
        pre = pre_ref[here, :]
        sig = sigmoid(pre)
        hidden = (pre * sig).astype(BF)
        normed, inv_std = norm_parts(nn(hidden, w2_ref[...]))
        grad_norm = norm_back(normed, inv_std, message_grad).astype(BF)
        grad_pre = (nt(grad_norm, w2_ref[...]) * slope(pre, sig)).astype(BF)
        hiddens.append(hidden)
        grad_norms.append(grad_norm)
        grad_pres.append(grad_pre)
    grad_pre = jnp.concatenate(grad_pres, axis=0)
    grad_pre_ref[...] = grad_pre
    gw2[...] += tn(jnp.concatenate(hiddens, axis=0), jnp.concatenate(grad_norms, axis=0))
    stacked = jnp.concatenate([src_ref[...], tgt_ref[0], edges_ref[...]], axis=1)
    gw1[...] += tn(stacked, grad_pre)
    source = source_ref[...] - rows
    by_ghost[...] += sum_rows(source, spread_column(source), grad_pre, by_ghost.shape[0])

    @pl.when(step == pl.num_programs(0) - 1)
    def _():
        place = 0
        for part in (gw1, gw2, gv1, gv2, c1_ref, c2_ref):
            size = part.shape[0]
            pack_ref[place : place + size, :] = part[...].astype(BF)
            place += size
        pack_ref[place:, :] = jnp.zeros((pack_ref.shape[0] - place, LANES), BF)
        ghost = times_transposed(unfold(by_ghost[...]), w1_ref[:LANES, :]).astype(BF)
        domains, both, _ = joint_ref.shape
        share = pack_ref.shape[0] // domains
        joint_ref[:, :share, :] = pack_ref[...].reshape(domains, share, LANES)
        joint_ref[:, share:, :] = ghost.reshape(domains, both - share, LANES)


def own_back_kernel(
    source_ref, target_ref, grad_pre_ref, cot_ref, local_ref, w1_ref,
    out_ref, edges_ref, by_source, by_target,
):
    step = pl.program_id(0)
    half = by_source.shape[0]

    @pl.when(step == 0)
    def _():
        by_source[...] = jnp.zeros_like(by_source)
        by_target[...] = jnp.zeros_like(by_target)

    grad_pre = grad_pre_ref[...]
    source, target = source_ref[...], target_ref[...]
    by_source[...] += sum_rows(source, spread_column(source), grad_pre, half)
    by_target[...] += sum_rows(target, spread_column(target), grad_pre, half)
    edges_ref[...] = cot_ref[...].astype(F32) + nt(grad_pre, w1_ref[2 * LANES :, :])

    @pl.when(step == pl.num_programs(0) - 1)
    def _():
        out_ref[...] = (
            local_ref[...]
            + times_transposed(unfold(by_source[...]), w1_ref[:LANES, :])
            + times_transposed(unfold(by_target[...]), w1_ref[LANES : 2 * LANES, :])
        )


def add_back_kernel(boundary_ref, wanted_ref, got_ref, local_ref, out_ref):
    rows = local_ref.shape[0]
    border = boundary_ref.shape[1]
    wanted = jnp.transpose(wanted_ref[...].astype(F32))[0:1, :].astype(I32)
    slots = wanted.shape[1] // got_ref.shape[0]
    got = got_ref[:, got_ref.shape[1] - slots :, :].reshape(wanted.shape[1], LANES)
    border_grad = nn(hit_rows(wanted, border), got)
    out_ref[...] = local_ref[...] + fold_wide(
        nn(hit_rows(boundary_ref[...], rows), split_wide(border_grad))
    )


def add_parts_kernel(got_ref, out_ref):
    size = out_ref.shape[0]
    total = got_ref[0, :size, :].astype(F32)
    for k in range(1, got_ref.shape[0]):
        total = total + got_ref[k, :size, :].astype(F32)
    out_ref[...] = total


def add_groups_kernel(*refs):
    part_refs, out_ref = refs[:-1], refs[-1]
    total = part_refs[0][...]
    for part_ref in part_refs[1:]:
        total = total + part_ref[...]
    total = total.astype(BF)
    for k in range(out_ref.shape[0]):
        out_ref[k] = total


def scale_kernel(pack_ref, *out_refs, scales):
    place = 0
    for out_ref, scale in zip(out_refs, scales):
        size = out_ref.shape[0]
        out_ref[...] = pack_ref[place : place + size, :].astype(F32) * scale
        place += size


def whole(shape):
    zeros = (0,) * len(shape)
    return pl.BlockSpec(shape, lambda *_: zeros)


def call(kernel, out_shapes, *args, flops=0, bytes_accessed=0, in_specs=None, out_specs=None,
         grid=None, scratch=(), name=None, vmem=40):
    single = not isinstance(out_shapes, (list, tuple))
    extra = {}
    if grid is not None:
        extra["grid"] = grid
    if in_specs is not None:
        extra["in_specs"] = in_specs
    if out_specs is not None:
        extra["out_specs"] = out_specs
    return pl.pallas_call(
        kernel,
        out_shape=out_shapes if single else list(out_shapes),
        scratch_shapes=list(scratch),
        compiler_params=pltpu.CompilerParams(vmem_limit_bytes=vmem * 2**20),
        cost_estimate=pl.CostEstimate(
            flops=flops, bytes_accessed=bytes_accessed, transcendentals=0
        ),
        name=name,
        **extra,
    )(*args)


def local(
    node_features, edge_features, coarse_features,
    edge_w_one, edge_w_two, node_w_one, node_w_two, coarse_w_one, coarse_w_two,
    edge_source, edge_target, boundary, ghost_pos, restr_order, restr_count, coarse_slot,
    node_cotangent, edge_cotangent, coarse_cotangent,
):
    rows, latent = node_features.shape
    edges = edge_features.shape[0]
    coarse = coarse_features.shape[0]
    groups = lax.axis_size("group")
    domains = lax.axis_size("dom")
    parts = groups * domains
    slots = ghost_pos.shape[2]
    ghosts = domains * slots
    shape = jax.ShapeDtypeStruct

    def edge_blocks(block):
        return (
            (edges // block,),
            pl.BlockSpec((1, block), lambda i: (0, i)),
            pl.BlockSpec((block, latent), lambda i: (i, 0)),
        )

    exchange = functools.partial(lax.all_to_all, split_axis=0, concat_axis=0, tiled=True)

    def turned(step):
        return [(k, (k - step) % groups) for k in range(groups)]

    source = edge_source.reshape(1, edges)
    target = edge_target.reshape(1, edges)
    spread = call(
        spread_kernel, shape((ghosts, latent), BF), ghost_pos,
        flops=10**6, bytes_accessed=10**5, name="spread", vmem=8,
    )
    asked = exchange(spread.reshape(domains, slots, latent), "dom").reshape(ghosts, latent)
    slot_list = coarse_slot.reshape(groups, -1)
    here = lax.axis_index("group").astype(I32).reshape(1, 1)

    grid_block = 2048
    grid, index_spec, edge_spec = edge_blocks(grid_block)
    own_rows = call(
        edge_first_kernel, shape((2, edges, latent), BF), source, target, node_features,
        grid=grid,
        in_specs=[index_spec, index_spec, whole((rows, latent))],
        out_specs=pl.BlockSpec((2, grid_block, latent), lambda i: (0, i, 0)),
        flops=4 * 10**9, bytes_accessed=3 * 10**6, name="edge_first", vmem=61,
    )
    asked, own_rows = lax.optimization_barrier((asked, own_rows))
    share = call(
        share_kernel, shape((ghosts, latent), BF), boundary, asked, node_features,
        flops=10**9, bytes_accessed=10**6, name="share", vmem=16,
    )
    share, slot_list = lax.optimization_barrier((share, slot_list))
    slot_lists = [slot_list] + [
        lax.ppermute(slot_list, "group", turned(ahead)) for ahead in range(1, groups)
    ]
    ghost_rows = exchange(share.reshape(domains, slots, latent), "dom").reshape(ghosts, latent)
    grid, index_spec, edge_spec = edge_blocks(4096)
    pre, src_rows, summed, updated = call(
        edge_second_kernel,
        [shape((edges, latent), F32), shape((edges, latent), BF), shape((rows, latent), BF),
         shape((rows, latent), BF)],
        source, target, own_rows, edge_features, ghost_rows, edge_w_one, edge_w_two,
        node_features, node_w_one, node_w_two,
        grid=grid,
        in_specs=[index_spec, index_spec, whole((2, edges, latent)), edge_spec,
                  whole((ghosts, latent)), whole((3 * latent, latent)), whole((latent, latent)),
                  whole((rows, latent)), whole((2 * latent, latent)), whole((latent, latent))],
        out_specs=[edge_spec, edge_spec, whole((rows, latent)), whole((rows, latent))],
        scratch=[pltpu.VMEM((rows // 2, 2 * latent), F32)],
        flops=5 * 10**9, bytes_accessed=8 * 10**6, name="edge_second",
    )
    goal, *send = call(
        pool_kernel, [shape((1, rows), I32)] + [shape((2 * coarse, latent), BF)] * groups,
        here, restr_count, restr_order, updated, node_cotangent, *slot_lists,
        in_specs=[pl.BlockSpec(memory_space=pltpu.SMEM)] * 2
        + [pl.BlockSpec(memory_space=pltpu.VMEM)] * (3 + groups),
        flops=10**9, bytes_accessed=10**6, name="pool", vmem=16,
    )
    got = [send[0]] + [
        lax.ppermute(send[ahead], "group", turned(-ahead)) for ahead in range(1, groups)
    ]
    grad_coarse, coarse_back, grad_c_one, grad_c_two = call(
        coarse_kernel,
        [shape((coarse, latent), F32), shape((coarse, latent), BF),
         shape((2 * latent, latent), F32), shape((latent, latent), F32)],
        coarse_features, coarse_cotangent, coarse_w_one, coarse_w_two, *got,
        flops=10**8, bytes_accessed=10**6, name="coarse", vmem=16,
    )
    returned = [coarse_back] + [
        lax.ppermute(coarse_back, "group", turned(ahead)) for ahead in range(1, groups)
    ]
    share_rows = 48
    pack_rows = domains * share_rows
    grid, index_spec, edge_spec = edge_blocks(4096)
    joint_shape = (domains, share_rows + slots, latent)
    grad_pre, node_local, joint = call(
        edge_back_kernel,
        [shape((edges, latent), BF), shape((rows, latent), F32), shape(joint_shape, BF)],
        source, target, pre, src_rows, own_rows, edge_features, edge_cotangent, edge_w_one, edge_w_two,
        goal, node_cotangent, node_features, summed, node_w_one, node_w_two,
        grad_c_one, grad_c_two, *returned,
        grid=grid,
        in_specs=[index_spec, index_spec, edge_spec, edge_spec,
                  pl.BlockSpec((1, edges, latent), lambda i: (1, 0, 0)), edge_spec, edge_spec,
                  whole((3 * latent, latent)), whole((latent, latent)),
                  whole((1, rows)),
                  whole((rows, latent)), whole((rows, latent)), whole((rows, latent)),
                  whole((2 * latent, latent)), whole((latent, latent)),
                  whole((2 * latent, latent)), whole((latent, latent))]
        + [whole((coarse, latent))] * groups,
        out_specs=[edge_spec, whole((rows, latent)), whole(joint_shape)],
        scratch=[pltpu.VMEM((rows // 2, 2 * latent), BF), pltpu.VMEM((3 * latent, latent), F32),
                 pltpu.VMEM((latent, latent), F32), pltpu.VMEM((2 * latent, latent), F32),
                 pltpu.VMEM((latent, latent), F32), pltpu.VMEM((ghosts // 2, 2 * latent), F32),
                 pltpu.VMEM((pack_rows, latent), BF)],
        flops=6 * 10**9, bytes_accessed=10**7, name="edge_back",
    )
    grid, index_spec, edge_spec = edge_blocks(4096)
    own_local, grad_edges = call(
        own_back_kernel,
        [shape((rows, latent), F32), shape((edges, latent), F32)],
        source, target, grad_pre, edge_cotangent, node_local, edge_w_one,
        grid=grid,
        in_specs=[index_spec, index_spec, edge_spec, edge_spec, whole((rows, latent)),
                  whole((3 * latent, latent))],
        out_specs=[whole((rows, latent)), edge_spec],
        scratch=[pltpu.VMEM((rows // 2, 2 * latent), F32)] * 2,
        flops=4 * 10**9, bytes_accessed=5 * 10**6, name="own_back",
    )
    joint_got, own_local = lax.optimization_barrier((exchange(joint, "dom"), own_local))
    part_sum = call(
        add_parts_kernel, shape((share_rows, latent), F32), joint_got,
        flops=10**6, bytes_accessed=10**6, name="add_parts", vmem=16,
    )
    part_sums = [part_sum] + [
        lax.ppermute(part_sum, "group", turned(ahead)) for ahead in range(1, groups)
    ]
    pack_sum = call(
        add_groups_kernel, shape((domains, share_rows, latent), BF), *part_sums,
        flops=10**6, bytes_accessed=10**6, name="add_groups", vmem=16,
    )
    pack_all = exchange(pack_sum, "dom").reshape(pack_rows, latent)
    grad_nodes = call(
        add_back_kernel, shape((rows, latent), F32), boundary, asked, joint_got, own_local,
        flops=10**9, bytes_accessed=10**6, name="add_back", vmem=16,
    )
    edge_scale = (edges * parts) ** (-0.5)
    node_scale = (rows * parts) ** (-0.5)
    coarse_scale = (coarse * parts) ** (-0.5)
    weight_grads = call(
        functools.partial(
            scale_kernel,
            scales=(edge_scale, edge_scale, node_scale, node_scale, coarse_scale, coarse_scale),
        ),
        [shape((size * latent, latent), F32) for size in (3, 1, 2, 1, 2, 1)],
        pack_all,
        flops=10**6, bytes_accessed=10**6, name="scale", vmem=16,
    )
    return (grad_nodes, grad_edges, grad_coarse, *weight_grads)


def solution(mesh):
    rows = P(("group", "dom"), None)
    cube = P(("group", "dom"), None, None)
    line = P(("group", "dom"))
    placed = (
        rows, rows, rows, P(), P(), P(), P(), P(), P(), line, line, rows, cube, rows, rows, cube,
        rows, rows, rows,
    )
    return jax.shard_map(
        local,
        mesh=mesh,
        in_specs=placed,
        out_specs=(rows, rows, rows, P(), P(), P(), P(), P(), P()),
        check_vma=False,
    )
```

```python
import functools

import jax
import jax.numpy as jnp
from jax import lax
from jax.experimental import pallas as pl
from jax.experimental.pallas import tpu as pltpu
from jax.sharding import PartitionSpec as P

NORM_EPSILON = 1e-05
POOL_SHARE = 0.25
BF = jnp.bfloat16
F32 = jnp.float32
I32 = jnp.int32
LANES = 128
SECOND_SUB = 512
BACK_SUB = 2048


def nn(a, b):
    return lax.dot_general(a, b, (((1,), (0,)), ((), ())), preferred_element_type=F32)


def nt(a, b):
    return lax.dot_general(a, b, (((1,), (1,)), ((), ())), preferred_element_type=F32)


def tn(a, b):
    return lax.dot_general(a, b, (((0,), (0,)), ((), ())), preferred_element_type=F32)


def as_hit(mask):
    return jnp.where(mask, 1.0, 0.0).astype(BF)


def hit_rows(index_row, count, base=0):
    width = index_row.shape[1]
    return as_hit(lax.broadcasted_iota(I32, (count, width), 0) == index_row - base)


def spread_column(index_row):
    width = index_row.shape[1]
    return jnp.transpose(jnp.broadcast_to(index_row, (LANES, width)))


def hit_columns(index_column, count, base=0):
    lane = lax.broadcasted_iota(I32, index_column.shape, 1)
    return jnp.concatenate(
        [as_hit(lane == index_column - (base + LANES * j)) for j in range(count // LANES)], axis=1
    )


def halves(table):
    half = table.shape[0] // 2
    return jnp.concatenate([table[:half], table[half:]], axis=1)


def pick_rows(index_column, table_halves):
    half = table_halves.shape[0]
    upper = index_column >= half
    wide = nn(hit_columns(jnp.where(upper, index_column - half, index_column), half), table_halves)
    return jnp.where(upper, wide[:, LANES:], wide[:, :LANES])


def sum_rows(index_row, index_column, values, half):
    upper = index_column >= half
    nothing = jnp.zeros_like(values)
    both = jnp.concatenate(
        [jnp.where(upper, nothing, values), jnp.where(upper, values, nothing)], axis=1
    )
    return nn(hit_rows(jnp.where(index_row >= half, index_row - half, index_row), half), both)


def unfold(sums):
    return jnp.concatenate([sums[:, :LANES], sums[:, LANES:]], axis=0)


def split_wide(values):
    high = values.astype(BF)
    low = (values - high.astype(F32)).astype(BF)
    return jnp.concatenate([high, low], axis=1)


def fold_wide(values):
    return values[:, :LANES] + values[:, LANES:]


def times_transposed(values, weights):
    return nt(split_wide(values), jnp.concatenate([weights, weights], axis=1))


def mean_lanes(values):
    return jnp.mean(values, axis=-1, keepdims=True)


def norm_parts(values):
    centred = values - mean_lanes(values)
    inv_std = lax.rsqrt(mean_lanes(centred * centred) + NORM_EPSILON)
    return centred * inv_std, inv_std


def norm_back(normed, inv_std, grad_in):
    return inv_std * (grad_in - mean_lanes(grad_in) - normed * mean_lanes(grad_in * normed))


def sigmoid(values):
    return 1.0 / (1.0 + jnp.exp(-values))


def slope(values, sig):
    return sig * (1.0 + values * (1.0 - sig))


def spread_kernel(wanted_ref, out_ref):
    _, domains, slots = wanted_ref.shape
    ghosts = out_ref.shape[0]
    first = lax.broadcasted_iota(I32, (ghosts, domains), 0) // slots
    pick = as_hit(first == lax.broadcasted_iota(I32, (ghosts, domains), 1))
    by_owner = nn(pick, wanted_ref[0].astype(F32).astype(BF))
    slot = lax.broadcasted_iota(I32, (ghosts, slots), 0) % slots
    own = jnp.where(slot == lax.broadcasted_iota(I32, (ghosts, slots), 1), by_owner, 0.0).astype(BF)
    out_ref[...] = nn(own, jnp.ones((slots, LANES), BF)).astype(BF)


def share_kernel(boundary_ref, wanted_ref, nodes_ref, out_ref):
    border = boundary_ref.shape[1]
    shared = pick_rows(spread_column(boundary_ref[...]), halves(nodes_ref[...])).astype(BF)
    wanted = wanted_ref[...].astype(F32).astype(I32)
    out_ref[...] = nn(hit_columns(wanted, border), shared).astype(BF)


def pool_kernel(group_ref, count_ref, order_ref, updated_ref, node_cot_ref, *refs):
    groups = (len(refs) - 1) // 2
    slot_refs, out_ref, send_refs = refs[:groups], refs[groups], refs[groups + 1 :]
    coarse = send_refs[0].shape[0] // 2
    capacity = slot_refs[0].shape[1]
    rows = order_ref.shape[1]
    here = group_ref[0, 0]
    place = lax.broadcasted_iota(I32, (8, rows), 1)
    owner = jnp.zeros((8, rows), I32)
    goal = jnp.zeros((8, rows), I32)
    for ahead, slot_ref in enumerate(slot_refs):
        k = lax.rem(here + ahead, groups)
        start = 0
        for other in range(groups - 1):
            start = start + jnp.where(other < k, count_ref[0, other], 0)
        line = jnp.concatenate(
            [slot_ref[pl.ds(here, 1), :], jnp.zeros((1, rows - capacity), I32)], axis=1
        )
        line = pltpu.roll(jnp.broadcast_to(line, (8, rows)), start, 1)
        inside = (place >= start) & (place < start + count_ref[0, k])
        owner = jnp.where(inside, ahead, owner)
        goal = jnp.where(inside, line, goal)
    digits = jnp.where(lax.broadcasted_iota(I32, (8, rows), 0) == 0, owner, goal)
    by_row = nt(digits.astype(F32).astype(BF), hit_rows(order_ref[...], rows))
    goal = (by_row[0:1, :] * coarse + by_row[1:2, :]).astype(I32)
    out_ref[...] = goal
    both = jnp.concatenate([updated_ref[...], node_cot_ref[...]], axis=1)
    pooled = nn(hit_rows(goal, groups * coarse), both).astype(BF)
    for k, send_ref in enumerate(send_refs):
        send_ref[:coarse, :] = pooled[k * coarse : (k + 1) * coarse, :LANES]
        send_ref[coarse:, :] = pooled[k * coarse : (k + 1) * coarse, LANES:]


def edge_first_kernel(source_ref, target_ref, nodes_ref, out_ref):
    nodes = halves(nodes_ref[...])
    out_ref[0] = pick_rows(spread_column(source_ref[...]), nodes).astype(BF)
    out_ref[1] = pick_rows(spread_column(target_ref[...]), nodes).astype(BF)


def edge_second_kernel(
    source_ref, target_ref, own_ref, edges_ref, ghosts_ref, w1_ref, w2_ref,
    nodes_ref, v1_ref, v2_ref,
    pre_ref, src_ref, summed_ref, updated_ref, total,
):
    step = pl.program_id(0)
    rows = nodes_ref.shape[0]

    @pl.when(step == 0)
    def _():
        total[...] = jnp.zeros_like(total)

    ghosts = halves(ghosts_ref[...])
    from_ghost = spread_column(source_ref[...]) - rows
    target = target_ref[...]
    messages = []
    for part in range(0, target.shape[1], SECOND_SUB):
        here = slice(part, part + SECOND_SUB)
        src = own_ref[0, here, :] + pick_rows(from_ghost[here], ghosts).astype(BF)
        src_ref[here, :] = src
        stacked = jnp.concatenate([src, own_ref[1, here, :], edges_ref[here, :]], axis=1)
        pre = nn(stacked, w1_ref[...])
        pre_ref[here, :] = pre
        hidden = (pre * sigmoid(pre)).astype(BF)
        message, _ = norm_parts(nn(hidden, w2_ref[...]))
        messages.append(message.astype(BF))
    total[...] += sum_rows(
        target, spread_column(target), jnp.concatenate(messages, axis=0), rows // 2
    )

    @pl.when(step == pl.num_programs(0) - 1)
    def _():
        summed = unfold(total[...]).astype(BF)
        summed_ref[...] = summed
        nodes = nodes_ref[...]
        pre_node = nn(jnp.concatenate([nodes, summed], axis=1), v1_ref[...])
        hidden_node = (pre_node * sigmoid(pre_node)).astype(BF)
        normed, _ = norm_parts(nn(hidden_node, v2_ref[...]))
        updated_ref[...] = (nodes.astype(F32) + normed).astype(BF)


def coarse_kernel(feat_ref, cot_ref, w1_ref, w2_ref, *refs):
    got_refs, (grad_ref, back_ref, g1_ref, g2_ref) = refs[:-4], refs[-4:]
    coarse = feat_ref.shape[0]
    got = got_refs[0][...].astype(F32)
    for got_ref in got_refs[1:]:
        got = got + got_ref[...].astype(F32)
    pooled = (got[:coarse] * POOL_SHARE).astype(BF)
    cot = cot_ref[...].astype(F32)
    grad_out = (cot + got[coarse:]).astype(BF)
    joined = jnp.concatenate([feat_ref[...], pooled], axis=1)
    pre = nn(joined, w1_ref[...])
    sig = sigmoid(pre)
    hidden = (pre * sig).astype(BF)
    g2_ref[...] = tn(hidden, grad_out)
    grad_pre = (nt(grad_out, w2_ref[...]) * slope(pre, sig)).astype(BF)
    g1_ref[...] = tn(joined, grad_pre)
    grad_in = nt(grad_pre, w1_ref[...])
    grad_ref[...] = cot + grad_in[:, :LANES]
    back_ref[...] = (grad_in[:, LANES:] * POOL_SHARE).astype(BF)


def slopes_kernel(
    pre_ref, w2_ref, nodes_ref, summed_ref, v1_ref, v2_ref,
    slope_ref, hidden_ref, normed_ref, std_ref,
    node_slope_ref, node_hidden_ref, node_normed_ref, node_std_ref,
):
    def fill(pre, weights, out_refs, here):
        sig = sigmoid(pre)
        hidden = (pre * sig).astype(BF)
        normed, inv_std = norm_parts(nn(hidden, weights))
        parts = (slope(pre, sig), hidden, normed, jnp.broadcast_to(inv_std, normed.shape))
        for out_ref, part in zip(out_refs, parts):
            out_ref[here, :] = part

    for part in range(0, pre_ref.shape[0], SECOND_SUB):
        here = slice(part, part + SECOND_SUB)
        fill(pre_ref[here, :], w2_ref[...], (slope_ref, hidden_ref, normed_ref, std_ref), here)
    joined = jnp.concatenate([nodes_ref[...], summed_ref[...]], axis=1)
    fill(
        nn(joined, v1_ref[...]), v2_ref[...],
        (node_slope_ref, node_hidden_ref, node_normed_ref, node_std_ref),
        slice(0, nodes_ref.shape[0]),
    )


def edge_back_kernel(
    node_slope_ref, node_hidden_ref, node_normed_ref, node_std_ref,
    source_ref, target_ref, slope_ref, hidden_ref, normed_ref, std_ref, src_ref, tgt_ref, edges_ref, cot_ref, w1_ref, w2_ref,
    goal_ref, node_cot_ref, nodes_ref, summed_ref, v1_ref, v2_ref, c1_ref, c2_ref, *rest,
):
    gp_refs = rest[:-10]
    grad_pre_ref, local_ref, joint_ref, wide, gw1, gw2, gv1, gv2, by_ghost, pack_ref = rest[-10:]
    step = pl.program_id(0)
    rows = nodes_ref.shape[0]

    @pl.when(step == 0)
    def _():
        by_ghost[...] = jnp.zeros_like(by_ghost)
        gw1[...] = jnp.zeros_like(gw1)
        gw2[...] = jnp.zeros_like(gw2)
        table = halves(jnp.concatenate([gp_ref[...] for gp_ref in gp_refs], axis=0))
        from_coarse = pick_rows(spread_column(goal_ref[...]), table)
        updated_grad = node_cot_ref[...].astype(F32) + from_coarse
        joined = jnp.concatenate([nodes_ref[...], summed_ref[...]], axis=1)
        grad_norm = norm_back(node_normed_ref[...], node_std_ref[...], updated_grad).astype(BF)
        gv2[...] = tn(node_hidden_ref[...], grad_norm)
        grad_pre = (nt(grad_norm, v2_ref[...]) * node_slope_ref[...]).astype(BF)
        gv1[...] = tn(joined, grad_pre)
        grad_in = nt(grad_pre, v1_ref[...])
        local_ref[...] = updated_grad + grad_in[:, :LANES]
        wide[...] = halves(grad_in[:, LANES:].astype(BF))

    target = spread_column(target_ref[...])
    grad_norms, grad_pres = [], []
    for part in range(0, target.shape[0], BACK_SUB):
        here = slice(part, part + BACK_SUB)
        message_grad = cot_ref[here, :].astype(F32) + pick_rows(target[here], wide[...])
        grad_norm = norm_back(normed_ref[here, :], std_ref[here, :], message_grad).astype(BF)
        grad_pre = (nt(grad_norm, w2_ref[...]) * slope_ref[here, :]).astype(BF)
        grad_norms.append(grad_norm)
        grad_pres.append(grad_pre)
    grad_pre = jnp.concatenate(grad_pres, axis=0)
    grad_pre_ref[...] = grad_pre
    gw2[...] += tn(hidden_ref[...], jnp.concatenate(grad_norms, axis=0))
    stacked = jnp.concatenate([src_ref[...], tgt_ref[0], edges_ref[...]], axis=1)
    gw1[...] += tn(stacked, grad_pre)
    source = source_ref[...] - rows
    by_ghost[...] += sum_rows(source, spread_column(source), grad_pre, by_ghost.shape[0])

    @pl.when(step == pl.num_programs(0) - 1)
    def _():
        place = 0
        for part in (gw1, gw2, gv1, gv2, c1_ref, c2_ref):
            size = part.shape[0]
            pack_ref[place : place + size, :] = part[...].astype(BF)
            place += size
        pack_ref[place:, :] = jnp.zeros((pack_ref.shape[0] - place, LANES), BF)
        ghost = times_transposed(unfold(by_ghost[...]), w1_ref[:LANES, :]).astype(BF)
        domains, both, _ = joint_ref.shape
        share = pack_ref.shape[0] // domains
        joint_ref[:, :share, :] = pack_ref[...].reshape(domains, share, LANES)
        joint_ref[:, share:, :] = ghost.reshape(domains, both - share, LANES)


def own_back_kernel(
    source_ref, target_ref, grad_pre_ref, cot_ref, local_ref, w1_ref,
    out_ref, edges_ref, by_source, by_target,
):
    step = pl.program_id(0)
    half = by_source.shape[0]

    @pl.when(step == 0)
    def _():
        by_source[...] = jnp.zeros_like(by_source)
        by_target[...] = jnp.zeros_like(by_target)

    grad_pre = grad_pre_ref[...]
    source, target = source_ref[...], target_ref[...]
    by_source[...] += sum_rows(source, spread_column(source), grad_pre, half)
    by_target[...] += sum_rows(target, spread_column(target), grad_pre, half)
    edges_ref[...] = cot_ref[...].astype(F32) + nt(grad_pre, w1_ref[2 * LANES :, :])

    @pl.when(step == pl.num_programs(0) - 1)
    def _():
        out_ref[...] = (
            local_ref[...]
            + times_transposed(unfold(by_source[...]), w1_ref[:LANES, :])
            + times_transposed(unfold(by_target[...]), w1_ref[LANES : 2 * LANES, :])
        )


def add_back_kernel(boundary_ref, wanted_ref, got_ref, local_ref, out_ref):
    rows = local_ref.shape[0]
    border = boundary_ref.shape[1]
    wanted = jnp.transpose(wanted_ref[...].astype(F32))[0:1, :].astype(I32)
    slots = wanted.shape[1] // got_ref.shape[0]
    got = got_ref[:, got_ref.shape[1] - slots :, :].reshape(wanted.shape[1], LANES)
    border_grad = nn(hit_rows(wanted, border), got)
    out_ref[...] = local_ref[...] + fold_wide(
        nn(hit_rows(boundary_ref[...], rows), split_wide(border_grad))
    )


def add_parts_kernel(got_ref, out_ref):
    size = out_ref.shape[0]
    total = got_ref[0, :size, :].astype(F32)
    for k in range(1, got_ref.shape[0]):
        total = total + got_ref[k, :size, :].astype(F32)
    out_ref[...] = total


def add_groups_kernel(*refs):
    part_refs, out_ref = refs[:-1], refs[-1]
    total = part_refs[0][...]
    for part_ref in part_refs[1:]:
        total = total + part_ref[...]
    total = total.astype(BF)
    for k in range(out_ref.shape[0]):
        out_ref[k] = total


def scale_kernel(pack_ref, *out_refs, scales):
    place = 0
    for out_ref, scale in zip(out_refs, scales):
        size = out_ref.shape[0]
        out_ref[...] = pack_ref[place : place + size, :].astype(F32) * scale
        place += size


def whole(shape):
    zeros = (0,) * len(shape)
    return pl.BlockSpec(shape, lambda *_: zeros)


def call(kernel, out_shapes, *args, flops=0, bytes_accessed=0, in_specs=None, out_specs=None,
         grid=None, scratch=(), name=None, vmem=40):
    single = not isinstance(out_shapes, (list, tuple))
    extra = {}
    if grid is not None:
        extra["grid"] = grid
    if in_specs is not None:
        extra["in_specs"] = in_specs
    if out_specs is not None:
        extra["out_specs"] = out_specs
    return pl.pallas_call(
        kernel,
        out_shape=out_shapes if single else list(out_shapes),
        scratch_shapes=list(scratch),
        compiler_params=pltpu.CompilerParams(vmem_limit_bytes=vmem * 2**20),
        cost_estimate=pl.CostEstimate(
            flops=flops, bytes_accessed=bytes_accessed, transcendentals=0
        ),
        name=name,
        **extra,
    )(*args)


def local(
    node_features, edge_features, coarse_features,
    edge_w_one, edge_w_two, node_w_one, node_w_two, coarse_w_one, coarse_w_two,
    edge_source, edge_target, boundary, ghost_pos, restr_order, restr_count, coarse_slot,
    node_cotangent, edge_cotangent, coarse_cotangent,
):
    rows, latent = node_features.shape
    edges = edge_features.shape[0]
    coarse = coarse_features.shape[0]
    groups = lax.axis_size("group")
    domains = lax.axis_size("dom")
    parts = groups * domains
    slots = ghost_pos.shape[2]
    ghosts = domains * slots
    shape = jax.ShapeDtypeStruct

    def edge_blocks(block):
        return (
            (edges // block,),
            pl.BlockSpec((1, block), lambda i: (0, i)),
            pl.BlockSpec((block, latent), lambda i: (i, 0)),
        )

    exchange = functools.partial(lax.all_to_all, split_axis=0, concat_axis=0, tiled=True)

    def turned(step):
        return [(k, (k - step) % groups) for k in range(groups)]

    source = edge_source.reshape(1, edges)
    target = edge_target.reshape(1, edges)
    spread = call(
        spread_kernel, shape((ghosts, latent), BF), ghost_pos,
        flops=10**6, bytes_accessed=10**5, name="spread", vmem=8,
    )
    asked = exchange(spread.reshape(domains, slots, latent), "dom").reshape(ghosts, latent)
    slot_list = coarse_slot.reshape(groups, -1)
    here = lax.axis_index("group").astype(I32).reshape(1, 1)

    grid_block = 2048
    grid, index_spec, edge_spec = edge_blocks(grid_block)
    own_rows = call(
        edge_first_kernel, shape((2, edges, latent), BF), source, target, node_features,
        grid=grid,
        in_specs=[index_spec, index_spec, whole((rows, latent))],
        out_specs=pl.BlockSpec((2, grid_block, latent), lambda i: (0, i, 0)),
        flops=4 * 10**9, bytes_accessed=3 * 10**6, name="edge_first", vmem=61,
    )
    asked, own_rows = lax.optimization_barrier((asked, own_rows))
    share = call(
        share_kernel, shape((ghosts, latent), BF), boundary, asked, node_features,
        flops=10**9, bytes_accessed=10**6, name="share", vmem=16,
    )
    share, slot_list = lax.optimization_barrier((share, slot_list))
    slot_lists = [slot_list] + [
        lax.ppermute(slot_list, "group", turned(ahead)) for ahead in range(1, groups)
    ]
    ghost_rows = exchange(share.reshape(domains, slots, latent), "dom").reshape(ghosts, latent)
    grid, index_spec, edge_spec = edge_blocks(4096)
    pre, src_rows, summed, updated = call(
        edge_second_kernel,
        [shape((edges, latent), F32), shape((edges, latent), BF), shape((rows, latent), BF),
         shape((rows, latent), BF)],
        source, target, own_rows, edge_features, ghost_rows, edge_w_one, edge_w_two,
        node_features, node_w_one, node_w_two,
        grid=grid,
        in_specs=[index_spec, index_spec, whole((2, edges, latent)), edge_spec,
                  whole((ghosts, latent)), whole((3 * latent, latent)), whole((latent, latent)),
                  whole((rows, latent)), whole((2 * latent, latent)), whole((latent, latent))],
        out_specs=[edge_spec, edge_spec, whole((rows, latent)), whole((rows, latent))],
        scratch=[pltpu.VMEM((rows // 2, 2 * latent), F32)],
        flops=5 * 10**9, bytes_accessed=8 * 10**6, name="edge_second",
    )
    goal, *send = call(
        pool_kernel, [shape((1, rows), I32)] + [shape((2 * coarse, latent), BF)] * groups,
        here, restr_count, restr_order, updated, node_cotangent, *slot_lists,
        in_specs=[pl.BlockSpec(memory_space=pltpu.SMEM)] * 2
        + [pl.BlockSpec(memory_space=pltpu.VMEM)] * (3 + groups),
        flops=10**9, bytes_accessed=10**6, name="pool", vmem=16,
    )
    slopes = call(
        slopes_kernel,
        [shape((size, latent), kind) for size in (edges, rows) for kind in (F32, BF, F32, F32)],
        pre, edge_w_two, node_features, summed, node_w_one, node_w_two,
        flops=10**9, bytes_accessed=10**7, name="slopes",
    )
    got = [send[0]] + [
        lax.ppermute(send[ahead], "group", turned(-ahead)) for ahead in range(1, groups)
    ]
    got, slopes = lax.optimization_barrier((got, slopes))
    grad_coarse, coarse_back, grad_c_one, grad_c_two = call(
        coarse_kernel,
        [shape((coarse, latent), F32), shape((coarse, latent), BF),
         shape((2 * latent, latent), F32), shape((latent, latent), F32)],
        coarse_features, coarse_cotangent, coarse_w_one, coarse_w_two, *got,
        flops=10**8, bytes_accessed=10**6, name="coarse", vmem=16,
    )
    returned = [coarse_back] + [
        lax.ppermute(coarse_back, "group", turned(ahead)) for ahead in range(1, groups)
    ]
    share_rows = 48
    pack_rows = domains * share_rows
    grid, index_spec, edge_spec = edge_blocks(4096)
    joint_shape = (domains, share_rows + slots, latent)
    grad_pre, node_local, joint = call(
        edge_back_kernel,
        [shape((edges, latent), BF), shape((rows, latent), F32), shape(joint_shape, BF)],
        *slopes[4:], source, target, *slopes[:4], src_rows, own_rows, edge_features, edge_cotangent, edge_w_one, edge_w_two,
        goal, node_cotangent, node_features, summed, node_w_one, node_w_two,
        grad_c_one, grad_c_two, *returned,
        grid=grid,
        in_specs=[whole((rows, latent))] * 4
        + [index_spec, index_spec] + [edge_spec] * 5 + [
                  pl.BlockSpec((1, edges, latent), lambda i: (1, 0, 0)), edge_spec, edge_spec,
                  whole((3 * latent, latent)), whole((latent, latent)),
                  whole((1, rows)),
                  whole((rows, latent)), whole((rows, latent)), whole((rows, latent)),
                  whole((2 * latent, latent)), whole((latent, latent)),
                  whole((2 * latent, latent)), whole((latent, latent))]
        + [whole((coarse, latent))] * groups,
        out_specs=[edge_spec, whole((rows, latent)), whole(joint_shape)],
        scratch=[pltpu.VMEM((rows // 2, 2 * latent), BF), pltpu.VMEM((3 * latent, latent), F32),
                 pltpu.VMEM((latent, latent), F32), pltpu.VMEM((2 * latent, latent), F32),
                 pltpu.VMEM((latent, latent), F32), pltpu.VMEM((ghosts // 2, 2 * latent), F32),
                 pltpu.VMEM((pack_rows, latent), BF)],
        flops=6 * 10**9, bytes_accessed=10**7, name="edge_back",
    )
    grid, index_spec, edge_spec = edge_blocks(4096)
    own_local, grad_edges = call(
        own_back_kernel,
        [shape((rows, latent), F32), shape((edges, latent), F32)],
        source, target, grad_pre, edge_cotangent, node_local, edge_w_one,
        grid=grid,
        in_specs=[index_spec, index_spec, edge_spec, edge_spec, whole((rows, latent)),
                  whole((3 * latent, latent))],
        out_specs=[whole((rows, latent)), edge_spec],
        scratch=[pltpu.VMEM((rows // 2, 2 * latent), F32)] * 2,
        flops=4 * 10**9, bytes_accessed=5 * 10**6, name="own_back",
    )
    joint_got, own_local = lax.optimization_barrier((exchange(joint, "dom"), own_local))
    part_sum = call(
        add_parts_kernel, shape((share_rows, latent), F32), joint_got,
        flops=10**6, bytes_accessed=10**6, name="add_parts", vmem=16,
    )
    part_sums = [part_sum] + [
        lax.ppermute(part_sum, "group", turned(ahead)) for ahead in range(1, groups)
    ]
    pack_sum = call(
        add_groups_kernel, shape((domains, share_rows, latent), BF), *part_sums,
        flops=10**6, bytes_accessed=10**6, name="add_groups", vmem=16,
    )
    pack_all = exchange(pack_sum, "dom").reshape(pack_rows, latent)
    grad_nodes = call(
        add_back_kernel, shape((rows, latent), F32), boundary, asked, joint_got, own_local,
        flops=10**9, bytes_accessed=10**6, name="add_back", vmem=16,
    )
    edge_scale = (edges * parts) ** (-0.5)
    node_scale = (rows * parts) ** (-0.5)
    coarse_scale = (coarse * parts) ** (-0.5)
    weight_grads = call(
        functools.partial(
            scale_kernel,
            scales=(edge_scale, edge_scale, node_scale, node_scale, coarse_scale, coarse_scale),
        ),
        [shape((size * latent, latent), F32) for size in (3, 1, 2, 1, 2, 1)],
        pack_all,
        flops=10**6, bytes_accessed=10**6, name="scale", vmem=16,
    )
    return (grad_nodes, grad_edges, grad_coarse, *weight_grads)


def solution(mesh):
    rows = P(("group", "dom"), None)
    cube = P(("group", "dom"), None, None)
    line = P(("group", "dom"))
    placed = (
        rows, rows, rows, P(), P(), P(), P(), P(), P(), line, line, rows, cube, rows, rows, cube,
        rows, rows, rows,
    )
    return jax.shard_map(
        local,
        mesh=mesh,
        in_specs=placed,
        out_specs=(rows, rows, rows, P(), P(), P(), P(), P(), P()),
        check_vma=False,
    )
```

```python
import functools

import jax
import jax.numpy as jnp
from jax import lax
from jax.experimental import pallas as pl
from jax.experimental.pallas import tpu as pltpu
from jax.sharding import PartitionSpec as P

NORM_EPSILON = 1e-05
POOL_SHARE = 0.25
BF = jnp.bfloat16
F32 = jnp.float32
I32 = jnp.int32
LANES = 128
SECOND_SUB = 512
BACK_SUB = 2048


def nn(a, b):
    return lax.dot_general(a, b, (((1,), (0,)), ((), ())), preferred_element_type=F32)


def nt(a, b):
    return lax.dot_general(a, b, (((1,), (1,)), ((), ())), preferred_element_type=F32)


def tn(a, b):
    return lax.dot_general(a, b, (((0,), (0,)), ((), ())), preferred_element_type=F32)


def as_hit(mask):
    return jnp.where(mask, 1.0, 0.0).astype(BF)


def hit_rows(index_row, count, base=0):
    width = index_row.shape[1]
    return as_hit(lax.broadcasted_iota(I32, (count, width), 0) == index_row - base)


def spread_column(index_row):
    width = index_row.shape[1]
    return jnp.transpose(jnp.broadcast_to(index_row, (LANES, width)))


def hit_columns(index_column, count, base=0):
    lane = lax.broadcasted_iota(I32, index_column.shape, 1)
    return jnp.concatenate(
        [as_hit(lane == index_column - (base + LANES * j)) for j in range(count // LANES)], axis=1
    )


def halves(table):
    half = table.shape[0] // 2
    return jnp.concatenate([table[:half], table[half:]], axis=1)


def pick_rows(index_column, table_halves):
    half = table_halves.shape[0]
    upper = index_column >= half
    wide = nn(hit_columns(jnp.where(upper, index_column - half, index_column), half), table_halves)
    return jnp.where(upper, wide[:, LANES:], wide[:, :LANES])


def sum_rows(index_row, index_column, values, half):
    upper = index_column >= half
    nothing = jnp.zeros_like(values)
    both = jnp.concatenate(
        [jnp.where(upper, nothing, values), jnp.where(upper, values, nothing)], axis=1
    )
    return nn(hit_rows(jnp.where(index_row >= half, index_row - half, index_row), half), both)


def unfold(sums):
    return jnp.concatenate([sums[:, :LANES], sums[:, LANES:]], axis=0)


def split_wide(values):
    high = values.astype(BF)
    low = (values - high.astype(F32)).astype(BF)
    return jnp.concatenate([high, low], axis=1)


def fold_wide(values):
    return values[:, :LANES] + values[:, LANES:]


def times_transposed(values, weights):
    return nt(split_wide(values), jnp.concatenate([weights, weights], axis=1))


def mean_lanes(values):
    return jnp.mean(values, axis=-1, keepdims=True)


def norm_parts(values):
    centred = values - mean_lanes(values)
    inv_std = lax.rsqrt(mean_lanes(centred * centred) + NORM_EPSILON)
    return centred * inv_std, inv_std


def norm_back(normed, inv_std, grad_in):
    return inv_std * (grad_in - mean_lanes(grad_in) - normed * mean_lanes(grad_in * normed))


def sigmoid(values):
    return 1.0 / (1.0 + jnp.exp(-values))


def slope(values, sig):
    return sig * (1.0 + values * (1.0 - sig))


def spread_kernel(wanted_ref, out_ref):
    _, domains, slots = wanted_ref.shape
    ghosts = out_ref.shape[0]
    first = lax.broadcasted_iota(I32, (ghosts, domains), 0) // slots
    pick = as_hit(first == lax.broadcasted_iota(I32, (ghosts, domains), 1))
    by_owner = nn(pick, wanted_ref[0].astype(F32).astype(BF))
    slot = lax.broadcasted_iota(I32, (ghosts, slots), 0) % slots
    own = jnp.where(slot == lax.broadcasted_iota(I32, (ghosts, slots), 1), by_owner, 0.0).astype(BF)
    out_ref[...] = nn(own, jnp.ones((slots, LANES), BF)).astype(BF)


def share_kernel(boundary_ref, wanted_ref, nodes_ref, out_ref):
    border = boundary_ref.shape[1]
    shared = pick_rows(spread_column(boundary_ref[...]), halves(nodes_ref[...])).astype(BF)
    wanted = wanted_ref[...].astype(F32).astype(I32)
    out_ref[...] = nn(hit_columns(wanted, border), shared).astype(BF)


def choose(index, lines):
    found = lines[0]
    for k in range(1, len(lines)):
        found = jnp.where(index == k, lines[k], found)
    return found


def order_kernel(group_ref, count_ref, order_ref, slot_ref, node_cot_ref, *out_refs):
    groups, capacity = slot_ref.shape
    rows = order_ref.shape[1]
    here = group_ref[0, 0]
    table = halves(node_cot_ref[...])
    order = jnp.broadcast_to(order_ref[...], (8, rows))
    place = lax.broadcasted_iota(I32, (1, capacity), 1)
    slots = jnp.concatenate(
        [slot_ref[k : k + 1, at : at + LANES] for k in range(groups) for at in range(0, capacity, LANES)],
        axis=0,
    ).astype(F32).astype(BF)
    for ahead, out_ref in enumerate(out_refs):
        k = lax.rem(here + (groups - ahead), groups)
        start = 0
        for other in range(groups - 1):
            start = start + jnp.where(other < k, count_ref[0, other], 0)
        line = pltpu.roll(order, lax.rem(rows - start, rows), 1)[0:1, :capacity]
        line = jnp.where(place < count_ref[0, k], line, -1)
        out_ref[:capacity, :] = pick_rows(spread_column(line), table).astype(BF)
        out_ref[capacity:, :] = slots


def cot_pool_kernel(group_ref, slot_ref, *refs):
    got_refs, out_ref = refs[:-1], refs[-1]
    groups, capacity = slot_ref.shape
    lines = [slot_ref[k : k + 1, :] for k in range(groups)]
    total = jnp.zeros(out_ref.shape, F32)
    for ahead, got_ref in enumerate(got_refs):
        line = choose(lax.rem(group_ref[0, 0] + ahead, groups), lines)
        total = total + nn(hit_rows(line, out_ref.shape[0]), got_ref[:capacity, :])
    out_ref[...] = total


def pool_kernel(group_ref, count_ref, order_ref, updated_ref, *refs):
    groups = (len(refs) - 1) // 2
    got_refs, out_ref, send_refs = refs[:groups], refs[groups], refs[groups + 1 :]
    coarse = send_refs[0].shape[0]
    rows = order_ref.shape[1]
    capacity = rows // 2
    pieces = capacity // LANES
    here = group_ref[0, 0]
    place = lax.broadcasted_iota(I32, (8, rows), 1)
    owner = jnp.zeros((8, rows), I32)
    goal = jnp.zeros((8, rows), I32)
    for ahead, got_ref in enumerate(got_refs):
        k = lax.rem(here + ahead, groups)
        start = 0
        for other in range(groups - 1):
            start = start + jnp.where(other < k, count_ref[0, other], 0)
        listed = got_ref[capacity:, :].astype(F32)
        line = choose(here, [
            jnp.concatenate(
                [listed[j * pieces + i : j * pieces + i + 1, :] for i in range(pieces)], axis=1
            )
            for j in range(groups)
        ]).astype(I32)
        line = jnp.concatenate([line, jnp.zeros((1, rows - capacity), I32)], axis=1)
        line = pltpu.roll(jnp.broadcast_to(line, (8, rows)), start, 1)
        inside = (place >= start) & (place < start + count_ref[0, k])
        owner = jnp.where(inside, ahead, owner)
        goal = jnp.where(inside, line, goal)
    digits = jnp.where(lax.broadcasted_iota(I32, (8, rows), 0) == 0, owner, goal)
    by_row = nt(digits.astype(F32).astype(BF), hit_rows(order_ref[...], rows))
    goal = (by_row[0:1, :] * coarse + by_row[1:2, :]).astype(I32)
    out_ref[...] = goal
    pooled = nn(hit_rows(goal, groups * coarse), updated_ref[...]).astype(BF)
    for k, send_ref in enumerate(send_refs):
        send_ref[...] = pooled[k * coarse : (k + 1) * coarse, :]


def edge_first_kernel(source_ref, target_ref, nodes_ref, out_ref):
    nodes = halves(nodes_ref[...])
    out_ref[0] = pick_rows(spread_column(source_ref[...]), nodes).astype(BF)
    out_ref[1] = pick_rows(spread_column(target_ref[...]), nodes).astype(BF)


def edge_second_kernel(
    source_ref, target_ref, own_ref, edges_ref, ghosts_ref, w1_ref, w2_ref,
    nodes_ref, v1_ref, v2_ref,
    pre_ref, src_ref, summed_ref, updated_ref, total,
):
    step = pl.program_id(0)
    rows = nodes_ref.shape[0]

    @pl.when(step == 0)
    def _():
        total[...] = jnp.zeros_like(total)

    ghosts = halves(ghosts_ref[...])
    from_ghost = spread_column(source_ref[...]) - rows
    target = target_ref[...]
    messages = []
    for part in range(0, target.shape[1], SECOND_SUB):
        here = slice(part, part + SECOND_SUB)
        src = own_ref[0, here, :] + pick_rows(from_ghost[here], ghosts).astype(BF)
        src_ref[here, :] = src
        stacked = jnp.concatenate([src, own_ref[1, here, :], edges_ref[here, :]], axis=1)
        pre = nn(stacked, w1_ref[...])
        pre_ref[here, :] = pre
        hidden = (pre * sigmoid(pre)).astype(BF)
        message, _ = norm_parts(nn(hidden, w2_ref[...]))
        messages.append(message.astype(BF))
    total[...] += sum_rows(
        target, spread_column(target), jnp.concatenate(messages, axis=0), rows // 2
    )

    @pl.when(step == pl.num_programs(0) - 1)
    def _():
        summed = unfold(total[...]).astype(BF)
        summed_ref[...] = summed
        nodes = nodes_ref[...]
        pre_node = nn(jnp.concatenate([nodes, summed], axis=1), v1_ref[...])
        hidden_node = (pre_node * sigmoid(pre_node)).astype(BF)
        normed, _ = norm_parts(nn(hidden_node, v2_ref[...]))
        updated_ref[...] = (nodes.astype(F32) + normed).astype(BF)


def coarse_kernel(feat_ref, cot_ref, from_fine_ref, w1_ref, w2_ref, *refs):
    got_refs, (grad_ref, back_ref, g1_ref, g2_ref) = refs[:-4], refs[-4:]
    got = got_refs[0][...].astype(F32)
    for got_ref in got_refs[1:]:
        got = got + got_ref[...].astype(F32)
    pooled = (got * POOL_SHARE).astype(BF)
    cot = cot_ref[...].astype(F32)
    grad_out = (cot + from_fine_ref[...]).astype(BF)
    joined = jnp.concatenate([feat_ref[...], pooled], axis=1)
    pre = nn(joined, w1_ref[...])
    sig = sigmoid(pre)
    hidden = (pre * sig).astype(BF)
    g2_ref[...] = tn(hidden, grad_out)
    grad_pre = (nt(grad_out, w2_ref[...]) * slope(pre, sig)).astype(BF)
    g1_ref[...] = tn(joined, grad_pre)
    grad_in = nt(grad_pre, w1_ref[...])
    grad_ref[...] = cot + grad_in[:, :LANES]
    back_ref[...] = (grad_in[:, LANES:] * POOL_SHARE).astype(BF)


def edge_back_kernel(
    source_ref, target_ref, pre_ref, src_ref, tgt_ref, edges_ref, cot_ref, w1_ref, w2_ref,
    goal_ref, node_cot_ref, nodes_ref, summed_ref, v1_ref, v2_ref, c1_ref, c2_ref, *rest,
):
    gp_refs = rest[:-10]
    grad_pre_ref, local_ref, joint_ref, wide, gw1, gw2, gv1, gv2, by_ghost, pack_ref = rest[-10:]
    step = pl.program_id(0)
    rows = nodes_ref.shape[0]

    @pl.when(step == 0)
    def _():
        by_ghost[...] = jnp.zeros_like(by_ghost)
        gw1[...] = jnp.zeros_like(gw1)
        gw2[...] = jnp.zeros_like(gw2)
        table = halves(jnp.concatenate([gp_ref[...] for gp_ref in gp_refs], axis=0))
        from_coarse = pick_rows(spread_column(goal_ref[...]), table)
        updated_grad = node_cot_ref[...].astype(F32) + from_coarse
        joined = jnp.concatenate([nodes_ref[...], summed_ref[...]], axis=1)
        pre = nn(joined, v1_ref[...])
        sig = sigmoid(pre)
        hidden = (pre * sig).astype(BF)
        normed, inv_std = norm_parts(nn(hidden, v2_ref[...]))
        grad_norm = norm_back(normed, inv_std, updated_grad).astype(BF)
        gv2[...] = tn(hidden, grad_norm)
        grad_pre = (nt(grad_norm, v2_ref[...]) * slope(pre, sig)).astype(BF)
        gv1[...] = tn(joined, grad_pre)
        grad_in = nt(grad_pre, v1_ref[...])
        local_ref[...] = updated_grad + grad_in[:, :LANES]
        wide[...] = halves(grad_in[:, LANES:].astype(BF))

    target = spread_column(target_ref[...])
    hiddens, grad_norms, grad_pres = [], [], []
    for part in range(0, target.shape[0], BACK_SUB):
        here = slice(part, part + BACK_SUB)
        message_grad = cot_ref[here, :].astype(F32) + pick_rows(target[here], wide[...])
        pre = pre_ref[here, :]
        sig = sigmoid(pre)
        hidden = (pre * sig).astype(BF)
        normed, inv_std = norm_parts(nn(hidden, w2_ref[...]))
        grad_norm = norm_back(normed, inv_std, message_grad).astype(BF)
        grad_pre = (nt(grad_norm, w2_ref[...]) * slope(pre, sig)).astype(BF)
        hiddens.append(hidden)
        grad_norms.append(grad_norm)
        grad_pres.append(grad_pre)
    grad_pre = jnp.concatenate(grad_pres, axis=0)
    grad_pre_ref[...] = grad_pre
    gw2[...] += tn(jnp.concatenate(hiddens, axis=0), jnp.concatenate(grad_norms, axis=0))
    stacked = jnp.concatenate([src_ref[...], tgt_ref[0], edges_ref[...]], axis=1)
    gw1[...] += tn(stacked, grad_pre)
    source = source_ref[...] - rows
    by_ghost[...] += sum_rows(source, spread_column(source), grad_pre, by_ghost.shape[0])

    @pl.when(step == pl.num_programs(0) - 1)
    def _():
        place = 0
        for part in (gw1, gw2, gv1, gv2, c1_ref, c2_ref):
            size = part.shape[0]
            pack_ref[place : place + size, :] = part[...].astype(BF)
            place += size
        pack_ref[place:, :] = jnp.zeros((pack_ref.shape[0] - place, LANES), BF)
        ghost = times_transposed(unfold(by_ghost[...]), w1_ref[:LANES, :]).astype(BF)
        domains, both, _ = joint_ref.shape
        share = pack_ref.shape[0] // domains
        joint_ref[:, :share, :] = pack_ref[...].reshape(domains, share, LANES)
        joint_ref[:, share:, :] = ghost.reshape(domains, both - share, LANES)


def own_back_kernel(
    source_ref, target_ref, grad_pre_ref, cot_ref, local_ref, w1_ref,
    out_ref, edges_ref, by_source, by_target,
):
    step = pl.program_id(0)
    half = by_source.shape[0]

    @pl.when(step == 0)
    def _():
        by_source[...] = jnp.zeros_like(by_source)
        by_target[...] = jnp.zeros_like(by_target)

    grad_pre = grad_pre_ref[...]
    source, target = source_ref[...], target_ref[...]
    by_source[...] += sum_rows(source, spread_column(source), grad_pre, half)
    by_target[...] += sum_rows(target, spread_column(target), grad_pre, half)
    edges_ref[...] = cot_ref[...].astype(F32) + nt(grad_pre, w1_ref[2 * LANES :, :])

    @pl.when(step == pl.num_programs(0) - 1)
    def _():
        out_ref[...] = (
            local_ref[...]
            + times_transposed(unfold(by_source[...]), w1_ref[:LANES, :])
            + times_transposed(unfold(by_target[...]), w1_ref[LANES : 2 * LANES, :])
        )


def add_back_kernel(boundary_ref, wanted_ref, got_ref, local_ref, out_ref):
    rows = local_ref.shape[0]
    border = boundary_ref.shape[1]
    wanted = jnp.transpose(wanted_ref[...].astype(F32))[0:1, :].astype(I32)
    slots = wanted.shape[1] // got_ref.shape[0]
    got = got_ref[:, got_ref.shape[1] - slots :, :].reshape(wanted.shape[1], LANES)
    border_grad = nn(hit_rows(wanted, border), got)
    out_ref[...] = local_ref[...] + fold_wide(
        nn(hit_rows(boundary_ref[...], rows), split_wide(border_grad))
    )


def add_parts_kernel(got_ref, out_ref):
    size = out_ref.shape[0]
    total = got_ref[0, :size, :].astype(F32)
    for k in range(1, got_ref.shape[0]):
        total = total + got_ref[k, :size, :].astype(F32)
    out_ref[...] = total


def add_groups_kernel(*refs):
    part_refs, out_ref = refs[:-1], refs[-1]
    total = part_refs[0][...]
    for part_ref in part_refs[1:]:
        total = total + part_ref[...]
    total = total.astype(BF)
    for k in range(out_ref.shape[0]):
        out_ref[k] = total


def scale_kernel(pack_ref, *out_refs, scales):
    place = 0
    for out_ref, scale in zip(out_refs, scales):
        size = out_ref.shape[0]
        out_ref[...] = pack_ref[place : place + size, :].astype(F32) * scale
        place += size


def whole(shape):
    zeros = (0,) * len(shape)
    return pl.BlockSpec(shape, lambda *_: zeros)


def call(kernel, out_shapes, *args, flops=0, bytes_accessed=0, in_specs=None, out_specs=None,
         grid=None, scratch=(), name=None, vmem=40):
    single = not isinstance(out_shapes, (list, tuple))
    extra = {}
    if grid is not None:
        extra["grid"] = grid
    if in_specs is not None:
        extra["in_specs"] = in_specs
    if out_specs is not None:
        extra["out_specs"] = out_specs
    return pl.pallas_call(
        kernel,
        out_shape=out_shapes if single else list(out_shapes),
        scratch_shapes=list(scratch),
        compiler_params=pltpu.CompilerParams(vmem_limit_bytes=vmem * 2**20),
        cost_estimate=pl.CostEstimate(
            flops=flops, bytes_accessed=bytes_accessed, transcendentals=0
        ),
        name=name,
        **extra,
    )(*args)


def local(
    node_features, edge_features, coarse_features,
    edge_w_one, edge_w_two, node_w_one, node_w_two, coarse_w_one, coarse_w_two,
    edge_source, edge_target, boundary, ghost_pos, restr_order, restr_count, coarse_slot,
    node_cotangent, edge_cotangent, coarse_cotangent,
):
    rows, latent = node_features.shape
    edges = edge_features.shape[0]
    coarse = coarse_features.shape[0]
    groups = lax.axis_size("group")
    domains = lax.axis_size("dom")
    parts = groups * domains
    slots = ghost_pos.shape[2]
    ghosts = domains * slots
    shape = jax.ShapeDtypeStruct

    def edge_blocks(block):
        return (
            (edges // block,),
            pl.BlockSpec((1, block), lambda i: (0, i)),
            pl.BlockSpec((block, latent), lambda i: (i, 0)),
        )

    exchange = functools.partial(lax.all_to_all, split_axis=0, concat_axis=0, tiled=True)

    def turned(step):
        return [(k, (k - step) % groups) for k in range(groups)]

    source = edge_source.reshape(1, edges)
    target = edge_target.reshape(1, edges)
    spread = call(
        spread_kernel, shape((ghosts, latent), BF), ghost_pos,
        flops=10**6, bytes_accessed=10**5, name="spread", vmem=8,
    )
    asked = exchange(spread.reshape(domains, slots, latent), "dom").reshape(ghosts, latent)
    slot_list = coarse_slot.reshape(groups, -1)
    here = lax.axis_index("group").astype(I32).reshape(1, 1)

    grid_block = 2048
    grid, index_spec, edge_spec = edge_blocks(grid_block)
    own_rows = call(
        edge_first_kernel, shape((2, edges, latent), BF), source, target, node_features,
        grid=grid,
        in_specs=[index_spec, index_spec, whole((rows, latent))],
        out_specs=pl.BlockSpec((2, grid_block, latent), lambda i: (0, i, 0)),
        flops=4 * 10**9, bytes_accessed=3 * 10**6, name="edge_first", vmem=61,
    )
    messages = call(
        order_kernel, [shape((rows // 2 + 16, latent), BF)] * groups,
        here, restr_count, restr_order, slot_list, node_cotangent,
        in_specs=[pl.BlockSpec(memory_space=pltpu.SMEM)] * 2
        + [pl.BlockSpec(memory_space=pltpu.VMEM)] * 3,
        flops=10**9, bytes_accessed=10**6, name="order", vmem=16,
    )
    asked, own_rows, messages = lax.optimization_barrier((asked, own_rows, messages))
    share = call(
        share_kernel, shape((ghosts, latent), BF), boundary, asked, node_features,
        flops=10**9, bytes_accessed=10**6, name="share", vmem=16,
    )
    share, messages = lax.optimization_barrier((share, messages))
    messages = [messages[0]] + [
        lax.ppermute(messages[ahead], "group", turned(ahead)) for ahead in range(1, groups)
    ]
    ghost_rows = exchange(share.reshape(domains, slots, latent), "dom").reshape(ghosts, latent)
    grid, index_spec, edge_spec = edge_blocks(4096)
    pre, src_rows, summed, updated = call(
        edge_second_kernel,
        [shape((edges, latent), F32), shape((edges, latent), BF), shape((rows, latent), BF),
         shape((rows, latent), BF)],
        source, target, own_rows, edge_features, ghost_rows, edge_w_one, edge_w_two,
        node_features, node_w_one, node_w_two,
        grid=grid,
        in_specs=[index_spec, index_spec, whole((2, edges, latent)), edge_spec,
                  whole((ghosts, latent)), whole((3 * latent, latent)), whole((latent, latent)),
                  whole((rows, latent)), whole((2 * latent, latent)), whole((latent, latent))],
        out_specs=[edge_spec, edge_spec, whole((rows, latent)), whole((rows, latent))],
        scratch=[pltpu.VMEM((rows // 2, 2 * latent), F32)],
        flops=5 * 10**9, bytes_accessed=8 * 10**6, name="edge_second",
    )
    goal, *send = call(
        pool_kernel, [shape((1, rows), I32)] + [shape((coarse, latent), BF)] * groups,
        here, restr_count, restr_order, updated, *messages,
        in_specs=[pl.BlockSpec(memory_space=pltpu.SMEM)] * 2
        + [pl.BlockSpec(memory_space=pltpu.VMEM)] * (2 + groups),
        flops=10**9, bytes_accessed=10**6, name="pool", vmem=16,
    )
    got = [send[0]] + [
        lax.ppermute(send[ahead], "group", turned(-ahead)) for ahead in range(1, groups)
    ]
    from_fine = call(
        cot_pool_kernel, shape((coarse, latent), F32), here, slot_list, *messages,
        in_specs=[pl.BlockSpec(memory_space=pltpu.SMEM)]
        + [pl.BlockSpec(memory_space=pltpu.VMEM)] * (1 + groups),
        flops=10**9, bytes_accessed=10**6, name="cot_pool", vmem=16,
    )
    got, from_fine = lax.optimization_barrier((got, from_fine))
    grad_coarse, coarse_back, grad_c_one, grad_c_two = call(
        coarse_kernel,
        [shape((coarse, latent), F32), shape((coarse, latent), BF),
         shape((2 * latent, latent), F32), shape((latent, latent), F32)],
        coarse_features, coarse_cotangent, from_fine, coarse_w_one, coarse_w_two, *got,
        flops=10**8, bytes_accessed=10**6, name="coarse", vmem=16,
    )
    returned = [coarse_back] + [
        lax.ppermute(coarse_back, "group", turned(ahead)) for ahead in range(1, groups)
    ]
    share_rows = 48
    pack_rows = domains * share_rows
    grid, index_spec, edge_spec = edge_blocks(4096)
    joint_shape = (domains, share_rows + slots, latent)
    grad_pre, node_local, joint = call(
        edge_back_kernel,
        [shape((edges, latent), BF), shape((rows, latent), F32), shape(joint_shape, BF)],
        source, target, pre, src_rows, own_rows, edge_features, edge_cotangent, edge_w_one, edge_w_two,
        goal, node_cotangent, node_features, summed, node_w_one, node_w_two,
        grad_c_one, grad_c_two, *returned,
        grid=grid,
        in_specs=[index_spec, index_spec, edge_spec, edge_spec,
                  pl.BlockSpec((1, edges, latent), lambda i: (1, 0, 0)), edge_spec, edge_spec,
                  whole((3 * latent, latent)), whole((latent, latent)),
                  whole((1, rows)),
                  whole((rows, latent)), whole((rows, latent)), whole((rows, latent)),
                  whole((2 * latent, latent)), whole((latent, latent)),
                  whole((2 * latent, latent)), whole((latent, latent))]
        + [whole((coarse, latent))] * groups,
        out_specs=[edge_spec, whole((rows, latent)), whole(joint_shape)],
        scratch=[pltpu.VMEM((rows // 2, 2 * latent), BF), pltpu.VMEM((3 * latent, latent), F32),
                 pltpu.VMEM((latent, latent), F32), pltpu.VMEM((2 * latent, latent), F32),
                 pltpu.VMEM((latent, latent), F32), pltpu.VMEM((ghosts // 2, 2 * latent), F32),
                 pltpu.VMEM((pack_rows, latent), BF)],
        flops=6 * 10**9, bytes_accessed=10**7, name="edge_back",
    )
    grid, index_spec, edge_spec = edge_blocks(4096)
    own_local, grad_edges = call(
        own_back_kernel,
        [shape((rows, latent), F32), shape((edges, latent), F32)],
        source, target, grad_pre, edge_cotangent, node_local, edge_w_one,
        grid=grid,
        in_specs=[index_spec, index_spec, edge_spec, edge_spec, whole((rows, latent)),
                  whole((3 * latent, latent))],
        out_specs=[whole((rows, latent)), edge_spec],
        scratch=[pltpu.VMEM((rows // 2, 2 * latent), F32)] * 2,
        flops=4 * 10**9, bytes_accessed=5 * 10**6, name="own_back",
    )
    joint_got, own_local = lax.optimization_barrier((exchange(joint, "dom"), own_local))
    part_sum = call(
        add_parts_kernel, shape((share_rows, latent), F32), joint_got,
        flops=10**6, bytes_accessed=10**6, name="add_parts", vmem=16,
    )
    part_sums = [part_sum] + [
        lax.ppermute(part_sum, "group", turned(ahead)) for ahead in range(1, groups)
    ]
    pack_sum = call(
        add_groups_kernel, shape((domains, share_rows, latent), BF), *part_sums,
        flops=10**6, bytes_accessed=10**6, name="add_groups", vmem=16,
    )
    pack_all = exchange(pack_sum, "dom").reshape(pack_rows, latent)
    grad_nodes = call(
        add_back_kernel, shape((rows, latent), F32), boundary, asked, joint_got, own_local,
        flops=10**9, bytes_accessed=10**6, name="add_back", vmem=16,
    )
    edge_scale = (edges * parts) ** (-0.5)
    node_scale = (rows * parts) ** (-0.5)
    coarse_scale = (coarse * parts) ** (-0.5)
    weight_grads = call(
        functools.partial(
            scale_kernel,
            scales=(edge_scale, edge_scale, node_scale, node_scale, coarse_scale, coarse_scale),
        ),
        [shape((size * latent, latent), F32) for size in (3, 1, 2, 1, 2, 1)],
        pack_all,
        flops=10**6, bytes_accessed=10**6, name="scale", vmem=16,
    )
    return (grad_nodes, grad_edges, grad_coarse, *weight_grads)


def solution(mesh):
    rows = P(("group", "dom"), None)
    cube = P(("group", "dom"), None, None)
    line = P(("group", "dom"))
    placed = (
        rows, rows, rows, P(), P(), P(), P(), P(), P(), line, line, rows, cube, rows, rows, cube,
        rows, rows, rows,
    )
    return jax.shard_map(
        local,
        mesh=mesh,
        in_specs=placed,
        out_specs=(rows, rows, rows, P(), P(), P(), P(), P(), P()),
        check_vma=False,
    )
```

```python
import functools

import jax
import jax.numpy as jnp
from jax import lax
from jax.experimental import pallas as pl
from jax.experimental.pallas import tpu as pltpu
from jax.sharding import PartitionSpec as P

NORM_EPSILON = 1e-05
POOL_SHARE = 0.25
BF = jnp.bfloat16
F32 = jnp.float32
I32 = jnp.int32
LANES = 128
SECOND_SUB = 512
BACK_SUB = 2048


def nn(a, b):
    return lax.dot_general(a, b, (((1,), (0,)), ((), ())), preferred_element_type=F32)


def nt(a, b):
    return lax.dot_general(a, b, (((1,), (1,)), ((), ())), preferred_element_type=F32)


def tn(a, b):
    return lax.dot_general(a, b, (((0,), (0,)), ((), ())), preferred_element_type=F32)


def as_hit(mask):
    return jnp.where(mask, 1.0, 0.0).astype(BF)


def hit_rows(index_row, count, base=0):
    width = index_row.shape[1]
    return as_hit(lax.broadcasted_iota(I32, (count, width), 0) == index_row - base)


def spread_column(index_row):
    width = index_row.shape[1]
    return jnp.transpose(jnp.broadcast_to(index_row, (LANES, width)))


def hit_columns(index_column, count, base=0):
    lane = lax.broadcasted_iota(I32, index_column.shape, 1)
    return jnp.concatenate(
        [as_hit(lane == index_column - (base + LANES * j)) for j in range(count // LANES)], axis=1
    )


def halves(table):
    half = table.shape[0] // 2
    return jnp.concatenate([table[:half], table[half:]], axis=1)


def pick_rows(index_column, table_halves):
    half = table_halves.shape[0]
    upper = index_column >= half
    wide = nn(hit_columns(jnp.where(upper, index_column - half, index_column), half), table_halves)
    return jnp.where(upper, wide[:, LANES:], wide[:, :LANES])


def sum_rows(index_row, index_column, values, half):
    upper = index_column >= half
    nothing = jnp.zeros_like(values)
    both = jnp.concatenate(
        [jnp.where(upper, nothing, values), jnp.where(upper, values, nothing)], axis=1
    )
    return nn(hit_rows(jnp.where(index_row >= half, index_row - half, index_row), half), both)


def unfold(sums):
    return jnp.concatenate([sums[:, :LANES], sums[:, LANES:]], axis=0)


def split_wide(values):
    high = values.astype(BF)
    low = (values - high.astype(F32)).astype(BF)
    return jnp.concatenate([high, low], axis=1)


def fold_wide(values):
    return values[:, :LANES] + values[:, LANES:]


def times_transposed(values, weights):
    return nt(split_wide(values), jnp.concatenate([weights, weights], axis=1))


def mean_lanes(values):
    return jnp.mean(values, axis=-1, keepdims=True)


def norm_parts(values):
    return scaled(values - mean_lanes(values))


def scaled(centred):
    inv_std = lax.rsqrt(mean_lanes(centred * centred) + NORM_EPSILON)
    return centred * inv_std, inv_std


def norm_back(normed, inv_std, grad_in):
    return inv_std * (grad_in - mean_lanes(grad_in) - normed * mean_lanes(grad_in * normed))


def sigmoid(values):
    return 1.0 / (1.0 + jnp.exp(-values))


def slope(values, sig):
    return sig * (1.0 + values * (1.0 - sig))


def spread_kernel(wanted_ref, out_ref):
    _, domains, slots = wanted_ref.shape
    ghosts = out_ref.shape[0]
    first = lax.broadcasted_iota(I32, (ghosts, domains), 0) // slots
    pick = as_hit(first == lax.broadcasted_iota(I32, (ghosts, domains), 1))
    by_owner = nn(pick, wanted_ref[0].astype(F32).astype(BF))
    slot = lax.broadcasted_iota(I32, (ghosts, slots), 0) % slots
    own = jnp.where(slot == lax.broadcasted_iota(I32, (ghosts, slots), 1), by_owner, 0.0).astype(BF)
    out_ref[...] = nn(own, jnp.ones((slots, LANES), BF)).astype(BF)


def share_kernel(boundary_ref, wanted_ref, nodes_ref, out_ref):
    border = boundary_ref.shape[1]
    shared = pick_rows(spread_column(boundary_ref[...]), halves(nodes_ref[...])).astype(BF)
    wanted = wanted_ref[...].astype(F32).astype(I32)
    out_ref[...] = nn(hit_columns(wanted, border), shared).astype(BF)


def choose(index, lines):
    found = lines[0]
    for k in range(1, len(lines)):
        found = jnp.where(index == k, lines[k], found)
    return found


def order_kernel(group_ref, count_ref, order_ref, slot_ref, node_cot_ref, *out_refs):
    groups, capacity = slot_ref.shape
    rows = order_ref.shape[1]
    here = group_ref[0, 0]
    table = halves(node_cot_ref[...])
    order = jnp.broadcast_to(order_ref[...], (8, rows))
    place = lax.broadcasted_iota(I32, (1, capacity), 1)
    slots = jnp.concatenate(
        [slot_ref[k : k + 1, at : at + LANES] for k in range(groups) for at in range(0, capacity, LANES)],
        axis=0,
    ).astype(F32).astype(BF)
    for ahead, out_ref in enumerate(out_refs):
        k = lax.rem(here + (groups - ahead), groups)
        start = 0
        for other in range(groups - 1):
            start = start + jnp.where(other < k, count_ref[0, other], 0)
        line = pltpu.roll(order, lax.rem(rows - start, rows), 1)[0:1, :capacity]
        line = jnp.where(place < count_ref[0, k], line, -1)
        out_ref[:capacity, :] = pick_rows(spread_column(line), table).astype(BF)
        out_ref[capacity:, :] = slots


def cot_pool_kernel(group_ref, slot_ref, *refs):
    got_refs, out_ref = refs[:-1], refs[-1]
    groups, capacity = slot_ref.shape
    lines = [slot_ref[k : k + 1, :] for k in range(groups)]
    total = jnp.zeros(out_ref.shape, F32)
    for ahead, got_ref in enumerate(got_refs):
        line = choose(lax.rem(group_ref[0, 0] + ahead, groups), lines)
        total = total + nn(hit_rows(line, out_ref.shape[0]), got_ref[:capacity, :])
    out_ref[...] = total


def pool_kernel(group_ref, count_ref, order_ref, updated_ref, *refs):
    groups = (len(refs) - 1) // 2
    got_refs, out_ref, send_refs = refs[:groups], refs[groups], refs[groups + 1 :]
    coarse = send_refs[0].shape[0]
    rows = order_ref.shape[1]
    capacity = rows // 2
    pieces = capacity // LANES
    here = group_ref[0, 0]
    place = lax.broadcasted_iota(I32, (8, rows), 1)
    owner = jnp.zeros((8, rows), I32)
    goal = jnp.zeros((8, rows), I32)
    for ahead, got_ref in enumerate(got_refs):
        k = lax.rem(here + ahead, groups)
        start = 0
        for other in range(groups - 1):
            start = start + jnp.where(other < k, count_ref[0, other], 0)
        listed = got_ref[capacity:, :].astype(F32)
        line = choose(here, [
            jnp.concatenate(
                [listed[j * pieces + i : j * pieces + i + 1, :] for i in range(pieces)], axis=1
            )
            for j in range(groups)
        ]).astype(I32)
        line = jnp.concatenate([line, jnp.zeros((1, rows - capacity), I32)], axis=1)
        line = pltpu.roll(jnp.broadcast_to(line, (8, rows)), start, 1)
        inside = (place >= start) & (place < start + count_ref[0, k])
        owner = jnp.where(inside, ahead, owner)
        goal = jnp.where(inside, line, goal)
    digits = jnp.where(lax.broadcasted_iota(I32, (8, rows), 0) == 0, owner, goal)
    by_row = nt(digits.astype(F32).astype(BF), hit_rows(order_ref[...], rows))
    goal = (by_row[0:1, :] * coarse + by_row[1:2, :]).astype(I32)
    out_ref[...] = goal
    pooled = nn(hit_rows(goal, groups * coarse), updated_ref[...]).astype(BF)
    for k, send_ref in enumerate(send_refs):
        send_ref[...] = pooled[k * coarse : (k + 1) * coarse, :]


def edge_first_kernel(source_ref, target_ref, nodes_ref, out_ref):
    nodes = halves(nodes_ref[...])
    out_ref[0] = pick_rows(spread_column(source_ref[...]), nodes).astype(BF)
    out_ref[1] = pick_rows(spread_column(target_ref[...]), nodes).astype(BF)


def edge_second_kernel(
    source_ref, target_ref, own_ref, edges_ref, ghosts_ref, w1_ref, w2_ref,
    nodes_ref, v1_ref, v2_ref,
    pre_ref, src_ref, summed_ref, updated_ref, total,
):
    step = pl.program_id(0)
    rows = nodes_ref.shape[0]

    @pl.when(step == 0)
    def _():
        total[...] = jnp.zeros_like(total)

    ghosts = halves(ghosts_ref[...])
    from_ghost = spread_column(source_ref[...]) - rows
    target = target_ref[...]
    messages = []
    for part in range(0, target.shape[1], SECOND_SUB):
        here = slice(part, part + SECOND_SUB)
        src = own_ref[0, here, :] + pick_rows(from_ghost[here], ghosts).astype(BF)
        src_ref[here, :] = src
        stacked = jnp.concatenate([src, own_ref[1, here, :], edges_ref[here, :]], axis=1)
        pre = nn(stacked, w1_ref[...])
        pre_ref[here, :] = pre
        hidden = (pre * sigmoid(pre)).astype(BF)
        message, _ = norm_parts(nn(hidden, w2_ref[...]))
        messages.append(message.astype(BF))
    total[...] += sum_rows(
        target, spread_column(target), jnp.concatenate(messages, axis=0), rows // 2
    )

    @pl.when(step == pl.num_programs(0) - 1)
    def _():
        summed = unfold(total[...]).astype(BF)
        summed_ref[...] = summed
        nodes = nodes_ref[...]
        pre_node = nn(jnp.concatenate([nodes, summed], axis=1), v1_ref[...])
        hidden_node = (pre_node * sigmoid(pre_node)).astype(BF)
        normed, _ = norm_parts(nn(hidden_node, v2_ref[...]))
        updated_ref[...] = (nodes.astype(F32) + normed).astype(BF)


def coarse_kernel(feat_ref, cot_ref, from_fine_ref, w1_ref, w2_ref, *refs):
    got_refs, (grad_ref, back_ref, g1_ref, g2_ref) = refs[:-4], refs[-4:]
    got = got_refs[0][...].astype(F32)
    for got_ref in got_refs[1:]:
        got = got + got_ref[...].astype(F32)
    pooled = (got * POOL_SHARE).astype(BF)
    cot = cot_ref[...].astype(F32)
    grad_out = (cot + from_fine_ref[...]).astype(BF)
    joined = jnp.concatenate([feat_ref[...], pooled], axis=1)
    pre = nn(joined, w1_ref[...])
    sig = sigmoid(pre)
    hidden = (pre * sig).astype(BF)
    g2_ref[...] = tn(hidden, grad_out)
    grad_pre = (nt(grad_out, w2_ref[...]) * slope(pre, sig)).astype(BF)
    g1_ref[...] = tn(joined, grad_pre)
    grad_in = nt(grad_pre, w1_ref[...])
    grad_ref[...] = cot + grad_in[:, :LANES]
    back_ref[...] = (grad_in[:, LANES:] * POOL_SHARE).astype(BF)


def slopes_kernel(
    pre_ref, w2_ref, nodes_ref, summed_ref, v1_ref, v2_ref,
    slope_ref, hidden_ref, centred_ref, node_slope_ref, node_hidden_ref, node_centred_ref,
):
    def fill(pre, weights, out_refs, here):
        sig = sigmoid(pre)
        hidden = (pre * sig).astype(BF)
        pre_norm = nn(hidden, weights)
        parts = (slope(pre, sig), hidden, pre_norm - mean_lanes(pre_norm))
        for out_ref, part in zip(out_refs, parts):
            out_ref[here, :] = part

    for part in range(0, pre_ref.shape[0], SECOND_SUB):
        here = slice(part, part + SECOND_SUB)
        fill(pre_ref[here, :], w2_ref[...], (slope_ref, hidden_ref, centred_ref), here)
    joined = jnp.concatenate([nodes_ref[...], summed_ref[...]], axis=1)
    fill(
        nn(joined, v1_ref[...]), v2_ref[...],
        (node_slope_ref, node_hidden_ref, node_centred_ref),
        slice(0, nodes_ref.shape[0]),
    )


def edge_back_kernel(
    node_slope_ref, node_hidden_ref, node_centred_ref,
    source_ref, target_ref, slope_ref, hidden_ref, centred_ref, src_ref, tgt_ref, edges_ref, cot_ref, w1_ref, w2_ref,
    goal_ref, node_cot_ref, nodes_ref, summed_ref, v1_ref, v2_ref, c1_ref, c2_ref, *rest,
):
    gp_refs = rest[:-10]
    grad_pre_ref, local_ref, joint_ref, wide, gw1, gw2, gv1, gv2, by_ghost, pack_ref = rest[-10:]
    step = pl.program_id(0)
    rows = nodes_ref.shape[0]

    @pl.when(step == 0)
    def _():
        by_ghost[...] = jnp.zeros_like(by_ghost)
        gw1[...] = jnp.zeros_like(gw1)
        gw2[...] = jnp.zeros_like(gw2)
        table = halves(jnp.concatenate([gp_ref[...] for gp_ref in gp_refs], axis=0))
        from_coarse = pick_rows(spread_column(goal_ref[...]), table)
        updated_grad = node_cot_ref[...].astype(F32) + from_coarse
        joined = jnp.concatenate([nodes_ref[...], summed_ref[...]], axis=1)
        grad_norm = norm_back(*scaled(node_centred_ref[...]), updated_grad).astype(BF)
        gv2[...] = tn(node_hidden_ref[...], grad_norm)
        grad_pre = (nt(grad_norm, v2_ref[...]) * node_slope_ref[...]).astype(BF)
        gv1[...] = tn(joined, grad_pre)
        grad_in = nt(grad_pre, v1_ref[...])
        local_ref[...] = updated_grad + grad_in[:, :LANES]
        wide[...] = halves(grad_in[:, LANES:].astype(BF))

    target = spread_column(target_ref[...])
    grad_norms, grad_pres = [], []
    for part in range(0, target.shape[0], BACK_SUB):
        here = slice(part, part + BACK_SUB)
        message_grad = cot_ref[here, :].astype(F32) + pick_rows(target[here], wide[...])
        grad_norm = norm_back(*scaled(centred_ref[here, :]), message_grad).astype(BF)
        grad_pre = (nt(grad_norm, w2_ref[...]) * slope_ref[here, :]).astype(BF)
        grad_norms.append(grad_norm)
        grad_pres.append(grad_pre)
    grad_pre = jnp.concatenate(grad_pres, axis=0)
    grad_pre_ref[...] = grad_pre
    gw2[...] += tn(hidden_ref[...], jnp.concatenate(grad_norms, axis=0))
    stacked = jnp.concatenate([src_ref[...], tgt_ref[0], edges_ref[...]], axis=1)
    gw1[...] += tn(stacked, grad_pre)
    source = source_ref[...] - rows
    by_ghost[...] += sum_rows(source, spread_column(source), grad_pre, by_ghost.shape[0])

    @pl.when(step == pl.num_programs(0) - 1)
    def _():
        place = 0
        for part in (gw1, gw2, gv1, gv2, c1_ref, c2_ref):
            size = part.shape[0]
            pack_ref[place : place + size, :] = part[...].astype(BF)
            place += size
        pack_ref[place:, :] = jnp.zeros((pack_ref.shape[0] - place, LANES), BF)
        ghost = times_transposed(unfold(by_ghost[...]), w1_ref[:LANES, :]).astype(BF)
        domains, both, _ = joint_ref.shape
        share = pack_ref.shape[0] // domains
        joint_ref[:, :share, :] = pack_ref[...].reshape(domains, share, LANES)
        joint_ref[:, share:, :] = ghost.reshape(domains, both - share, LANES)


def own_back_kernel(
    source_ref, target_ref, grad_pre_ref, cot_ref, local_ref, w1_ref,
    out_ref, edges_ref, by_source, by_target,
):
    step = pl.program_id(0)
    half = by_source.shape[0]

    @pl.when(step == 0)
    def _():
        by_source[...] = jnp.zeros_like(by_source)
        by_target[...] = jnp.zeros_like(by_target)

    grad_pre = grad_pre_ref[...]
    source, target = source_ref[...], target_ref[...]
    by_source[...] += sum_rows(source, spread_column(source), grad_pre, half)
    by_target[...] += sum_rows(target, spread_column(target), grad_pre, half)
    edges_ref[...] = cot_ref[...].astype(F32) + nt(grad_pre, w1_ref[2 * LANES :, :])

    @pl.when(step == pl.num_programs(0) - 1)
    def _():
        out_ref[...] = (
            local_ref[...]
            + times_transposed(unfold(by_source[...]), w1_ref[:LANES, :])
            + times_transposed(unfold(by_target[...]), w1_ref[LANES : 2 * LANES, :])
        )


def add_back_kernel(boundary_ref, wanted_ref, got_ref, local_ref, out_ref):
    rows = local_ref.shape[0]
    border = boundary_ref.shape[1]
    wanted = jnp.transpose(wanted_ref[...].astype(F32))[0:1, :].astype(I32)
    slots = wanted.shape[1] // got_ref.shape[0]
    got = got_ref[:, got_ref.shape[1] - slots :, :].reshape(wanted.shape[1], LANES)
    border_grad = nn(hit_rows(wanted, border), got)
    out_ref[...] = local_ref[...] + fold_wide(
        nn(hit_rows(boundary_ref[...], rows), split_wide(border_grad))
    )


def add_parts_kernel(got_ref, out_ref):
    size = out_ref.shape[0]
    total = got_ref[0, :size, :].astype(F32)
    for k in range(1, got_ref.shape[0]):
        total = total + got_ref[k, :size, :].astype(F32)
    out_ref[...] = total


def add_groups_kernel(*refs):
    part_refs, out_ref = refs[:-1], refs[-1]
    total = part_refs[0][...]
    for part_ref in part_refs[1:]:
        total = total + part_ref[...]
    total = total.astype(BF)
    for k in range(out_ref.shape[0]):
        out_ref[k] = total


def scale_kernel(pack_ref, *out_refs, scales):
    place = 0
    for out_ref, scale in zip(out_refs, scales):
        size = out_ref.shape[0]
        out_ref[...] = pack_ref[place : place + size, :].astype(F32) * scale
        place += size


def whole(shape):
    zeros = (0,) * len(shape)
    return pl.BlockSpec(shape, lambda *_: zeros)


def call(kernel, out_shapes, *args, flops=0, bytes_accessed=0, in_specs=None, out_specs=None,
         grid=None, scratch=(), name=None, vmem=40):
    single = not isinstance(out_shapes, (list, tuple))
    extra = {}
    if grid is not None:
        extra["grid"] = grid
    if in_specs is not None:
        extra["in_specs"] = in_specs
    if out_specs is not None:
        extra["out_specs"] = out_specs
    return pl.pallas_call(
        kernel,
        out_shape=out_shapes if single else list(out_shapes),
        scratch_shapes=list(scratch),
        compiler_params=pltpu.CompilerParams(vmem_limit_bytes=vmem * 2**20),
        cost_estimate=pl.CostEstimate(
            flops=flops, bytes_accessed=bytes_accessed, transcendentals=0
        ),
        name=name,
        **extra,
    )(*args)


def local(
    node_features, edge_features, coarse_features,
    edge_w_one, edge_w_two, node_w_one, node_w_two, coarse_w_one, coarse_w_two,
    edge_source, edge_target, boundary, ghost_pos, restr_order, restr_count, coarse_slot,
    node_cotangent, edge_cotangent, coarse_cotangent,
):
    rows, latent = node_features.shape
    edges = edge_features.shape[0]
    coarse = coarse_features.shape[0]
    groups = lax.axis_size("group")
    domains = lax.axis_size("dom")
    parts = groups * domains
    slots = ghost_pos.shape[2]
    ghosts = domains * slots
    shape = jax.ShapeDtypeStruct

    def edge_blocks(block):
        return (
            (edges // block,),
            pl.BlockSpec((1, block), lambda i: (0, i)),
            pl.BlockSpec((block, latent), lambda i: (i, 0)),
        )

    exchange = functools.partial(lax.all_to_all, split_axis=0, concat_axis=0, tiled=True)

    def turned(step):
        return [(k, (k - step) % groups) for k in range(groups)]

    source = edge_source.reshape(1, edges)
    target = edge_target.reshape(1, edges)
    spread = call(
        spread_kernel, shape((ghosts, latent), BF), ghost_pos,
        flops=10**6, bytes_accessed=10**5, name="spread", vmem=8,
    )
    asked = exchange(spread.reshape(domains, slots, latent), "dom").reshape(ghosts, latent)
    slot_list = coarse_slot.reshape(groups, -1)
    here = lax.axis_index("group").astype(I32).reshape(1, 1)

    grid_block = 2048
    grid, index_spec, edge_spec = edge_blocks(grid_block)
    own_rows = call(
        edge_first_kernel, shape((2, edges, latent), BF), source, target, node_features,
        grid=grid,
        in_specs=[index_spec, index_spec, whole((rows, latent))],
        out_specs=pl.BlockSpec((2, grid_block, latent), lambda i: (0, i, 0)),
        flops=4 * 10**9, bytes_accessed=3 * 10**6, name="edge_first", vmem=61,
    )
    messages = call(
        order_kernel, [shape((rows // 2 + 16, latent), BF)] * groups,
        here, restr_count, restr_order, slot_list, node_cotangent,
        in_specs=[pl.BlockSpec(memory_space=pltpu.SMEM)] * 2
        + [pl.BlockSpec(memory_space=pltpu.VMEM)] * 3,
        flops=10**9, bytes_accessed=10**6, name="order", vmem=16,
    )
    asked, own_rows, messages = lax.optimization_barrier((asked, own_rows, messages))
    share = call(
        share_kernel, shape((ghosts, latent), BF), boundary, asked, node_features,
        flops=10**9, bytes_accessed=10**6, name="share", vmem=16,
    )
    share, messages = lax.optimization_barrier((share, messages))
    messages = [messages[0]] + [
        lax.ppermute(messages[ahead], "group", turned(ahead)) for ahead in range(1, groups)
    ]
    ghost_rows = exchange(share.reshape(domains, slots, latent), "dom").reshape(ghosts, latent)
    grid, index_spec, edge_spec = edge_blocks(4096)
    pre, src_rows, summed, updated = call(
        edge_second_kernel,
        [shape((edges, latent), F32), shape((edges, latent), BF), shape((rows, latent), BF),
         shape((rows, latent), BF)],
        source, target, own_rows, edge_features, ghost_rows, edge_w_one, edge_w_two,
        node_features, node_w_one, node_w_two,
        grid=grid,
        in_specs=[index_spec, index_spec, whole((2, edges, latent)), edge_spec,
                  whole((ghosts, latent)), whole((3 * latent, latent)), whole((latent, latent)),
                  whole((rows, latent)), whole((2 * latent, latent)), whole((latent, latent))],
        out_specs=[edge_spec, edge_spec, whole((rows, latent)), whole((rows, latent))],
        scratch=[pltpu.VMEM((rows // 2, 2 * latent), F32)],
        flops=5 * 10**9, bytes_accessed=8 * 10**6, name="edge_second",
    )
    goal, *send = call(
        pool_kernel, [shape((1, rows), I32)] + [shape((coarse, latent), BF)] * groups,
        here, restr_count, restr_order, updated, *messages,
        in_specs=[pl.BlockSpec(memory_space=pltpu.SMEM)] * 2
        + [pl.BlockSpec(memory_space=pltpu.VMEM)] * (2 + groups),
        flops=10**9, bytes_accessed=10**6, name="pool", vmem=16,
    )
    slopes = call(
        slopes_kernel,
        [shape((size, latent), kind) for size in (edges, rows) for kind in (F32, BF, F32)],
        pre, edge_w_two, node_features, summed, node_w_one, node_w_two,
        flops=10**9, bytes_accessed=10**7, name="slopes",
    )
    got = [send[0]] + [
        lax.ppermute(send[ahead], "group", turned(-ahead)) for ahead in range(1, groups)
    ]
    from_fine = call(
        cot_pool_kernel, shape((coarse, latent), F32), here, slot_list, *messages,
        in_specs=[pl.BlockSpec(memory_space=pltpu.SMEM)]
        + [pl.BlockSpec(memory_space=pltpu.VMEM)] * (1 + groups),
        flops=10**9, bytes_accessed=10**6, name="cot_pool", vmem=16,
    )
    got, from_fine = lax.optimization_barrier((got, from_fine))
    grad_coarse, coarse_back, grad_c_one, grad_c_two = call(
        coarse_kernel,
        [shape((coarse, latent), F32), shape((coarse, latent), BF),
         shape((2 * latent, latent), F32), shape((latent, latent), F32)],
        coarse_features, coarse_cotangent, from_fine, coarse_w_one, coarse_w_two, *got,
        flops=10**8, bytes_accessed=10**6, name="coarse", vmem=16,
    )
    returned = [coarse_back] + [
        lax.ppermute(coarse_back, "group", turned(ahead)) for ahead in range(1, groups)
    ]
    share_rows = 48
    pack_rows = domains * share_rows
    grid, index_spec, edge_spec = edge_blocks(4096)
    joint_shape = (domains, share_rows + slots, latent)
    grad_pre, node_local, joint = call(
        edge_back_kernel,
        [shape((edges, latent), BF), shape((rows, latent), F32), shape(joint_shape, BF)],
        *slopes[3:], source, target, *slopes[:3], src_rows, own_rows, edge_features, edge_cotangent, edge_w_one, edge_w_two,
        goal, node_cotangent, node_features, summed, node_w_one, node_w_two,
        grad_c_one, grad_c_two, *returned,
        grid=grid,
        in_specs=[whole((rows, latent))] * 3
        + [index_spec, index_spec] + [edge_spec] * 4 + [
                  pl.BlockSpec((1, edges, latent), lambda i: (1, 0, 0)), edge_spec, edge_spec,
                  whole((3 * latent, latent)), whole((latent, latent)),
                  whole((1, rows)),
                  whole((rows, latent)), whole((rows, latent)), whole((rows, latent)),
                  whole((2 * latent, latent)), whole((latent, latent)),
                  whole((2 * latent, latent)), whole((latent, latent))]
        + [whole((coarse, latent))] * groups,
        out_specs=[edge_spec, whole((rows, latent)), whole(joint_shape)],
        scratch=[pltpu.VMEM((rows // 2, 2 * latent), BF), pltpu.VMEM((3 * latent, latent), F32),
                 pltpu.VMEM((latent, latent), F32), pltpu.VMEM((2 * latent, latent), F32),
                 pltpu.VMEM((latent, latent), F32), pltpu.VMEM((ghosts // 2, 2 * latent), F32),
                 pltpu.VMEM((pack_rows, latent), BF)],
        flops=6 * 10**9, bytes_accessed=10**7, name="edge_back",
    )
    grid, index_spec, edge_spec = edge_blocks(4096)
    own_local, grad_edges = call(
        own_back_kernel,
        [shape((rows, latent), F32), shape((edges, latent), F32)],
        source, target, grad_pre, edge_cotangent, node_local, edge_w_one,
        grid=grid,
        in_specs=[index_spec, index_spec, edge_spec, edge_spec, whole((rows, latent)),
                  whole((3 * latent, latent))],
        out_specs=[whole((rows, latent)), edge_spec],
        scratch=[pltpu.VMEM((rows // 2, 2 * latent), F32)] * 2,
        flops=4 * 10**9, bytes_accessed=5 * 10**6, name="own_back",
    )
    joint_got, own_local = lax.optimization_barrier((exchange(joint, "dom"), own_local))
    part_sum = call(
        add_parts_kernel, shape((share_rows, latent), F32), joint_got,
        flops=10**6, bytes_accessed=10**6, name="add_parts", vmem=16,
    )
    part_sums = [part_sum] + [
        lax.ppermute(part_sum, "group", turned(ahead)) for ahead in range(1, groups)
    ]
    pack_sum = call(
        add_groups_kernel, shape((domains, share_rows, latent), BF), *part_sums,
        flops=10**6, bytes_accessed=10**6, name="add_groups", vmem=16,
    )
    pack_all = exchange(pack_sum, "dom").reshape(pack_rows, latent)
    grad_nodes = call(
        add_back_kernel, shape((rows, latent), F32), boundary, asked, joint_got, own_local,
        flops=10**9, bytes_accessed=10**6, name="add_back", vmem=16,
    )
    edge_scale = (edges * parts) ** (-0.5)
    node_scale = (rows * parts) ** (-0.5)
    coarse_scale = (coarse * parts) ** (-0.5)
    weight_grads = call(
        functools.partial(
            scale_kernel,
            scales=(edge_scale, edge_scale, node_scale, node_scale, coarse_scale, coarse_scale),
        ),
        [shape((size * latent, latent), F32) for size in (3, 1, 2, 1, 2, 1)],
        pack_all,
        flops=10**6, bytes_accessed=10**6, name="scale", vmem=16,
    )
    return (grad_nodes, grad_edges, grad_coarse, *weight_grads)


def solution(mesh):
    rows = P(("group", "dom"), None)
    cube = P(("group", "dom"), None, None)
    line = P(("group", "dom"))
    placed = (
        rows, rows, rows, P(), P(), P(), P(), P(), P(), line, line, rows, cube, rows, rows, cube,
        rows, rows, rows,
    )
    return jax.shard_map(
        local,
        mesh=mesh,
        in_specs=placed,
        out_specs=(rows, rows, rows, P(), P(), P(), P(), P(), P()),
        check_vma=False,
    )
```

```python
import functools

import jax
import jax.numpy as jnp
from jax import lax
from jax.experimental import pallas as pl
from jax.experimental.pallas import tpu as pltpu
from jax.sharding import PartitionSpec as P

NORM_EPSILON = 1e-05
POOL_SHARE = 0.25
BF = jnp.bfloat16
F32 = jnp.float32
I32 = jnp.int32
LANES = 128
SECOND_SUB = 512
BACK_SUB = 2048


def nn(a, b):
    return lax.dot_general(a, b, (((1,), (0,)), ((), ())), preferred_element_type=F32)


def nt(a, b):
    return lax.dot_general(a, b, (((1,), (1,)), ((), ())), preferred_element_type=F32)


def tn(a, b):
    return lax.dot_general(a, b, (((0,), (0,)), ((), ())), preferred_element_type=F32)


def as_hit(mask):
    return jnp.where(mask, 1.0, 0.0).astype(BF)


def hit_rows(index_row, count, base=0):
    width = index_row.shape[1]
    return as_hit(lax.broadcasted_iota(I32, (count, width), 0) == index_row - base)


def spread_column(index_row):
    width = index_row.shape[1]
    return jnp.transpose(jnp.broadcast_to(index_row, (LANES, width)))


def hit_columns(index_column, count, base=0):
    lane = lax.broadcasted_iota(I32, index_column.shape, 1)
    return jnp.concatenate(
        [as_hit(lane == index_column - (base + LANES * j)) for j in range(count // LANES)], axis=1
    )


def halves(table):
    half = table.shape[0] // 2
    return jnp.concatenate([table[:half], table[half:]], axis=1)


def pick_rows(index_column, table_halves):
    half = table_halves.shape[0]
    upper = index_column >= half
    wide = nn(hit_columns(jnp.where(upper, index_column - half, index_column), half), table_halves)
    return jnp.where(upper, wide[:, LANES:], wide[:, :LANES])


def sum_rows(index_row, index_column, values, half):
    upper = index_column >= half
    nothing = jnp.zeros_like(values)
    both = jnp.concatenate(
        [jnp.where(upper, nothing, values), jnp.where(upper, values, nothing)], axis=1
    )
    return nn(hit_rows(jnp.where(index_row >= half, index_row - half, index_row), half), both)


def unfold(sums):
    return jnp.concatenate([sums[:, :LANES], sums[:, LANES:]], axis=0)


def split_wide(values):
    high = values.astype(BF)
    low = (values - high.astype(F32)).astype(BF)
    return jnp.concatenate([high, low], axis=1)


def fold_wide(values):
    return values[:, :LANES] + values[:, LANES:]


def times_transposed(values, weights):
    return nt(split_wide(values), jnp.concatenate([weights, weights], axis=1))


def mean_lanes(values):
    return jnp.mean(values, axis=-1, keepdims=True)


def norm_parts(values):
    centred = values - mean_lanes(values)
    inv_std = lax.rsqrt(mean_lanes(centred * centred) + NORM_EPSILON)
    return centred * inv_std, inv_std


def norm_back(normed, inv_std, grad_in):
    return inv_std * (grad_in - mean_lanes(grad_in) - normed * mean_lanes(grad_in * normed))


def sigmoid(values):
    return 1.0 / (1.0 + jnp.exp(-values))


def slope(values, sig):
    return sig * (1.0 + values * (1.0 - sig))


def spread_kernel(wanted_ref, out_ref):
    _, domains, slots = wanted_ref.shape
    ghosts = out_ref.shape[0]
    first = lax.broadcasted_iota(I32, (ghosts, domains), 0) // slots
    pick = as_hit(first == lax.broadcasted_iota(I32, (ghosts, domains), 1))
    by_owner = nn(pick, wanted_ref[0].astype(F32).astype(BF))
    slot = lax.broadcasted_iota(I32, (ghosts, slots), 0) % slots
    own = jnp.where(slot == lax.broadcasted_iota(I32, (ghosts, slots), 1), by_owner, 0.0).astype(BF)
    out_ref[...] = nn(own, jnp.ones((slots, LANES), BF)).astype(BF)


def share_kernel(boundary_ref, wanted_ref, nodes_ref, out_ref):
    border = boundary_ref.shape[1]
    shared = pick_rows(spread_column(boundary_ref[...]), halves(nodes_ref[...])).astype(BF)
    wanted = wanted_ref[...].astype(F32).astype(I32)
    out_ref[...] = nn(hit_columns(wanted, border), shared).astype(BF)


def choose(index, lines):
    found = lines[0]
    for k in range(1, len(lines)):
        found = jnp.where(index == k, lines[k], found)
    return found


def order_kernel(group_ref, count_ref, order_ref, slot_ref, node_cot_ref, *out_refs):
    groups, capacity = slot_ref.shape
    rows = order_ref.shape[1]
    here = group_ref[0, 0]
    table = halves(node_cot_ref[...])
    order = jnp.broadcast_to(order_ref[...], (8, rows))
    place = lax.broadcasted_iota(I32, (1, capacity), 1)
    slots = jnp.concatenate(
        [slot_ref[k : k + 1, at : at + LANES] for k in range(groups) for at in range(0, capacity, LANES)],
        axis=0,
    ).astype(F32).astype(BF)
    for ahead, out_ref in enumerate(out_refs):
        k = lax.rem(here + (groups - ahead), groups)
        start = 0
        for other in range(groups - 1):
            start = start + jnp.where(other < k, count_ref[0, other], 0)
        line = pltpu.roll(order, lax.rem(rows - start, rows), 1)[0:1, :capacity]
        line = jnp.where(place < count_ref[0, k], line, -1)
        out_ref[:capacity, :] = pick_rows(spread_column(line), table).astype(BF)
        out_ref[capacity:, :] = slots


def cot_pool_kernel(group_ref, slot_ref, *refs):
    got_refs, out_ref = refs[:-1], refs[-1]
    groups, capacity = slot_ref.shape
    lines = [slot_ref[k : k + 1, :] for k in range(groups)]
    total = jnp.zeros(out_ref.shape, F32)
    for ahead, got_ref in enumerate(got_refs):
        line = choose(lax.rem(group_ref[0, 0] + ahead, groups), lines)
        total = total + nn(hit_rows(line, out_ref.shape[0]), got_ref[:capacity, :])
    out_ref[...] = total


def pool_kernel(group_ref, count_ref, order_ref, updated_ref, *refs):
    groups = (len(refs) - 1) // 2
    got_refs, out_ref, send_refs = refs[:groups], refs[groups], refs[groups + 1 :]
    coarse = send_refs[0].shape[0]
    rows = order_ref.shape[1]
    capacity = rows // 2
    pieces = capacity // LANES
    here = group_ref[0, 0]
    place = lax.broadcasted_iota(I32, (8, rows), 1)
    owner = jnp.zeros((8, rows), I32)
    goal = jnp.zeros((8, rows), I32)
    for ahead, got_ref in enumerate(got_refs):
        k = lax.rem(here + ahead, groups)
        start = 0
        for other in range(groups - 1):
            start = start + jnp.where(other < k, count_ref[0, other], 0)
        listed = got_ref[capacity:, :].astype(F32)
        line = choose(here, [
            jnp.concatenate(
                [listed[j * pieces + i : j * pieces + i + 1, :] for i in range(pieces)], axis=1
            )
            for j in range(groups)
        ]).astype(I32)
        line = jnp.concatenate([line, jnp.zeros((1, rows - capacity), I32)], axis=1)
        line = pltpu.roll(jnp.broadcast_to(line, (8, rows)), start, 1)
        inside = (place >= start) & (place < start + count_ref[0, k])
        owner = jnp.where(inside, ahead, owner)
        goal = jnp.where(inside, line, goal)
    digits = jnp.where(lax.broadcasted_iota(I32, (8, rows), 0) == 0, owner, goal)
    by_row = nt(digits.astype(F32).astype(BF), hit_rows(order_ref[...], rows))
    goal = (by_row[0:1, :] * coarse + by_row[1:2, :]).astype(I32)
    out_ref[...] = goal
    pooled = nn(hit_rows(goal, groups * coarse), updated_ref[...]).astype(BF)
    for k, send_ref in enumerate(send_refs):
        send_ref[...] = pooled[k * coarse : (k + 1) * coarse, :]


def edge_first_kernel(source_ref, target_ref, nodes_ref, out_ref):
    nodes = halves(nodes_ref[...])
    out_ref[0] = pick_rows(spread_column(source_ref[...]), nodes).astype(BF)
    out_ref[1] = pick_rows(spread_column(target_ref[...]), nodes).astype(BF)


def edge_second_kernel(
    source_ref, target_ref, own_ref, edges_ref, ghosts_ref, w1_ref, w2_ref,
    nodes_ref, v1_ref, v2_ref,
    pre_ref, src_ref, summed_ref, updated_ref, total,
):
    step = pl.program_id(0)
    rows = nodes_ref.shape[0]

    @pl.when(step == 0)
    def _():
        total[...] = jnp.zeros_like(total)

    ghosts = halves(ghosts_ref[...])
    from_ghost = spread_column(source_ref[...]) - rows
    target = target_ref[...]
    messages = []
    for part in range(0, target.shape[1], SECOND_SUB):
        here = slice(part, part + SECOND_SUB)
        src = own_ref[0, here, :] + pick_rows(from_ghost[here], ghosts).astype(BF)
        src_ref[here, :] = src
        stacked = jnp.concatenate([src, own_ref[1, here, :], edges_ref[here, :]], axis=1)
        pre = nn(stacked, w1_ref[...])
        pre_ref[here, :] = pre
        hidden = (pre * sigmoid(pre)).astype(BF)
        message, _ = norm_parts(nn(hidden, w2_ref[...]))
        messages.append(message.astype(BF))
    total[...] += sum_rows(
        target, spread_column(target), jnp.concatenate(messages, axis=0), rows // 2
    )

    @pl.when(step == pl.num_programs(0) - 1)
    def _():
        summed = unfold(total[...]).astype(BF)
        summed_ref[...] = summed
        nodes = nodes_ref[...]
        pre_node = nn(jnp.concatenate([nodes, summed], axis=1), v1_ref[...])
        hidden_node = (pre_node * sigmoid(pre_node)).astype(BF)
        normed, _ = norm_parts(nn(hidden_node, v2_ref[...]))
        updated_ref[...] = (nodes.astype(F32) + normed).astype(BF)


def coarse_kernel(feat_ref, cot_ref, from_fine_ref, w1_ref, w2_ref, *refs):
    got_refs, (grad_ref, back_ref, g1_ref, g2_ref) = refs[:-4], refs[-4:]
    got = got_refs[0][...].astype(F32)
    for got_ref in got_refs[1:]:
        got = got + got_ref[...].astype(F32)
    pooled = (got * POOL_SHARE).astype(BF)
    cot = cot_ref[...].astype(F32)
    grad_out = (cot + from_fine_ref[...]).astype(BF)
    joined = jnp.concatenate([feat_ref[...], pooled], axis=1)
    pre = nn(joined, w1_ref[...])
    sig = sigmoid(pre)
    hidden = (pre * sig).astype(BF)
    g2_ref[...] = tn(hidden, grad_out)
    grad_pre = (nt(grad_out, w2_ref[...]) * slope(pre, sig)).astype(BF)
    g1_ref[...] = tn(joined, grad_pre)
    grad_in = nt(grad_pre, w1_ref[...])
    grad_ref[...] = cot + grad_in[:, :LANES]
    back_ref[...] = (grad_in[:, LANES:] * POOL_SHARE).astype(BF)


def edge_back_kernel(
    source_ref, target_ref, pre_ref, src_ref, tgt_ref, edges_ref, cot_ref, w1_ref, w2_ref,
    goal_ref, node_cot_ref, nodes_ref, summed_ref, v1_ref, v2_ref, c1_ref, c2_ref, *rest,
):
    gp_refs = rest[:-10]
    grad_pre_ref, local_ref, joint_ref, wide, gw1, gw2, gv1, gv2, by_ghost, pack_ref = rest[-10:]
    step = pl.program_id(0)
    rows = nodes_ref.shape[0]

    @pl.when(step == 0)
    def _():
        by_ghost[...] = jnp.zeros_like(by_ghost)
        gw1[...] = jnp.zeros_like(gw1)
        gw2[...] = jnp.zeros_like(gw2)
        table = halves(jnp.concatenate([gp_ref[...] for gp_ref in gp_refs], axis=0))
        from_coarse = pick_rows(spread_column(goal_ref[...]), table)
        updated_grad = node_cot_ref[...].astype(F32) + from_coarse
        joined = jnp.concatenate([nodes_ref[...], summed_ref[...]], axis=1)
        pre = nn(joined, v1_ref[...])
        sig = sigmoid(pre)
        hidden = (pre * sig).astype(BF)
        normed, inv_std = norm_parts(nn(hidden, v2_ref[...]))
        grad_norm = norm_back(normed, inv_std, updated_grad).astype(BF)
        gv2[...] = tn(hidden, grad_norm)
        grad_pre = (nt(grad_norm, v2_ref[...]) * slope(pre, sig)).astype(BF)
        gv1[...] = tn(joined, grad_pre)
        grad_in = nt(grad_pre, v1_ref[...])
        local_ref[...] = updated_grad + grad_in[:, :LANES]
        wide[...] = halves(grad_in[:, LANES:].astype(BF))

    target = spread_column(target_ref[...])
    hiddens, grad_norms, grad_pres = [], [], []
    for part in range(0, target.shape[0], BACK_SUB):
        here = slice(part, part + BACK_SUB)
        message_grad = cot_ref[here, :].astype(F32) + pick_rows(target[here], wide[...])
        pre = pre_ref[here, :]
        sig = sigmoid(pre)
        hidden = (pre * sig).astype(BF)
        normed, inv_std = norm_parts(nn(hidden, w2_ref[...]))
        grad_norm = norm_back(normed, inv_std, message_grad).astype(BF)
        grad_pre = (nt(grad_norm, w2_ref[...]) * slope(pre, sig)).astype(BF)
        hiddens.append(hidden)
        grad_norms.append(grad_norm)
        grad_pres.append(grad_pre)
    grad_pre = jnp.concatenate(grad_pres, axis=0)
    grad_pre_ref[...] = grad_pre
    gw2[...] += tn(jnp.concatenate(hiddens, axis=0), jnp.concatenate(grad_norms, axis=0))
    stacked = jnp.concatenate([src_ref[...], tgt_ref[0], edges_ref[...]], axis=1)
    gw1[...] += tn(stacked, grad_pre)
    source = source_ref[...] - rows
    by_ghost[...] += sum_rows(source, spread_column(source), grad_pre, by_ghost.shape[0])

    @pl.when(step == pl.num_programs(0) - 1)
    def _():
        place = 0
        for part in (gw1, gw2, gv1, gv2, c1_ref, c2_ref):
            size = part.shape[0]
            pack_ref[place : place + size, :] = part[...].astype(BF)
            place += size
        pack_ref[place:, :] = jnp.zeros((pack_ref.shape[0] - place, LANES), BF)
        ghost = times_transposed(unfold(by_ghost[...]), w1_ref[:LANES, :]).astype(BF)
        domains, both, _ = joint_ref.shape
        share = pack_ref.shape[0] // domains
        joint_ref[:, :share, :] = pack_ref[...].reshape(domains, share, LANES)
        joint_ref[:, share:, :] = ghost.reshape(domains, both - share, LANES)


def own_back_kernel(
    source_ref, target_ref, grad_pre_ref, cot_ref, local_ref, w1_ref,
    out_ref, edges_ref, by_source, by_target,
):
    step = pl.program_id(0)
    half = by_source.shape[0]

    @pl.when(step == 0)
    def _():
        by_source[...] = jnp.zeros_like(by_source)
        by_target[...] = jnp.zeros_like(by_target)

    grad_pre = grad_pre_ref[...]
    source, target = source_ref[...], target_ref[...]
    by_source[...] += sum_rows(source, spread_column(source), grad_pre, half)
    by_target[...] += sum_rows(target, spread_column(target), grad_pre, half)
    edges_ref[...] = cot_ref[...].astype(F32) + nt(grad_pre, w1_ref[2 * LANES :, :])

    @pl.when(step == pl.num_programs(0) - 1)
    def _():
        out_ref[...] = (
            local_ref[...]
            + times_transposed(unfold(by_source[...]), w1_ref[:LANES, :])
            + times_transposed(unfold(by_target[...]), w1_ref[LANES : 2 * LANES, :])
        )


def add_back_kernel(boundary_ref, wanted_ref, got_ref, local_ref, out_ref):
    rows = local_ref.shape[0]
    border = boundary_ref.shape[1]
    wanted = jnp.transpose(wanted_ref[...].astype(F32))[0:1, :].astype(I32)
    slots = wanted.shape[1] // got_ref.shape[0]
    got = got_ref[:, got_ref.shape[1] - slots :, :].reshape(wanted.shape[1], LANES)
    border_grad = nn(hit_rows(wanted, border), got)
    out_ref[...] = local_ref[...] + fold_wide(
        nn(hit_rows(boundary_ref[...], rows), split_wide(border_grad))
    )


def add_parts_kernel(got_ref, out_ref):
    size = out_ref.shape[0]
    total = got_ref[0, :size, :].astype(F32)
    for k in range(1, got_ref.shape[0]):
        total = total + got_ref[k, :size, :].astype(F32)
    out_ref[...] = total


def add_groups_kernel(*refs):
    part_refs, out_ref = refs[:-1], refs[-1]
    total = part_refs[0][...]
    for part_ref in part_refs[1:]:
        total = total + part_ref[...]
    total = total.astype(BF)
    for k in range(out_ref.shape[0]):
        out_ref[k] = total


def scale_kernel(pack_ref, *out_refs, scales):
    place = 0
    for out_ref, scale in zip(out_refs, scales):
        size = out_ref.shape[0]
        out_ref[...] = pack_ref[place : place + size, :].astype(F32) * scale
        place += size


def whole(shape):
    zeros = (0,) * len(shape)
    return pl.BlockSpec(shape, lambda *_: zeros)


def call(kernel, out_shapes, *args, flops=0, bytes_accessed=0, in_specs=None, out_specs=None,
         grid=None, scratch=(), name=None, vmem=40):
    single = not isinstance(out_shapes, (list, tuple))
    extra = {}
    if grid is not None:
        extra["grid"] = grid
    if in_specs is not None:
        extra["in_specs"] = in_specs
    if out_specs is not None:
        extra["out_specs"] = out_specs
    return pl.pallas_call(
        kernel,
        out_shape=out_shapes if single else list(out_shapes),
        scratch_shapes=list(scratch),
        compiler_params=pltpu.CompilerParams(vmem_limit_bytes=vmem * 2**20),
        cost_estimate=pl.CostEstimate(
            flops=flops, bytes_accessed=bytes_accessed, transcendentals=0
        ),
        name=name,
        **extra,
    )(*args)


def local(
    node_features, edge_features, coarse_features,
    edge_w_one, edge_w_two, node_w_one, node_w_two, coarse_w_one, coarse_w_two,
    edge_source, edge_target, boundary, ghost_pos, restr_order, restr_count, coarse_slot,
    node_cotangent, edge_cotangent, coarse_cotangent,
):
    rows, latent = node_features.shape
    edges = edge_features.shape[0]
    coarse = coarse_features.shape[0]
    groups = lax.axis_size("group")
    domains = lax.axis_size("dom")
    parts = groups * domains
    slots = ghost_pos.shape[2]
    ghosts = domains * slots
    shape = jax.ShapeDtypeStruct

    def edge_blocks(block):
        return (
            (edges // block,),
            pl.BlockSpec((1, block), lambda i: (0, i)),
            pl.BlockSpec((block, latent), lambda i: (i, 0)),
        )

    exchange = functools.partial(lax.all_to_all, split_axis=0, concat_axis=0, tiled=True)

    def turned(step):
        return [(k, (k - step) % groups) for k in range(groups)]

    source = edge_source.reshape(1, edges)
    target = edge_target.reshape(1, edges)
    spread = call(
        spread_kernel, shape((ghosts, latent), BF), ghost_pos,
        flops=10**6, bytes_accessed=10**5, name="spread", vmem=61,
    )
    asked = exchange(spread.reshape(domains, slots, latent), "dom").reshape(ghosts, latent)
    slot_list = coarse_slot.reshape(groups, -1)
    here = lax.axis_index("group").astype(I32).reshape(1, 1)

    grid_block = 2048
    grid, index_spec, edge_spec = edge_blocks(grid_block)
    own_rows = call(
        edge_first_kernel, shape((2, edges, latent), BF), source, target, node_features,
        grid=grid,
        in_specs=[index_spec, index_spec, whole((rows, latent))],
        out_specs=pl.BlockSpec((2, grid_block, latent), lambda i: (0, i, 0)),
        flops=4 * 10**9, bytes_accessed=3 * 10**6, name="edge_first", vmem=61,
    )
    messages = call(
        order_kernel, [shape((rows // 2 + 16, latent), BF)] * groups,
        here, restr_count, restr_order, slot_list, node_cotangent,
        in_specs=[pl.BlockSpec(memory_space=pltpu.SMEM)] * 2
        + [pl.BlockSpec(memory_space=pltpu.VMEM)] * 3,
        flops=10**9, bytes_accessed=10**6, name="order", vmem=16,
    )
    asked, own_rows, messages = lax.optimization_barrier((asked, own_rows, messages))
    share = call(
        share_kernel, shape((ghosts, latent), BF), boundary, asked, node_features,
        flops=10**9, bytes_accessed=10**6, name="share", vmem=16,
    )
    share, messages = lax.optimization_barrier((share, messages))
    messages = [messages[0]] + [
        lax.ppermute(messages[ahead], "group", turned(ahead)) for ahead in range(1, groups)
    ]
    ghost_rows = exchange(share.reshape(domains, slots, latent), "dom").reshape(ghosts, latent)
    grid, index_spec, edge_spec = edge_blocks(4096)
    pre, src_rows, summed, updated = call(
        edge_second_kernel,
        [shape((edges, latent), F32), shape((edges, latent), BF), shape((rows, latent), BF),
         shape((rows, latent), BF)],
        source, target, own_rows, edge_features, ghost_rows, edge_w_one, edge_w_two,
        node_features, node_w_one, node_w_two,
        grid=grid,
        in_specs=[index_spec, index_spec, whole((2, edges, latent)), edge_spec,
                  whole((ghosts, latent)), whole((3 * latent, latent)), whole((latent, latent)),
                  whole((rows, latent)), whole((2 * latent, latent)), whole((latent, latent))],
        out_specs=[edge_spec, edge_spec, whole((rows, latent)), whole((rows, latent))],
        scratch=[pltpu.VMEM((rows // 2, 2 * latent), F32)],
        flops=5 * 10**9, bytes_accessed=8 * 10**6, name="edge_second",
    )
    goal, *send = call(
        pool_kernel, [shape((1, rows), I32)] + [shape((coarse, latent), BF)] * groups,
        here, restr_count, restr_order, updated, *messages,
        in_specs=[pl.BlockSpec(memory_space=pltpu.SMEM)] * 2
        + [pl.BlockSpec(memory_space=pltpu.VMEM)] * (2 + groups),
        flops=10**9, bytes_accessed=10**6, name="pool", vmem=16,
    )
    got = [send[0]] + [
        lax.ppermute(send[ahead], "group", turned(-ahead)) for ahead in range(1, groups)
    ]
    from_fine = call(
        cot_pool_kernel, shape((coarse, latent), F32), here, slot_list, *messages,
        in_specs=[pl.BlockSpec(memory_space=pltpu.SMEM)]
        + [pl.BlockSpec(memory_space=pltpu.VMEM)] * (1 + groups),
        flops=10**9, bytes_accessed=10**6, name="cot_pool", vmem=16,
    )
    got, from_fine = lax.optimization_barrier((got, from_fine))
    grad_coarse, coarse_back, grad_c_one, grad_c_two = call(
        coarse_kernel,
        [shape((coarse, latent), F32), shape((coarse, latent), BF),
         shape((2 * latent, latent), F32), shape((latent, latent), F32)],
        coarse_features, coarse_cotangent, from_fine, coarse_w_one, coarse_w_two, *got,
        flops=10**8, bytes_accessed=10**6, name="coarse", vmem=16,
    )
    returned = [coarse_back] + [
        lax.ppermute(coarse_back, "group", turned(ahead)) for ahead in range(1, groups)
    ]
    share_rows = 48
    pack_rows = domains * share_rows
    grid, index_spec, edge_spec = edge_blocks(4096)
    joint_shape = (domains, share_rows + slots, latent)
    grad_pre, node_local, joint = call(
        edge_back_kernel,
        [shape((edges, latent), BF), shape((rows, latent), F32), shape(joint_shape, BF)],
        source, target, pre, src_rows, own_rows, edge_features, edge_cotangent, edge_w_one, edge_w_two,
        goal, node_cotangent, node_features, summed, node_w_one, node_w_two,
        grad_c_one, grad_c_two, *returned,
        grid=grid,
        in_specs=[index_spec, index_spec, edge_spec, edge_spec,
                  pl.BlockSpec((1, edges, latent), lambda i: (1, 0, 0)), edge_spec, edge_spec,
                  whole((3 * latent, latent)), whole((latent, latent)),
                  whole((1, rows)),
                  whole((rows, latent)), whole((rows, latent)), whole((rows, latent)),
                  whole((2 * latent, latent)), whole((latent, latent)),
                  whole((2 * latent, latent)), whole((latent, latent))]
        + [whole((coarse, latent))] * groups,
        out_specs=[edge_spec, whole((rows, latent)), whole(joint_shape)],
        scratch=[pltpu.VMEM((rows // 2, 2 * latent), BF), pltpu.VMEM((3 * latent, latent), F32),
                 pltpu.VMEM((latent, latent), F32), pltpu.VMEM((2 * latent, latent), F32),
                 pltpu.VMEM((latent, latent), F32), pltpu.VMEM((ghosts // 2, 2 * latent), F32),
                 pltpu.VMEM((pack_rows, latent), BF)],
        flops=6 * 10**9, bytes_accessed=10**7, name="edge_back",
    )
    grid, index_spec, edge_spec = edge_blocks(4096)
    own_local, grad_edges = call(
        own_back_kernel,
        [shape((rows, latent), F32), shape((edges, latent), F32)],
        source, target, grad_pre, edge_cotangent, node_local, edge_w_one,
        grid=grid,
        in_specs=[index_spec, index_spec, edge_spec, edge_spec, whole((rows, latent)),
                  whole((3 * latent, latent))],
        out_specs=[whole((rows, latent)), edge_spec],
        scratch=[pltpu.VMEM((rows // 2, 2 * latent), F32)] * 2,
        flops=4 * 10**9, bytes_accessed=5 * 10**6, name="own_back",
    )
    joint_got, own_local = lax.optimization_barrier((exchange(joint, "dom"), own_local))
    part_sum = call(
        add_parts_kernel, shape((share_rows, latent), F32), joint_got,
        flops=10**6, bytes_accessed=10**6, name="add_parts", vmem=16,
    )
    part_sums = [part_sum] + [
        lax.ppermute(part_sum, "group", turned(ahead)) for ahead in range(1, groups)
    ]
    pack_sum = call(
        add_groups_kernel, shape((domains, share_rows, latent), BF), *part_sums,
        flops=10**6, bytes_accessed=10**6, name="add_groups", vmem=16,
    )
    pack_all = exchange(pack_sum, "dom").reshape(pack_rows, latent)
    grad_nodes = call(
        add_back_kernel, shape((rows, latent), F32), boundary, asked, joint_got, own_local,
        flops=10**9, bytes_accessed=10**6, name="add_back", vmem=16,
    )
    edge_scale = (edges * parts) ** (-0.5)
    node_scale = (rows * parts) ** (-0.5)
    coarse_scale = (coarse * parts) ** (-0.5)
    weight_grads = call(
        functools.partial(
            scale_kernel,
            scales=(edge_scale, edge_scale, node_scale, node_scale, coarse_scale, coarse_scale),
        ),
        [shape((size * latent, latent), F32) for size in (3, 1, 2, 1, 2, 1)],
        pack_all,
        flops=10**6, bytes_accessed=10**6, name="scale", vmem=16,
    )
    return (grad_nodes, grad_edges, grad_coarse, *weight_grads)


def solution(mesh):
    rows = P(("group", "dom"), None)
    cube = P(("group", "dom"), None, None)
    line = P(("group", "dom"))
    placed = (
        rows, rows, rows, P(), P(), P(), P(), P(), P(), line, line, rows, cube, rows, rows, cube,
        rows, rows, rows,
    )
    return jax.shard_map(
        local,
        mesh=mesh,
        in_specs=placed,
        out_specs=(rows, rows, rows, P(), P(), P(), P(), P(), P()),
        check_vma=False,
    )
```
